128 devices in a mesh: lat: 4 (over z_lo, core), lon: 32 (over y, x, z_hi).
Axes of the slice: x: 4, y: 4, z: 4 (z_hi: 2, z_lo: 2; z = z_hi * 2 + z_lo), core: 2. Of those that a mesh axis runs over, the one named last changes fastest.
Arguments:
- lattice_site_embedding: bfloat16 [512, 256, 768], P('lat', 'lon'), may hold values from -24 to 24
- final_lattice_sensitivity: bfloat16 [512, 256, 768], P('lat', 'lon'), may hold values from -6 to 6
- patch_rescale_coeffs: float32 [768], replicated, may hold values from 0.25 to 1.75
- patch_triple_linear: bfloat16 [768, 2304], replicated, may hold values from -0.21875 to 0.21875
- patch_exit_linear: bfloat16 [768, 768], replicated, may hold values from -0.21875 to 0.21875
- patch_logit_temper: float32 [12], replicated, may hold values from 2 to 25
- bearer_rescale_coeffs: float32 [768], replicated, may hold values from 0.25 to 1.75
- bearer_triple_linear: bfloat16 [768, 2304], replicated, may hold values from -0.21875 to 0.21875
- bearer_exit_linear: bfloat16 [768, 768], replicated, may hold values from -0.21875 to 0.21875
- bearer_logit_temper: float32 [12], replicated, may hold values from 2 to 25
- bearer_sequence_place: int32 [128, 64], P('lat', 'lon'), may hold values from 0 to 2047, as said below
Outputs:
- out_field: bfloat16 [512, 256, 768], P('lat', 'lon')
- field_grad: bfloat16 [512, 256, 768], P('lat', 'lon')
The draws below stay inside these ranges and needn't reach their ends.
Inputs may be any that keep to these rules, and one draw needn't show every extreme that they name: `bearer_sequence_place`: places within one row of devices (the carriers of 128 grid rows) are all different. Of the 64 carriers of one device, exactly 2 have place // 64 equal to each lon index, and for these (place % 64) // 2 is the lon index of the device that holds the carrier.
All inputs are finite; a program needn't handle non-finite values.
Results may differ from the reference program's by a relative error of at most 0.014.
Values may be sent and summed in bfloat16 or wider, within the bound.
A program may use at most 192 MiB of HBM per device.

```python
import math
import jax
import jax.numpy as jnp
from jax import lax

SUBSPACE_COUNT = 12
HEAD_DIM = 64
EMBEDDING_SIZE = 768
TILE_LINE_COUNT = 128
TILE_COLUMN_COUNT = 8
BEARERS_PER_CHIP = 64
BEARERS_PER_SET = 256
NLAT = 512
NLON = 256
BEARER_LINES = 128
BEARER_COLUMNS = 64
N_LON = 32


def draw_lattice_site_embedding(key, part):
    key = jax.random.fold_in(key, 11)
    base_key, row_key, col_key = jax.random.split(key, 3)
    base_values = jax.random.normal(base_key, (NLAT, NLON, EMBEDDING_SIZE), jnp.float32)
    row_scale = jnp.exp(jax.random.uniform(row_key, (NLAT, NLON, 1), jnp.float32, math.log(0.3), math.log(3.0)))
    col_scale = jnp.exp(jax.random.uniform(col_key, (EMBEDDING_SIZE,), jnp.float32, math.log(0.5), math.log(2.0)))
    return jnp.clip(base_values * row_scale * col_scale, -24.0, 24.0).astype(jnp.bfloat16)


def draw_bearer_sequence_place(key, part):
    key = jax.random.fold_in(key, 23)
    chip_line_count = NLAT // TILE_LINE_COUNT
    chip_column_count = NLON // TILE_COLUMN_COUNT
    each_neighbor = BEARERS_PER_CHIP // chip_column_count
    chip_probe_list = jax.random.split(key, chip_line_count * chip_column_count)
    permutation_list = jax.vmap(lambda lone_member: jax.random.permutation(lone_member, BEARERS_PER_CHIP))(chip_probe_list).astype(jnp.int32)
    sender_side = (jnp.arange(chip_line_count * chip_column_count, dtype=jnp.int32) % chip_column_count)[:, None]
    bearer_sequence_places = permutation_list // each_neighbor * BEARERS_PER_CHIP + sender_side * each_neighbor + permutation_list % each_neighbor
    bearer_sequence_places = bearer_sequence_places.reshape(chip_line_count, chip_column_count, TILE_LINE_COUNT // 4, TILE_COLUMN_COUNT // 4)
    return jnp.transpose(bearer_sequence_places, (0, 2, 1, 3)).reshape(BEARER_LINES, BEARER_COLUMNS).astype(jnp.int32)


def block_levels(stream_key, shape, cuts, low, largest):
    loudness = 1.0
    for axis_at, parts in cuts:
        heights = jax.random.uniform(jax.random.fold_in(jax.random.fold_in(stream_key, 6), axis_at), (parts,), jnp.float32, low / len(cuts), largest / len(cuts))
        loudness = loudness * jnp.repeat(jnp.exp(heights), shape[axis_at] // parts).reshape((-1,) + (1,) * (len(shape) - 1 - axis_at))
    return loudness


def centred(rng, shape, deviation, most, cuts=(), kind=jnp.bfloat16):
    values = deviation * jax.random.normal(rng, shape, jnp.float32)
    if cuts:
        values = values * block_levels(rng, shape, cuts, -0.22, 0.18)
    return jnp.clip(values, -most, most).astype(kind)


def setup_inputs(seed: int = 0) -> dict:
    key_of = jax.random.split(jax.random.key(seed), 12)
    return {
        "lattice_site_embedding": draw_lattice_site_embedding(jax.random.fold_in(key_of[11], 71), 0),
        "final_lattice_sensitivity": centred(key_of[1], (NLAT, NLON, EMBEDDING_SIZE), 1.0, 6.0, ((0, 4), (1, 32))),
        "patch_rescale_coeffs": jnp.clip(1.0 + 0.15 * jax.random.normal(key_of[2], (EMBEDDING_SIZE,), jnp.float32), 0.25, 1.75),
        "patch_triple_linear": centred(key_of[3], (EMBEDDING_SIZE, 3 * EMBEDDING_SIZE), EMBEDDING_SIZE ** -0.5, 0.21875),
        "patch_exit_linear": centred(key_of[4], (EMBEDDING_SIZE, EMBEDDING_SIZE), EMBEDDING_SIZE ** -0.5, 0.21875),
        "patch_logit_temper": jnp.clip(jnp.exp(jax.random.uniform(key_of[5], (SUBSPACE_COUNT,), jnp.float32, math.log(2.0), math.log(25.0))), 2.0, 25.0),
        "bearer_rescale_coeffs": jnp.clip(1.0 + 0.15 * jax.random.normal(key_of[6], (EMBEDDING_SIZE,), jnp.float32), 0.25, 1.75),
        "bearer_triple_linear": centred(key_of[7], (EMBEDDING_SIZE, 3 * EMBEDDING_SIZE), EMBEDDING_SIZE ** -0.5, 0.21875),
        "bearer_exit_linear": centred(key_of[8], (EMBEDDING_SIZE, EMBEDDING_SIZE), EMBEDDING_SIZE ** -0.5, 0.21875),
        "bearer_logit_temper": jnp.clip(jnp.exp(jax.random.uniform(key_of[9], (SUBSPACE_COUNT,), jnp.float32, math.log(2.0), math.log(25.0))), 2.0, 25.0),
        "bearer_sequence_place": draw_bearer_sequence_place(jax.random.fold_in(key_of[11], 71), 0),
    }


def standardized_lines(payload_lines, rescale_coefficients):
    return payload_lines * lax.rsqrt(lax.optimization_barrier(jnp.mean(payload_lines * payload_lines, axis=-1, keepdims=True)) + 1e-05) * rescale_coefficients

def unit_heads(payload_lines):
    shaped = payload_lines.reshape(payload_lines.shape[:-1] + (payload_lines.shape[-1] // HEAD_DIM, HEAD_DIM))
    scaled = shaped * lax.rsqrt(lax.optimization_barrier(jnp.mean(shaped * shaped, axis=-1, keepdims=True)) + 1e-06)
    return scaled * HEAD_DIM ** (-0.5)

def swap_there_and_home(payload_lines):
    return lax.optimization_barrier(payload_lines.astype(jnp.bfloat16)).astype(jnp.float32)

def quarter_table():
    cell_index = jnp.arange(64, dtype=jnp.int32)
    quarter_index = cell_index // 32 * 2 + cell_index % 8 // 4
    return (quarter_index[:, None] == jnp.arange(4, dtype=jnp.int32)[None, :]).astype(jnp.float32)

def to_windows(field_grid):
    tile_rows, tile_cols, channels = field_grid.shape
    shaped = field_grid.reshape(tile_rows // 8, 8, tile_cols // 8, 8, channels)
    return jnp.transpose(shaped, (0, 2, 1, 3, 4)).reshape(-1, 64, channels)

def from_windows(blocks, tile_rows, tile_cols):
    channels = blocks.shape[-1]
    shaped = blocks.reshape(tile_rows // 8, tile_cols // 8, 8, 8, channels)
    return jnp.transpose(shaped, (0, 2, 1, 3, 4)).reshape(tile_rows, tile_cols, channels)

def to_quarters(field_grid):
    quarter_rows, quarter_cols, channels = field_grid.shape
    shaped = field_grid.reshape(quarter_rows // 2, 2, quarter_cols // 2, 2, channels)
    return jnp.transpose(shaped, (0, 2, 1, 3, 4)).reshape(-1, 4, channels)

def bearer_linear_map(latent_activation, linear_coefficients):
    channels = latent_activation.shape[-1]
    convex_combination = jnp.dot(latent_activation, linear_coefficients, preferred_element_type=jnp.float32)
    asker_lines = unit_heads(convex_combination[:, :channels]).reshape(-1, channels)
    collected_probes = lax.optimization_barrier(unit_heads(convex_combination[:, channels:2 * channels]).reshape(-1, channels).astype(jnp.bfloat16))
    collected_payloads = lax.optimization_barrier(convex_combination[:, 2 * channels:].astype(jnp.bfloat16))
    return (asker_lines, collected_probes, collected_payloads)

def cluster_softmax_apply(asker_lines, collected_probes, collected_payloads, subspace_tempers):
    asker_subspaces = asker_lines.reshape(asker_lines.shape[0], -1, HEAD_DIM)
    probe_subspaces = collected_probes.reshape(collected_probes.shape[0], -1, HEAD_DIM)
    payload_subspaces = collected_payloads.reshape(collected_payloads.shape[0], -1, HEAD_DIM)
    scores = jnp.einsum('qhd,khd->hqk', asker_subspaces, probe_subspaces, precision=lax.Precision.HIGHEST) * subspace_tempers[:, None, None]
    weights = jnp.exp(scores)
    aggregate_sums = lax.optimization_barrier(jnp.sum(weights, axis=-1))
    softmax_combined = jnp.einsum('hqk,khd->qhd', weights, payload_subspaces, precision=lax.Precision.HIGHEST)
    softmax_combined = softmax_combined / jnp.transpose(aggregate_sums)[:, :, None]
    return softmax_combined.reshape(asker_lines.shape[0], -1)

def patch_softmax_update(lattice_site_lines, bearer_embeddings, rescale_coefficients, triple_linear_map, exit_linear_map, subspace_tempers):
    window_count, cell_count, channels = lattice_site_lines.shape
    merged_embeddings = jnp.concatenate([lattice_site_lines, bearer_embeddings], axis=1)
    latent_activation = standardized_lines(merged_embeddings, rescale_coefficients).astype(jnp.bfloat16)
    convex_combination = jnp.dot(latent_activation.reshape(-1, channels), triple_linear_map, preferred_element_type=jnp.float32)
    convex_combination = convex_combination.reshape(window_count, merged_embeddings.shape[1], 3 * channels)
    asker_subspaces = unit_heads(convex_combination[:, :cell_count, :channels])
    probe_subspaces = swap_there_and_home(unit_heads(convex_combination[:, :, channels:2 * channels]))
    payload_subspaces = swap_there_and_home(convex_combination[:, :, 2 * channels:]).reshape(window_count, merged_embeddings.shape[1], -1, HEAD_DIM)
    scores = jnp.einsum('wqhd,wkhd->whqk', asker_subspaces, probe_subspaces, precision=lax.Precision.HIGHEST)
    weights = jnp.exp(scores * subspace_tempers[None, :, None, None])
    aggregate_sums = lax.optimization_barrier(jnp.sum(weights, axis=-1))
    softmax_combined = jnp.einsum('whqk,wkhd->wqhd', weights, payload_subspaces, precision=lax.Precision.HIGHEST)
    softmax_combined = softmax_combined / jnp.transpose(aggregate_sums, (0, 2, 1))[:, :, :, None]
    softmax_combined = softmax_combined.reshape(window_count, cell_count, channels).astype(jnp.bfloat16)
    projected_tokens = jnp.dot(softmax_combined.reshape(-1, channels), exit_linear_map, preferred_element_type=jnp.float32)
    projected_tokens = projected_tokens.reshape(window_count, cell_count, channels)
    scattered_embeddings = jnp.einsum('qd,ndl->nql', quarter_table(), bearer_embeddings, precision=lax.Precision.HIGHEST)
    return (lattice_site_lines + projected_tokens + scattered_embeddings).astype(jnp.bfloat16)

def primal_evaluation(lattice_site_embedding, patch_rescale_coeffs, patch_triple_linear, patch_exit_linear, patch_logit_temper, bearer_rescale_coeffs, bearer_triple_linear, bearer_exit_linear, bearer_logit_temper, bearer_sequence_place):
    whole_grid = lattice_site_embedding.astype(jnp.float32)
    padded = jnp.concatenate([whole_grid[4:], jnp.zeros((4, NLON, EMBEDDING_SIZE), jnp.float32)], axis=0)
    shifted = jnp.roll(padded, -4, axis=1)
    averaged_embeddings = shifted.reshape(BEARER_LINES, 4, BEARER_COLUMNS, 4, EMBEDDING_SIZE).mean(axis=(1, 3))
    bearer_embeddings = swap_there_and_home(averaged_embeddings)
    holder_chip_number = (bearer_sequence_place // BEARERS_PER_CHIP).astype(jnp.int32)
    chip_line_band = (jnp.arange(BEARER_LINES, dtype=jnp.int32) // (TILE_LINE_COUNT // 4))[:, None]
    bearer_seat_number = (chip_line_band * BEARERS_PER_CHIP + bearer_sequence_place % BEARERS_PER_CHIP).astype(jnp.int32)
    cluster_embeddings = jnp.zeros((N_LON, BEARERS_PER_SET, EMBEDDING_SIZE), jnp.float32).at[holder_chip_number, bearer_seat_number].set(bearer_embeddings)
    latent_activation = standardized_lines(cluster_embeddings, bearer_rescale_coeffs).astype(jnp.bfloat16)
    asker_lines, collected_probes, collected_payloads = bearer_linear_map(latent_activation.reshape(-1, EMBEDDING_SIZE), bearer_triple_linear)

    def cluster_softmax_mix(portions):
        return cluster_softmax_apply(portions[0], portions[1].astype(jnp.float32), portions[2].astype(jnp.float32), bearer_logit_temper)
    softmax_combined = lax.map(cluster_softmax_mix, (asker_lines.reshape(N_LON, BEARERS_PER_SET, EMBEDDING_SIZE), collected_probes.reshape(N_LON, BEARERS_PER_SET, EMBEDDING_SIZE), collected_payloads.reshape(N_LON, BEARERS_PER_SET, EMBEDDING_SIZE)))
    blended_activation = jnp.dot(softmax_combined.reshape(-1, EMBEDDING_SIZE).astype(jnp.bfloat16), bearer_exit_linear, preferred_element_type=jnp.float32)
    refreshed_activation = (cluster_embeddings + blended_activation.reshape(N_LON, BEARERS_PER_SET, EMBEDDING_SIZE)).astype(jnp.bfloat16)
    brought_home = lax.optimization_barrier(refreshed_activation[holder_chip_number, bearer_seat_number]).astype(jnp.float32)
    cell_blocks = to_windows(shifted).reshape(NLAT // 8, -1, 64, EMBEDDING_SIZE)
    quarters = to_quarters(brought_home).reshape(NLAT // 8, -1, 4, EMBEDDING_SIZE)

    def patchwise_softmax_mix(portions):
        return patch_softmax_update(portions[0], portions[1], patch_rescale_coeffs, patch_triple_linear, patch_exit_linear, patch_logit_temper)
    outputs = lax.map(patchwise_softmax_mix, (cell_blocks, quarters))
    return from_windows(outputs.reshape(-1, 64, EMBEDDING_SIZE), NLAT, NLON)

def reference(lattice_site_embedding, final_lattice_sensitivity, patch_rescale_coeffs, patch_triple_linear, patch_exit_linear, patch_logit_temper, bearer_rescale_coeffs, bearer_triple_linear, bearer_exit_linear, bearer_logit_temper, bearer_sequence_place):

    def apply_block(complete_lattice):
        return primal_evaluation(complete_lattice, patch_rescale_coeffs, patch_triple_linear, patch_exit_linear, patch_logit_temper, bearer_rescale_coeffs, bearer_triple_linear, bearer_exit_linear, bearer_logit_temper, bearer_sequence_place)
    out_field, pullback = jax.vjp(apply_block, lattice_site_embedding)
    field_grad = pullback(final_lattice_sensitivity)[0]
    return (out_field, field_grad)
```

```python
import types

import jax
import jax.numpy as jnp
from jax import lax
from jax.experimental import pallas as pl
from jax.experimental.pallas import tpu as pltpu
from jax.sharding import PartitionSpec as P

BF = jnp.bfloat16
F32 = jnp.float32
LOG2E = 1.4426950408889634
LN2 = 0.6931471805599453
D = 768
GROUPS = 3
WINDOWS = 16
CELLS = 64


def nn(a, b):
    return lax.dot_general(a, b, (((1,), (0,)), ((), ())), preferred_element_type=F32)


def nt(a, b):
    return lax.dot_general(a, b, (((1,), (1,)), ((), ())), preferred_element_type=F32)


def tn(a, b):
    return lax.dot_general(a, b, (((0,), (0,)), ((), ())), preferred_element_type=F32)


def iota(shape, axis):
    return lax.broadcasted_iota(jnp.int32, shape, axis)


def one_where(condition):
    return jnp.where(condition, 1.0, 0.0).astype(BF)


def lanes(n):
    return slice(n * 256, (n + 1) * 256)


def fill_constants(k):
    k.heads[...] = one_where(iota((256, 256), 0) // 64 == iota((256, 256), 1) // 64)
    k.carrier_heads[...] = one_where(iota((64, D), 0) % 16 == iota((64, D), 1) // 64)
    k.spread[...] = one_where(iota((1024, 64), 0) // 16 == iota((1024, 64), 1))
    k.gather[...] = one_where(iota((64, 1024), 1) // 16 == iota((64, 1024), 0))


def rms_inverse(x):
    return lax.rsqrt(jnp.mean(x * x, axis=-1, keepdims=True) + 1e-05)


def rms_back(x, gain, grad):
    inverse = rms_inverse(x)
    scaled = grad * gain
    along = jnp.mean(x * scaled, axis=-1, keepdims=True)
    return inverse * (scaled - x * (inverse * inverse * along))


def unit_scale(u, heads):
    return lax.rsqrt(nn((u * u).astype(BF), heads) + 64e-06)


def key_back(scale, key, grad, heads):
    along = nn((key * grad).astype(BF), heads)
    return scale * (grad - key * along)


def query_back(scale, query, temper, raw, heads):
    along = nn((query * raw).astype(BF), heads)
    return scale * (temper * raw - query * along * (LN2 * LN2 / temper))


def block_diagonal(rows, heads):
    return jnp.concatenate([rows] * 4, axis=0) * heads


def cells_project(k, chunk):
    rows = pl.ds(pl.multiple_of(chunk * 256, 256), 256)
    x = k.x[rows, :].astype(F32)
    hidden = (x * rms_inverse(x) * k.gain[...]).astype(BF)
    heads = k.heads[...]
    for n in range(GROUPS):
        u = nn(hidden, k.w[:, lanes(n)])
        scale = unit_scale(u, heads)
        k.sq[rows, lanes(n)] = scale
        k.q[rows, lanes(n)] = (u * scale * (k.temper[:, lanes(n)] * LOG2E)).astype(BF)
    for n in range(GROUPS):
        u = nn(hidden, k.w[:, lanes(3 + n)])
        scale = unit_scale(u, heads)
        k.sk[rows, lanes(n)] = scale
        k.k[rows, lanes(n)] = (u * scale).astype(BF)
    for n in range(GROUPS):
        k.v[rows, lanes(n)] = nn(hidden, k.w[:, lanes(6 + n)]).astype(BF)


def cells_sensitivity(k, chunk):
    rows = pl.ds(pl.multiple_of(chunk * 256, 256), 256)
    k.do[rows, :] = nt(k.g[rows, :], k.we[...]).astype(BF)


def window_rows(w):
    return pl.ds(pl.multiple_of(w * CELLS, CELLS), CELLS)


def cells_attend(k, w):
    rows = window_rows(w)
    heads = k.heads[...]
    for n in range(GROUPS):
        keys = block_diagonal(k.k[rows, lanes(n)], heads)
        values = block_diagonal(k.v[rows, lanes(n)], heads)
        weights = jnp.exp2(nt(k.q[rows, lanes(n)], keys)).astype(BF)
        k.p[rows, lanes(n)] = weights
        k.op[rows, lanes(n)] = nn(weights, values)
        k.lp[rows, lanes(n)] = nn(weights, heads)


def carriers_project(k):
    c = k.cn[...].astype(F32)
    hidden = (c * rms_inverse(c) * k.gain[...]).astype(BF)
    heads = k.heads[...]
    for n in range(GROUPS):
        u = nn(hidden, k.w[:, lanes(3 + n)])
        scale = unit_scale(u, heads)
        k.skc[:, lanes(n)] = scale
        key = (u * scale).astype(BF)
        k.kc[:, lanes(n)] = key
        value = nn(hidden, k.w[:, lanes(6 + n)]).astype(BF)
        k.vc[:, lanes(n)] = value
    for chunk in range(4):
        rows = slice(chunk * 256, (chunk + 1) * 256)
        mask = jnp.concatenate([k.carrier_heads[...]] * 4, axis=0)
        k.kcb[rows, :] = nn(k.spread[rows, :], k.kc[...]).astype(BF) * mask
        k.vcb[rows, :] = nn(k.spread[rows, :], k.vc[...]).astype(BF) * mask


def window_finish(k, w):
    rows = window_rows(w)
    mask = k.carrier_heads[...]
    keys, values = k.kcb[rows, :], k.vcb[rows, :]
    query = k.q[rows, :]
    weights = jnp.exp2(nt(query, keys)).astype(BF)
    inverse = 1.0 / (k.lp[rows, :] + nn(weights, mask))
    attended = (k.op[rows, :] + nn(weights, values)) * inverse
    k.o[rows, :] = attended.astype(BF)
    sensitivity = k.do[rows, :].astype(F32) * inverse
    product = (sensitivity * attended).astype(BF)
    k.t[rows, :] = product
    sensitivity = sensitivity.astype(BF)
    k.do[rows, :] = sensitivity
    grads = weights.astype(F32) * (nt(sensitivity, values) - nt(product, mask))
    grads = grads.astype(BF)
    k.op[rows, :] = nn(grads, keys)
    k.kcb[rows, :] = (tn(grads, query) * LN2).astype(BF) * mask
    k.vcb[rows, :] = tn(weights, sensitivity).astype(BF) * mask


def carriers_back(k):
    heads = k.heads[...]
    select = k.gather[...]
    grad = jnp.zeros((64, D), F32)
    for n in range(GROUPS):
        dk = nn(select, k.kcb[:, lanes(n)])
        du = key_back(k.skc[:, lanes(n)], k.kc[:, lanes(n)].astype(F32), dk, heads)
        grad += nt(du.astype(BF), k.w[:, lanes(3 + n)])
        dv = nn(select, k.vcb[:, lanes(n)]).astype(BF)
        grad += nt(dv, k.w[:, lanes(6 + n)])
    grad = grad.astype(BF).astype(F32)
    back = rms_back(k.cn[...].astype(F32), k.gain[...], grad)
    k.dcn[...] = (back + nn(select, k.g[...])).astype(BF)


def cells_result(k, chunk):
    rows = pl.ds(pl.multiple_of(chunk * 256, 256), 256)
    total = k.x[rows, :].astype(F32) + nn(k.o[rows, :], k.we[...])
    k.out[rows, :] = (total + nn(k.spread[rows, :], k.cn[...])).astype(BF)


def cells_back(k, w):
    rows = window_rows(w)
    heads = k.heads[...]
    low = iota((64, 128), 1) < 64
    for n in range(GROUPS):
        query, key = k.q[rows, lanes(n)], k.k[rows, lanes(n)]
        weights, sensitivity = k.p[rows, lanes(n)], k.do[rows, lanes(n)]
        values = block_diagonal(k.v[rows, lanes(n)], heads)
        offset = nn(k.t[rows, lanes(n)], heads)
        grads = (weights.astype(F32) * (nt(sensitivity, values) - offset)).astype(BF)
        raw = k.op[rows, lanes(n)] + nn(grads, block_diagonal(key, heads))
        k.dqkv[rows, lanes(n)] = query_back(
            k.sq[rows, lanes(n)], query.astype(F32), k.temper[:, lanes(n)], raw, heads
        ).astype(BF)
        key_parts, value_parts = [], []
        for pair in range(2):
            part = slice(pair * 128, (pair + 1) * 128)
            both = tn(grads[:, part], query[:, part])
            key_parts.append(jnp.where(low, both[:64], both[64:]))
            both = tn(weights[:, part], sensitivity[:, part])
            value_parts.append(jnp.where(low, both[:64], both[64:]))
        dk = (jnp.concatenate(key_parts, axis=1) * LN2).astype(BF).astype(F32)
        k.dqkv[rows, lanes(3 + n)] = key_back(
            k.sk[rows, lanes(n)], key.astype(F32), dk, heads
        ).astype(BF)
        k.dqkv[rows, lanes(6 + n)] = jnp.concatenate(value_parts, axis=1).astype(BF)


def cells_gradient(k, chunk):
    rows = pl.ds(pl.multiple_of(chunk * 256, 256), 256)
    grad = nt(k.dqkv[rows, :], k.w[...]).astype(BF).astype(F32)
    back = rms_back(k.x[rows, :].astype(F32), k.gain[...], grad)
    k.dx[rows, :] = (back + k.g[rows, :].astype(F32)).astype(BF)


def group_forward(k):
    c = k.car[...].astype(F32)
    hidden = (c * rms_inverse(c) * k.cgain[...]).astype(BF)
    heads = k.heads[...]
    for n in range(GROUPS):
        u = nn(hidden, k.cw[:, lanes(n)])
        scale = unit_scale(u, heads)
        k.csq[:, lanes(n)] = scale[:64]
        query = (u * scale * (k.ctemper[:, lanes(n)] * LOG2E)).astype(BF)
        k.cq[:, lanes(n)] = query
        u = nn(hidden, k.cw[:, lanes(3 + n)])
        scale = unit_scale(u, heads)
        k.csk[:, lanes(n)] = scale[:64]
        key = (u * scale).astype(BF)
        k.ck[:, lanes(n)] = key
        value = nn(hidden, k.cw[:, lanes(6 + n)]).astype(BF)
        k.cv[:, lanes(n)] = value
        total = jnp.zeros((256, 256), F32)
        denominator = jnp.zeros((256, 256), F32)
        for h in range(4):
            mine = one_where(iota((256, 256), 1) // 64 == h)
            weights = jnp.exp2(nt(query, key * mine)).astype(BF)
            k.cp[n * 4 + h] = weights
            total += nn(weights, value * mine)
            denominator += nn(weights, mine)
        inverse = 1.0 / denominator
        k.cl[:, lanes(n)] = inverse
        k.co[:, lanes(n)] = total * inverse
    mixed = nn(k.co[:64, :].astype(BF), k.cwe[...])
    k.cnew[...] = (k.car[:64, :].astype(F32) + mixed).astype(BF)


def group_back(k):
    heads = k.heads[...]
    grad = jnp.zeros((64, D), F32)
    for n in range(GROUPS):
        sensitivity = nt(k.cgrad[...], k.cwe[lanes(n), :]).astype(BF).astype(F32)
        sensitivity = sensitivity * k.cl[:, lanes(n)]
        product = (sensitivity * k.co[:, lanes(n)]).astype(BF)
        sensitivity = sensitivity.astype(BF)
        query, key, value = k.cq[:, lanes(n)], k.ck[:, lanes(n)], k.cv[:, lanes(n)]
        raw = jnp.zeros((64, 256), F32)
        dk = jnp.zeros((64, 256), F32)
        dv = jnp.zeros((64, 256), F32)
        for h in range(4):
            mine = one_where(iota((256, 256), 1) // 64 == h)
            ones = one_where(iota((256, 256), 0) // 64 == h)
            own = jnp.where(iota((64, 256), 1) // 64 == h, 1.0, 0.0)
            weights = k.cp[n * 4 + h]
            along = nt(sensitivity, value * mine) - nn(product, ones)
            grads = (weights.astype(F32) * along).astype(BF)
            raw += nn(grads[:64, :], key * mine)
            dk += tn(grads[:, :128], query)[:64] * own
            dv += tn(weights[:, :128], sensitivity)[:64] * own
        du = query_back(
            k.csq[:, lanes(n)], query[:64].astype(F32), k.ctemper[:, lanes(n)], raw, heads
        )
        grad += nt(du.astype(BF), k.cw[:, lanes(n)])
        dk = (dk * LN2).astype(BF).astype(F32)
        du = key_back(k.csk[:, lanes(n)], key[:64].astype(F32), dk, heads)
        grad += nt(du.astype(BF), k.cw[:, lanes(3 + n)])
        grad += nt(dv.astype(BF), k.cw[:, lanes(6 + n)])
    grad = grad.astype(BF).astype(F32)
    back = rms_back(k.car[:64, :].astype(F32), k.cgain[...], grad)
    k.cback[...] = (back + k.cgrad[:64, :].astype(F32)).astype(BF)


CONSTANTS = {
    "heads": ((256, 256), BF),
    "carrier_heads": ((64, D), BF),
    "spread": ((1024, 64), BF),
    "gather": ((64, 1024), BF),
}
WINDOW_SCRATCH = {
    "q": ((1024, D), BF),
    "k": ((1024, D), BF),
    "v": ((1024, D), BF),
    "do": ((1024, D), BF),
    "o": ((1024, D), BF),
    "t": ((1024, D), BF),
    "p": ((1024, D), BF),
    "sq": ((1024, D), F32),
    "sk": ((1024, D), F32),
    "op": ((1024, D), F32),
    "lp": ((1024, D), F32),
    "kcb": ((1024, D), BF),
    "vcb": ((1024, D), BF),
    "kc": ((64, D), BF),
    "vc": ((64, D), BF),
    "skc": ((64, D), F32),
    "dqkv": ((1024, 3 * D), BF),
}
GROUP_SCRATCH = {
    "cq": ((256, D), BF),
    "ck": ((256, D), BF),
    "cv": ((256, D), BF),
    "cp": ((12, 256, 256), BF),
    "csq": ((64, D), F32),
    "csk": ((64, D), F32),
    "cl": ((256, D), F32),
    "co": ((256, D), F32),
}


def call(body, inputs, outputs, scratch, name):
    names = list(inputs) + list(outputs) + list(scratch)

    def kernel(*refs):
        body(types.SimpleNamespace(**dict(zip(names, refs))))

    return pl.pallas_call(
        kernel,
        out_shape=[jax.ShapeDtypeStruct(shape, kind) for shape, kind in outputs.values()],
        in_specs=[pl.BlockSpec(memory_space=pltpu.VMEM)] * len(inputs),
        out_specs=[pl.BlockSpec(memory_space=pltpu.VMEM)] * len(outputs),
        scratch_shapes=[pltpu.VMEM(shape, kind) for shape, kind in scratch.values()],
        compiler_params=pltpu.CompilerParams(vmem_limit_bytes=60 * 1024 * 1024),
        name=name,
    )(*inputs.values())


def loop(count, step, k):
    lax.fori_loop(0, count, lambda i, _: (step(k, i), 0)[1], 0)


def window_body(k):
    fill_constants(k)
    loop(4, cells_project, k)
    loop(4, cells_sensitivity, k)
    loop(WINDOWS, cells_attend, k)
    carriers_project(k)
    loop(WINDOWS, window_finish, k)
    carriers_back(k)
    loop(4, cells_result, k)
    loop(WINDOWS, cells_back, k)
    loop(4, cells_gradient, k)


def group_forward_body(k):
    fill_heads(k)
    group_forward(k)


def group_back_body(k):
    fill_heads(k)
    group_forward(k)
    group_back(k)


def fill_heads(k):
    k.heads[...] = one_where(iota((256, 256), 0) // 64 == iota((256, 256), 1) // 64)


def lat_pass(value, steps):
    count = lax.axis_size("lat")
    first, last = (max(0, -steps), min(count, count - steps))
    return lax.ppermute(value, "lat", [(i, i + steps) for i in range(first, last)])


def lon_pass(value, steps):
    count = lax.axis_size("lon")
    return lax.ppermute(value, "lon", [(i, (i + steps) % count) for i in range(count)])


def route(rows):
    return lax.all_to_all(rows, "lon", split_axis=0, concat_axis=0, tiled=True)


def to_windows(grid):
    shaped = grid.reshape(16, 8, 2, 4, D)
    return jnp.transpose(shaped, (0, 2, 1, 3, 4)).reshape(1024, D)


def from_windows(rows):
    shaped = rows.reshape(16, 2, 8, 4, D)
    return jnp.transpose(shaped, (0, 2, 1, 3, 4)).reshape(128, 8, D)


def gather_group(rows):
    everyone = lax.all_gather(rows, "lat", axis=0, tiled=True)
    twice = jnp.concatenate([everyone, everyone], axis=0)
    return lax.dynamic_slice_in_dim(twice, lax.axis_index("lat") * 64, 256, axis=0)


def per_device(x, g, gain, w, we, temper, cgain, cw, cwe, ctemper, place):
    below = lat_pass(x[:4], -1)
    extended = jnp.concatenate([x[4:], below], axis=0)
    beside = lon_pass(extended[:, :4], -1)
    shifted = jnp.concatenate([extended[:, 4:], beside], axis=1)
    xw = to_windows(shifted)
    gw = to_windows(g)
    carriers = xw.astype(F32).reshape(64, 16, D).mean(axis=1).astype(BF)
    places = jnp.transpose(place.reshape(16, 2, 2), (0, 2, 1)).reshape(-1)
    slot = places // 64 * 2 + places % 2
    choose = (slot[None, :] == jnp.arange(64, dtype=jnp.int32)[:, None]).astype(BF)

    def to_owner(rows):
        return route(jnp.dot(choose, rows, preferred_element_type=F32).astype(BF))

    def to_home(rows):
        return jnp.dot(choose.T, route(rows), preferred_element_type=F32).astype(BF)

    temper = jnp.repeat(temper, 64)[None, :]
    ctemper = jnp.repeat(ctemper, 64)[None, :]
    gain, cgain = gain[None, :], cgain[None, :]
    group_inputs = {
        "car": gather_group(to_owner(carriers)),
        "cgain": cgain,
        "cw": cw,
        "cwe": cwe,
        "ctemper": ctemper,
    }
    heads = {"heads": CONSTANTS["heads"]}
    (cnew,) = call(
        group_forward_body,
        group_inputs,
        {"cnew": ((64, D), BF)},
        heads | GROUP_SCRATCH,
        "group_forward",
    )
    cn = to_home(cnew)
    out, dx, dcn = call(
        window_body,
        {"x": xw, "g": gw, "cn": cn, "gain": gain, "w": w, "we": we, "temper": temper},
        {"out": ((1024, D), BF), "dx": ((1024, D), BF), "dcn": ((64, D), BF)},
        CONSTANTS | WINDOW_SCRATCH,
        "windows",
    )
    cgrad = gather_group(to_owner(dcn))
    cback, _ = call(
        group_back_body,
        group_inputs | {"cgrad": cgrad},
        {"cback": ((64, D), BF), "cnew": ((64, D), BF)},
        heads | GROUP_SCRATCH,
        "group_back",
    )
    pooled = to_home(cback).astype(F32) / 16.0
    total = dx.reshape(64, 16, D).astype(F32) + pooled[:, None, :]
    grad_shifted = from_windows(total.astype(BF).reshape(1024, D))
    beside = lon_pass(grad_shifted[:, 4:], 1)
    grad_extended = jnp.concatenate([beside, grad_shifted[:, :4]], axis=1)
    below = lat_pass(grad_extended[124:], 1)
    field_grad = jnp.concatenate([below, grad_extended[:124]], axis=0)
    return from_windows(out), field_grad


def solution(mesh):
    placed = (P("lat", "lon", None),) * 2 + (P(),) * 8 + (P("lat", "lon"),)
    return jax.shard_map(
        per_device,
        mesh=mesh,
        in_specs=placed,
        out_specs=(P("lat", "lon", None),) * 2,
        check_vma=False,
    )
```

```python
import types

import jax
import jax.numpy as jnp
from jax import lax
from jax.experimental import pallas as pl
from jax.experimental.pallas import tpu as pltpu
from jax.sharding import PartitionSpec as P

BF = jnp.bfloat16
F32 = jnp.float32
LOG2E = 1.4426950408889634
LN2 = 0.6931471805599453
D = 768
GROUPS = 3
WINDOWS = 16
CELLS = 64
HALF = 512
MESH = pl.DeviceIdType.MESH


def nn(a, b):
    return lax.dot_general(a, b, (((1,), (0,)), ((), ())), preferred_element_type=F32)


def nt(a, b):
    return lax.dot_general(a, b, (((1,), (1,)), ((), ())), preferred_element_type=F32)


def tn(a, b):
    return lax.dot_general(a, b, (((0,), (0,)), ((), ())), preferred_element_type=F32)


def iota(shape, axis):
    return lax.broadcasted_iota(jnp.int32, shape, axis)


def one_where(condition):
    return jnp.where(condition, 1.0, 0.0).astype(BF)


def lanes(n):
    return slice(n * 256, (n + 1) * 256)


def fill_constants(k):
    k.heads[...] = one_where(iota((256, 256), 0) // 64 == iota((256, 256), 1) // 64)
    k.carrier_heads[...] = one_where(iota((256, D), 0) % 16 == iota((256, D), 1) // 64)
    k.same[...] = one_where(iota((256, 256), 0) % 128 // 32 == iota((256, 256), 1) % 128 // 32)
    k.spread[...] = one_where(iota((1024, 64), 0) // 16 == iota((1024, 64), 1))
    k.gather[...] = one_where(iota((64, 1024), 1) // 16 == iota((64, 1024), 0))
    split, cell = iota((256, 256), 0), iota((256, 256), 1)
    k.split[...] = one_where(cell == split % 128 // 4 * 8 + split // 128 * 4 + split % 4)
    cell, split = iota((256, 256), 0), iota((256, 256), 1)
    k.join[...] = one_where(cell == split % 128 // 4 * 8 + split // 128 * 4 + split % 4)
    row, slab = iota((384, HALF), 0), iota((384, HALF), 1)
    member = row % 64
    k.unpack[...] = one_where(slab == member // 2 * 16 + row // 64 * 2 + member % 2)
    k.gain[...] = k.gains[...].reshape(1, D)
    k.cgain[...] = k.cgains[...].reshape(1, D)
    lane = iota((1, D), 1) // 64
    for tempers, wide in ((k.tempers, k.temper), (k.ctempers, k.ctemper)):
        total = jnp.zeros((1, D), F32)
        for h in range(12):
            total = jnp.where(lane == h, tempers[h], total)
        wide[...] = total


def fill_routes(k, lon):
    slab = iota((32, HALF), 1)
    eye = jnp.where(iota((32, 32), 0) == iota((32, 32), 1), 1.0, 0.0)
    for b in range(2):
        place = k.place[b : b + 1, :]
        place = jnp.sum(jnp.where(eye > 0, place, 0), axis=1, keepdims=True)
        partner = (place // 64 - lon + 32) % 32
        slot = partner * 16 + place % 2
        for c in range(6):
            rows = slice(b * 192 + c * 32, b * 192 + c * 32 + 32)
            k.routes[rows, :] = one_where(slab == slot + 2 * c)


def pack(matrix, parts):
    return tn(matrix, jnp.concatenate(parts, axis=0)).astype(BF).reshape(32, 16, 128)


def lane_parts(rows):
    return [rows[:, c * 128 : (c + 1) * 128] for c in range(6)]


def pack_home(k, rows):
    return pack(k.routes[...], lane_parts(rows[:32]) + lane_parts(rows[32:]))


def unpack_home(k, slabs):
    parts = nn(k.routes[...], slabs[...].reshape(HALF, 128)).astype(BF)
    sides = []
    for b in range(2):
        pieces = [parts[b * 192 + c * 32 : b * 192 + c * 32 + 32] for c in range(6)]
        sides.append(jnp.concatenate(pieces, axis=1))
    return jnp.concatenate(sides, axis=0)


def pack_owner(k, rows):
    return pack(k.unpack[...], lane_parts(rows))


def unpack_owner(k, slabs):
    parts = nn(k.unpack[...], slabs[...].reshape(HALF, 128)).astype(BF)
    return jnp.concatenate([parts[c * 64 : c * 64 + 64] for c in range(6)], axis=1)


def rms_inverse(x):
    return lax.rsqrt(jnp.mean(x * x, axis=-1, keepdims=True) + 1e-05)


def rms_back(x, gain, grad):
    inverse = rms_inverse(x)
    scaled = grad * gain
    along = jnp.mean(x * scaled, axis=-1, keepdims=True)
    return inverse * (scaled - x * (inverse * inverse * along))


def unit_scale(u, heads):
    return lax.rsqrt(nn((u * u).astype(BF), heads) + 64e-06)


def key_back(scale, key, grad, heads):
    along = nn((key * grad).astype(BF), heads)
    return scale * (grad - key * along)


def query_back(scale, query, temper, raw, heads):
    along = nn((query * raw).astype(BF), heads)
    return scale * (temper * raw - query * along * (LN2 * LN2 / temper))


def block_diagonal(rows, heads):
    return jnp.concatenate([rows] * 4, axis=0) * heads


def chunk_rows(chunk):
    return pl.ds(pl.multiple_of(chunk * 256, 256), 256)


def both(ref, quad, columns=slice(None)):
    first = pl.multiple_of(quad * 128, 128)
    return jnp.concatenate(
        [ref[pl.ds(first, 128), columns], ref[pl.ds(first + HALF, 128), columns]], axis=0
    )


def put_both(ref, quad, value, columns=slice(None)):
    first = pl.multiple_of(quad * 128, 128)
    ref[pl.ds(first, 128), columns] = value[:128]
    ref[pl.ds(first + HALF, 128), columns] = value[128:]


def window(rows, w):
    return jnp.concatenate([rows[w * 32 : w * 32 + 32], rows[w * 32 + 128 : w * 32 + 160]], axis=0)


def from_parts(parts):
    return jnp.concatenate([p[:32] for p in parts] + [p[32:] for p in parts], axis=0)


def cells_project(k, chunk):
    rows = chunk_rows(chunk)
    x = k.x[rows, :].astype(F32)
    hidden = (x * rms_inverse(x) * k.gain[...]).astype(BF)
    heads = k.heads[...]
    for n in range(GROUPS):
        u = nn(hidden, k.w[:, lanes(n)])
        scale = unit_scale(u, heads)
        k.sq[rows, lanes(n)] = scale
        k.q[rows, lanes(n)] = (u * scale * (k.temper[:, lanes(n)] * LOG2E)).astype(BF)
    for n in range(GROUPS):
        u = nn(hidden, k.w[:, lanes(3 + n)])
        scale = unit_scale(u, heads)
        k.sk[rows, lanes(n)] = scale
        k.k[rows, lanes(n)] = (u * scale).astype(BF)
    for n in range(GROUPS):
        k.v[rows, lanes(n)] = nn(hidden, k.w[:, lanes(6 + n)]).astype(BF)


def cells_sensitivity(k, quad):
    halves = nn(k.split[...], k.graw[chunk_rows(quad), :]).astype(BF)
    put_both(k.g, quad, halves)
    put_both(k.do, quad, nt(halves, k.we[...]).astype(BF))


def cells_attend(k, quad):
    heads = k.heads[...]
    for n in range(GROUPS):
        query, key, value = (both(ref, quad, lanes(n)) for ref in (k.q, k.k, k.v))
        weights, sums = [], []
        for w in range(4):
            keys = block_diagonal(window(key, w), heads)
            weights.append(jnp.exp2(nt(window(query, w), keys)).astype(BF))
        for w in range(4):
            sums.append(nn(weights[w], block_diagonal(window(value, w), heads)))
        weights = from_parts(weights)
        put_both(k.p, quad, weights, lanes(n))
        put_both(k.op, quad, from_parts(sums), lanes(n))
        put_both(k.lp, quad, nn(weights, heads), lanes(n))


def carriers_project(k):
    c = k.cn[...].astype(F32)
    hidden = (c * rms_inverse(c) * k.gain[...]).astype(BF)
    heads = k.heads[...]
    for n in range(GROUPS):
        u = nn(hidden, k.w[:, lanes(3 + n)])
        scale = unit_scale(u, heads)
        k.skc[:, lanes(n)] = scale
        key = (u * scale).astype(BF)
        k.kc[:, lanes(n)] = key
        value = nn(hidden, k.w[:, lanes(6 + n)]).astype(BF)
        k.vc[:, lanes(n)] = value
    for chunk in range(4):
        rows = slice(chunk * 256, (chunk + 1) * 256)
        mask = k.carrier_heads[...]
        k.kcb[rows, :] = nn(k.spread[rows, :], k.kc[...]).astype(BF) * mask
        k.vcb[rows, :] = nn(k.spread[rows, :], k.vc[...]).astype(BF) * mask


def windows_finish(k, quad):
    keys, values, query = both(k.kcb, quad), both(k.vcb, quad), both(k.q, quad)
    mask = k.carrier_heads[...]
    weights = jnp.exp2(nt(query, keys)).astype(BF) * k.same[...]
    along = jnp.zeros((256, 256), F32)
    for n in range(GROUPS):
        inverse = 1.0 / (both(k.lp, quad, lanes(n)) + nn(weights, mask[:, lanes(n)]))
        attended = both(k.op, quad, lanes(n)) + nn(weights, values[:, lanes(n)])
        attended = attended * inverse
        put_both(k.o, quad, attended.astype(BF), lanes(n))
        sensitivity = both(k.do, quad, lanes(n)).astype(F32) * inverse
        product = (sensitivity * attended).astype(BF)
        put_both(k.t, quad, product, lanes(n))
        sensitivity = sensitivity.astype(BF)
        put_both(k.do, quad, sensitivity, lanes(n))
        along += nt(sensitivity, values[:, lanes(n)]) - nt(product, mask[:, lanes(n)])
    grads = (weights.astype(F32) * along).astype(BF)
    for n in range(GROUPS):
        put_both(k.op, quad, nn(grads, keys[:, lanes(n)]), lanes(n))
    key_grads = (tn(grads, query) * LN2).astype(BF) * mask
    value_grads = tn(weights, both(k.do, quad)).astype(BF) * mask
    put_both(k.kcb, quad, key_grads)
    put_both(k.vcb, quad, value_grads)


def carriers_back(k):
    heads = k.heads[...]
    select = k.gather[...]
    grad = jnp.zeros((64, D), F32)
    for n in range(GROUPS):
        dk = nn(select, k.kcb[:, lanes(n)])
        du = key_back(k.skc[:, lanes(n)], k.kc[:, lanes(n)].astype(F32), dk, heads)
        grad += nt(du.astype(BF), k.w[:, lanes(3 + n)])
        dv = nn(select, k.vcb[:, lanes(n)]).astype(BF)
        grad += nt(dv, k.w[:, lanes(6 + n)])
    grad = grad.astype(BF).astype(F32)
    back = rms_back(k.cn[...].astype(F32), k.gain[...], grad)
    return (back + nn(select, k.g[...])).astype(BF)


def cells_result(k, quad):
    total = both(k.x, quad).astype(F32) + nn(both(k.o, quad), k.we[...])
    total = (total + nn(both(k.spread, quad), k.cn[...])).astype(BF)
    k.xraw[chunk_rows(quad), :] = nn(k.join[...], total).astype(BF)


def cells_back(k, quad):
    heads = k.heads[...]
    low = iota((64, 128), 1) < 64
    for n in range(GROUPS):
        query, key, value = (both(ref, quad, lanes(n)) for ref in (k.q, k.k, k.v))
        weights, sensitivity = (both(ref, quad, lanes(n)) for ref in (k.p, k.do))
        offset = nn(both(k.t, quad, lanes(n)), heads)
        along = []
        for w in range(4):
            values = block_diagonal(window(value, w), heads)
            along.append(nt(window(sensitivity, w), values))
        grads = (weights.astype(F32) * (from_parts(along) - offset)).astype(BF)
        raw, dk, dv = [], [], []
        for w in range(4):
            mine = window(grads, w)
            raw.append(nn(mine, block_diagonal(window(key, w), heads)))
            key_parts, value_parts = [], []
            for pair in range(2):
                part = slice(pair * 128, (pair + 1) * 128)
                pairs = tn(mine[:, part], window(query, w)[:, part])
                key_parts.append(jnp.where(low, pairs[:64], pairs[64:]))
                pairs = tn(window(weights, w)[:, part], window(sensitivity, w)[:, part])
                value_parts.append(jnp.where(low, pairs[:64], pairs[64:]))
            dk.append(jnp.concatenate(key_parts, axis=1))
            dv.append(jnp.concatenate(value_parts, axis=1))
        put_both(k.dqkv, quad, from_parts(dv).astype(BF), lanes(6 + n))
        raw = both(k.op, quad, lanes(n)) + from_parts(raw)
        scale = both(k.sq, quad, lanes(n))
        du = query_back(scale, query.astype(F32), k.temper[:, lanes(n)], raw, heads)
        put_both(k.dqkv, quad, du.astype(BF), lanes(n))
        dk = (from_parts(dk) * LN2).astype(BF).astype(F32)
        du = key_back(both(k.sk, quad, lanes(n)), key.astype(F32), dk, heads)
        put_both(k.dqkv, quad, du.astype(BF), lanes(3 + n))


def cells_gradient(k, chunk):
    rows = chunk_rows(chunk)
    grad = nt(k.dqkv[rows, :], k.w[...]).astype(BF).astype(F32)
    back = rms_back(k.x[rows, :].astype(F32), k.gain[...], grad)
    k.dx[rows, :] = (back + k.g[rows, :].astype(F32)).astype(BF)


def group_forward(k):
    c = k.car[...].astype(F32)
    hidden = (c * rms_inverse(c) * k.cgain[...]).astype(BF)
    heads = k.heads[...]
    for n in range(GROUPS):
        u = nn(hidden, k.cw[:, lanes(n)])
        scale = unit_scale(u, heads)
        k.csq[:, lanes(n)] = scale[:64]
        query = (u * scale * (k.ctemper[:, lanes(n)] * LOG2E)).astype(BF)
        k.cq[:, lanes(n)] = query
        u = nn(hidden, k.cw[:, lanes(3 + n)])
        scale = unit_scale(u, heads)
        k.csk[:, lanes(n)] = scale[:64]
        key = (u * scale).astype(BF)
        k.ck[:, lanes(n)] = key
        value = nn(hidden, k.cw[:, lanes(6 + n)]).astype(BF)
        k.cv[:, lanes(n)] = value
        total = jnp.zeros((256, 256), F32)
        denominator = jnp.zeros((256, 256), F32)
        for h in range(4):
            mine = one_where(iota((256, 256), 1) // 64 == h)
            weights = jnp.exp2(nt(query, key * mine)).astype(BF)
            k.cp[n * 4 + h] = weights
            total += nn(weights, value * mine)
            denominator += nn(weights, mine)
        inverse = 1.0 / denominator
        k.cl[:, lanes(n)] = inverse
        k.co[:, lanes(n)] = total * inverse
    mixed = nn(k.co[:64, :].astype(BF), k.cwe[...])
    return (k.car[:64, :].astype(F32) + mixed).astype(BF)


def group_back(k):
    heads = k.heads[...]
    grad = jnp.zeros((64, D), F32)
    for n in range(GROUPS):
        sensitivity = nt(k.cgrad[...], k.cwe[lanes(n), :]).astype(BF).astype(F32)
        sensitivity = sensitivity * k.cl[:, lanes(n)]
        product = (sensitivity * k.co[:, lanes(n)]).astype(BF)
        sensitivity = sensitivity.astype(BF)
        query, key, value = k.cq[:, lanes(n)], k.ck[:, lanes(n)], k.cv[:, lanes(n)]
        raw = jnp.zeros((64, 256), F32)
        dk = jnp.zeros((64, 256), F32)
        dv = jnp.zeros((64, 256), F32)
        for h in range(4):
            mine = one_where(iota((256, 256), 1) // 64 == h)
            ones = one_where(iota((256, 256), 0) // 64 == h)
            own = jnp.where(iota((64, 256), 1) // 64 == h, 1.0, 0.0)
            weights = k.cp[n * 4 + h]
            along = nt(sensitivity, value * mine) - nn(product, ones)
            grads = (weights.astype(F32) * along).astype(BF)
            raw += nn(grads[:64, :], key * mine)
            dk += tn(grads[:, :128], query)[:64] * own
            dv += tn(weights[:, :128], sensitivity)[:64] * own
        du = query_back(
            k.csq[:, lanes(n)], query[:64].astype(F32), k.ctemper[:, lanes(n)], raw, heads
        )
        grad += nt(du.astype(BF), k.cw[:, lanes(n)])
        dk = (dk * LN2).astype(BF).astype(F32)
        du = key_back(k.csk[:, lanes(n)], key[:64].astype(F32), dk, heads)
        grad += nt(du.astype(BF), k.cw[:, lanes(3 + n)])
        grad += nt(dv.astype(BF), k.cw[:, lanes(6 + n)])
    grad = grad.astype(BF).astype(F32)
    back = rms_back(k.car[:64, :].astype(F32), k.cgain[...], grad)
    return (back + k.cgrad[:64, :].astype(F32)).astype(BF)


def cells_split(k, quad):
    halves = nn(k.split[...], k.xraw[chunk_rows(quad), :]).astype(BF)
    first = quad * 128
    k.away[first : first + 128, :] = halves[:128]
    if quad == 0:
        k.rise[...] = halves[128:144]
        k.x[0:112, :] = halves[144:]
    else:
        k.x[first - 16 : first + 112, :] = halves[128:]
    means = nn(one_where(iota((16, 256), 1) // 16 == iota((16, 256), 0)), halves) * 0.0625
    k.means[0, quad * 8 : quad * 8 + 8, :] = means[:8]
    k.means[1, quad * 8 : quad * 8 + 8, :] = means[8:]


def field_rows(k, quad):
    first = quad * 128
    rows = slice(first, first + 128)
    mine = iota((128, 32), 0) // 16 + quad * 8 - 1 == iota((128, 32), 1)
    mine = one_where(mine)
    edge = one_where((iota((128, 16), 0) // 16 + quad * 8 == 0) & (iota((128, 16), 1) == 15))
    left = k.back[rows, :].astype(F32)
    left += (nn(mine, k.pool_beside[...]) + nn(edge, k.pool_corner[...])) * 0.0625
    if quad == 0:
        right = jnp.concatenate([k.fall[...], k.dx[0:112, :]], axis=0).astype(F32)
    else:
        right = k.dx[first - 16 : first + 112, :].astype(F32)
    right += (nn(mine, k.pool[0:32, :]) + nn(edge, k.pool_below[...])) * 0.0625
    both = jnp.concatenate([left.astype(BF), right.astype(BF)], axis=0)
    k.graw[quad * 256 : quad * 256 + 256, :] = nn(k.join[...], both).astype(BF)


def body(k):
    lat, lon = lax.axis_index("lat"), lax.axis_index("lon")
    has_above, has_below = lat > 0, lat < 3
    above, below = lax.rem(lat + 3, 4), lax.rem(lat + 1, 4)
    west, east = lax.rem(lon + 31, 32), lax.rem(lon + 1, 32)

    loads = []
    for i, (source, target) in enumerate(
        (
            (k.x_hbm, k.xraw),
            (k.w_hbm, k.w),
            (k.g_hbm, k.graw),
            (k.we_hbm, k.we),
            (k.cw_hbm, k.cw),
            (k.cwe_hbm, k.cwe),
        )
    ):
        load = pltpu.make_async_copy(source, target, k.load_sem.at[i])
        load.start()
        loads.append(load)
    load_x, load_w, load_g, load_we, load_cw, load_cwe = loads

    @pl.when(jnp.logical_not(has_below))
    def _():
        k.x[496:512, :] = jnp.zeros((16, D), BF)
        k.x[1008:1024, :] = jnp.zeros((16, D), BF)
        k.car_below[...] = jnp.zeros((16, D), BF)
        k.car_corner[...] = jnp.zeros((16, D), BF)

    @pl.when(jnp.logical_not(has_above))
    def _():
        k.back[0:16, :] = jnp.zeros((16, D), BF)
        k.fall[...] = jnp.zeros((16, D), BF)
        k.pool_below[...] = jnp.zeros((16, D), BF)
        k.pool_corner[...] = jnp.zeros((16, D), BF)

    barrier = pltpu.get_barrier_semaphore()

    def greet(to_lat, to_lon):
        pl.semaphore_signal(barrier, inc=1, device_id=(to_lat, to_lon), device_id_type=MESH)

    far, sibling = lax.rem(lat + 2, 4), lat // 2 * 2 + (1 - lat % 2)

    def greet_lon(i, carry):
        greet(lat, lax.rem(lon + i, 32))
        greet(far, lax.rem(lon + i, 32))
        return carry

    lax.fori_loop(1, 32, greet_lon, 0)
    for s in range(1, 4):
        greet(lax.rem(lat + s, 4), lon)
    greet(above, west)
    greet(below, east)

    def send(source, target, sem, to_lat, to_lon):
        return pltpu.make_async_remote_copy(
            src_ref=source,
            dst_ref=target,
            send_sem=k.send_sem.at[sem],
            recv_sem=k.recv_sem.at[sem],
            device_id=(to_lat, to_lon),
            device_id_type=MESH,
        )

    def start(copies):
        for copy in copies:
            copy.start()

    def wait_received(copies):
        for copy in copies:
            copy.wait_recv()

    def await_bytes(ref, sem):
        pltpu.make_async_copy(ref, ref, sem).wait()

    fill_constants(k)
    fill_routes(k, lon)

    load_x.wait()
    for quad in range(4):
        cells_split(k, quad)
    up = one_where(iota((32, 32), 1) == iota((32, 32), 0) + 1)
    top = one_where((iota((16, 32), 0) == 15) & (iota((16, 32), 1) == 0))
    left, right = k.means[0].astype(BF), k.means[1].astype(BF)
    k.car_send[0:32, :] = nn(up, left).astype(BF)
    k.car_send[32:48, :] = nn(top, left).astype(BF)
    k.car_send[48:64, :] = nn(top, right).astype(BF)
    own = nn(up, right)
    pl.semaphore_wait(barrier, 67)
    carriers_west = send(k.car_send.at[0:32], k.car_beside, 0, lat, west)
    carriers_corner = send(k.car_send.at[32:48], k.car_corner, 1, above, west)
    carriers_above = send(k.car_send.at[48:64], k.car_below, 2, above, lon)
    cells = []
    for first in range(0, 496, 64):
        last = min(first + 64, 496)
        cells.append(
            send(
                k.away.at[16 + first : 16 + last],
                k.x.at[512 + first : 512 + last],
                20 + first // 64,
                lat,
                west,
            )
        )
    cells_corner = send(k.away.at[0:16], k.x.at[1008:1024], 5, above, west)
    cells_above = send(k.rise, k.x.at[496:512], 6, above, lon)
    carriers_west.start()

    @pl.when(has_above)
    def _():
        carriers_corner.start()
        carriers_above.start()
        cells_above.start()
        cells_corner.start()

    start(cells[0:2])
    load_w.wait()
    cells_project(k, 0)
    load_g.wait()
    load_we.wait()
    loop(2, cells_sensitivity, k)

    carriers_west.wait_recv()

    @pl.when(has_below)
    def _():
        carriers_corner.wait_recv()
        carriers_above.wait_recv()

    lower = jnp.concatenate([jnp.zeros((16, D), F32), k.car_below[...].astype(F32)], axis=0)
    own = (own + lower).astype(BF)
    lower = jnp.concatenate([jnp.zeros((16, D), F32), k.car_corner[...].astype(F32)], axis=0)
    beside = (k.car_beside[...].astype(F32) + lower).astype(BF)

    def exchange(index, slabs, direction):
        out, back = k.slab_out.at[index], k.slab_in.at[index]
        out[...] = slabs
        back[0] = slabs[0]

        def step(i, carry):
            to_lon = lax.rem(lon + direction * i + 32, 32)
            pltpu.make_async_remote_copy(
                src_ref=out.at[i],
                dst_ref=back.at[i],
                send_sem=k.slab_send_sem.at[index],
                recv_sem=k.slab_recv_sem.at[index],
                device_id=(lat, to_lon),
                device_id_type=MESH,
            ).start()
            return carry

        def far_step(i, carry):
            to_lon = lax.rem(lon + direction * i + 32, 32)
            pltpu.make_async_remote_copy(
                src_ref=out.at[i],
                dst_ref=k.slab_far.at[index // 2, i],
                send_sem=k.far_send_sem.at[index // 2],
                recv_sem=k.far_recv_sem.at[index // 2],
                device_id=(far, to_lon),
                device_id_type=MESH,
            ).start()
            return carry

        lax.fori_loop(1, 32, step, 0)
        if direction == 1:
            lax.fori_loop(0, 32, far_step, 0)

    def group_gather(index, ref, sem):
        ref[0:64, :] = unpack_owner(k, exchanged(index))
        await_bytes(k.slab_far.at[index // 2], k.far_recv_sem.at[index // 2])
        ref[64:128, :] = unpack_owner(k, k.slab_far.at[index // 2])
        copy = send(ref.at[0:128], ref.at[128:256], sem, sibling, lon)
        copy.start()
        return copy

    def exchanged(index):
        await_bytes(k.slab_in.at[index, 1:32], k.slab_recv_sem.at[index])
        return k.slab_in.at[index]

    exchange(0, pack_home(k, jnp.concatenate([own, beside], axis=0)), 1)

    @pl.when(has_below)
    def _():
        cells_above.wait_recv()

    start(cells[2:4])
    cells_project(k, 1)
    loop_from(2, 4, cells_sensitivity, k)
    wait_received(cells[0:4])
    cells_project(k, 2)

    members = group_gather(0, k.car, 7)
    start(cells[4:8])
    cells_attend(k, 0)
    load_cw.wait()
    load_cwe.wait()
    members.wait_recv()
    exchange(1, pack_owner(k, group_forward(k)), -1)

    wait_received(cells[4:8])

    @pl.when(has_below)
    def _():
        cells_corner.wait_recv()

    cells_project(k, 3)
    loop_from(1, 4, cells_attend, k)

    k.cn[...] = unpack_home(k, exchanged(1))
    carriers_project(k)
    loop(4, windows_finish, k)
    exchange(2, pack_home(k, carriers_back(k)), 1)

    grads = []
    for first in range(0, 496, 64):
        last = min(first + 64, 496)
        grads.append(
            send(
                k.dx.at[512 + first : 512 + last],
                k.back.at[16 + first : 16 + last],
                28 + first // 64,
                lat,
                east,
            )
        )
    grads_corner = send(k.dx.at[1008:1024], k.back.at[0:16], 15, below, east)
    grads_below = send(k.dx.at[496:512], k.fall, 16, below, lon)
    loop(2, cells_back, k)
    cells_gradient(k, 2)
    start(grads[0:2])
    cells_back(k, 2)
    sensitivities = group_gather(2, k.cgrad, 8)
    start(grads[2:4])
    cells_back(k, 3)
    cells_gradient(k, 3)
    sensitivities.wait_recv()
    start(grads[4:6])
    exchange(3, pack_owner(k, group_back(k)), -1)
    start(grads[6:8])

    @pl.when(has_below)
    def _():
        grads_corner.start()

    cells_gradient(k, 1)
    cells_gradient(k, 0)

    @pl.when(has_below)
    def _():
        grads_below.start()

    loop(4, cells_result, k)
    store_out = pltpu.make_async_copy(k.xraw, k.out_hbm, k.load_sem.at[6])
    store_out.start()

    k.pool[...] = unpack_home(k, exchanged(3))
    pool_east = send(k.pool.at[32:64], k.pool_beside, 17, lat, east)
    pool_corner = send(k.pool.at[48:64], k.pool_corner, 18, below, east)
    pool_below = send(k.pool.at[16:32], k.pool_below, 19, below, lon)
    pool_east.start()

    @pl.when(has_below)
    def _():
        pool_corner.start()
        pool_below.start()

    wait_received(grads)
    pool_east.wait_recv()

    @pl.when(has_above)
    def _():
        grads_corner.wait_recv()
        grads_below.wait_recv()
        pool_corner.wait_recv()
        pool_below.wait_recv()

    stores = []
    for quad in range(4):
        field_rows(k, quad)
        rows = slice(quad * 256, quad * 256 + 256)
        store = pltpu.make_async_copy(k.graw.at[rows], k.field_hbm.at[rows], k.store_sem.at[quad])
        store.start()
        stores.append(store)

    for copy in [carriers_west, members, sensitivities, pool_east] + cells + grads:
        copy.wait_send()

    @pl.when(has_above)
    def _():
        for copy in (carriers_corner, carriers_above, cells_corner, cells_above):
            copy.wait_send()

    @pl.when(has_below)
    def _():
        for copy in (grads_corner, grads_below, pool_corner, pool_below):
            copy.wait_send()

    for index in range(4):
        await_bytes(k.slab_out.at[index, 1:32], k.slab_send_sem.at[index])
    for index in range(2):
        await_bytes(k.slab_out.at[0], k.far_send_sem.at[index])
    store_out.wait()
    for store in stores:
        store.wait()


def loop(count, step, k):
    loop_from(0, count, step, k)


def loop_from(first, last, step, k):
    lax.fori_loop(first, last, lambda i, _: (step(k, i), 0)[1], 0)


SCRATCH = {
    "heads": ((256, 256), BF),
    "carrier_heads": ((256, D), BF),
    "same": ((256, 256), BF),
    "spread": ((1024, 64), BF),
    "gather": ((64, 1024), BF),
    "split": ((256, 256), BF),
    "join": ((256, 256), BF),
    "unpack": ((384, HALF), BF),
    "routes": ((384, HALF), BF),
    "gain": ((1, D), F32),
    "cgain": ((1, D), F32),
    "temper": ((1, D), F32),
    "ctemper": ((1, D), F32),
    "xraw": ((1024, D), BF),
    "graw": ((1024, D), BF),
    "w": ((D, 3 * D), BF),
    "we": ((D, D), BF),
    "cw": ((D, 3 * D), BF),
    "cwe": ((D, D), BF),
    "x": ((1024, D), BF),
    "g": ((1024, D), BF),
    "away": ((HALF, D), BF),
    "rise": ((16, D), BF),
    "means": ((2, 32, D), F32),
    "car_send": ((64, D), BF),
    "car_beside": ((32, D), BF),
    "car_corner": ((16, D), BF),
    "car_below": ((16, D), BF),
    "slab_out": ((4, 32, 16, 128), BF),
    "slab_in": ((4, 32, 16, 128), BF),
    "slab_far": ((2, 32, 16, 128), BF),
    "car": ((256, D), BF),
    "cgrad": ((256, D), BF),
    "cn": ((64, D), BF),
    "pool": ((64, D), BF),
    "pool_beside": ((32, D), BF),
    "pool_corner": ((16, D), BF),
    "pool_below": ((16, D), BF),
    "back": ((HALF, D), BF),
    "fall": ((16, D), BF),
    "dx": ((1024, D), BF),
    "q": ((1024, D), BF),
    "k": ((1024, D), BF),
    "v": ((1024, D), BF),
    "do": ((1024, D), BF),
    "o": ((1024, D), BF),
    "t": ((1024, D), BF),
    "p": ((1024, D), BF),
    "sq": ((1024, D), F32),
    "sk": ((1024, D), F32),
    "op": ((1024, D), F32),
    "lp": ((1024, D), F32),
    "kcb": ((1024, D), BF),
    "vcb": ((1024, D), BF),
    "kc": ((64, D), BF),
    "vc": ((64, D), BF),
    "skc": ((64, D), F32),
    "dqkv": ((1024, 3 * D), BF),
    "cq": ((256, D), BF),
    "ck": ((256, D), BF),
    "cv": ((256, D), BF),
    "cp": ((12, 256, 256), BF),
    "csq": ((64, D), F32),
    "csk": ((64, D), F32),
    "cl": ((256, D), F32),
    "co": ((256, D), F32),
}
SEMAPHORES = {
    "load_sem": 7,
    "store_sem": 4,
    "send_sem": 36,
    "recv_sem": 36,
    "far_send_sem": 2,
    "far_recv_sem": 2,
    "slab_send_sem": 4,
    "slab_recv_sem": 4,
}
INPUTS = (
    "x_hbm",
    "g_hbm",
    "w_hbm",
    "we_hbm",
    "cw_hbm",
    "cwe_hbm",
    "gains",
    "cgains",
    "place",
    "tempers",
    "ctempers",
)


def per_device(x, g, gain, w, we, tempers, cgain, cw, cwe, ctempers, place):
    names = INPUTS + ("out_hbm", "field_hbm") + tuple(SCRATCH) + tuple(SEMAPHORES)

    def kernel(*refs):
        body(types.SimpleNamespace(**dict(zip(names, refs))))

    anywhere = pl.BlockSpec(memory_space=pl.ANY)
    vmem = pl.BlockSpec(memory_space=pltpu.VMEM)
    smem = pl.BlockSpec(memory_space=pltpu.SMEM)
    out, field = pl.pallas_call(
        kernel,
        out_shape=[jax.ShapeDtypeStruct((1024, D), BF)] * 2,
        in_specs=[anywhere] * 6 + [vmem] * 3 + [smem] * 2,
        out_specs=[anywhere] * 2,
        scratch_shapes=[pltpu.VMEM(shape, kind) for shape, kind in SCRATCH.values()]
        + [pltpu.SemaphoreType.DMA((count,)) for count in SEMAPHORES.values()],
        compiler_params=pltpu.CompilerParams(
            collective_id=0, has_side_effects=True, vmem_limit_bytes=62 * 1024 * 1024
        ),
        name="block",
    )(
        x.reshape(1024, D),
        g.reshape(1024, D),
        w,
        we,
        cw,
        cwe,
        gain,
        cgain,
        place.T,
        tempers,
        ctempers,
    )
    return out.reshape(128, 8, D), field.reshape(128, 8, D)


def solution(mesh):
    placed = (P("lat", "lon", None),) * 2 + (P(),) * 8 + (P("lat", "lon"),)
    return jax.shard_map(
        per_device,
        mesh=mesh,
        in_specs=placed,
        out_specs=(P("lat", "lon", None),) * 2,
        check_vma=False,
    )
```

```python
import types

import jax
import jax.numpy as jnp
from jax import lax
from jax.experimental import pallas as pl
from jax.experimental.pallas import tpu as pltpu
from jax.sharding import PartitionSpec as P

BF = jnp.bfloat16
F32 = jnp.float32
LOG2E = 1.4426950408889634
LN2 = 0.6931471805599453
D = 768
GROUPS = 3
WINDOWS = 16
CELLS = 64
HALF = 512
MESH = pl.DeviceIdType.MESH


def nn(a, b):
    return lax.dot_general(a, b, (((1,), (0,)), ((), ())), preferred_element_type=F32)


def nt(a, b):
    return lax.dot_general(a, b, (((1,), (1,)), ((), ())), preferred_element_type=F32)


def tn(a, b):
    return lax.dot_general(a, b, (((0,), (0,)), ((), ())), preferred_element_type=F32)


def iota(shape, axis):
    return lax.broadcasted_iota(jnp.int32, shape, axis)


def one_where(condition):
    return jnp.where(condition, 1.0, 0.0).astype(BF)


def lanes(n):
    return slice(n * 256, (n + 1) * 256)


def fill_constants(k):
    k.heads[...] = one_where(iota((256, 256), 0) // 64 == iota((256, 256), 1) // 64)
    k.carrier_heads[...] = one_where(iota((256, D), 0) % 16 == iota((256, D), 1) // 64)
    k.same[...] = one_where(iota((256, 256), 0) % 128 // 32 == iota((256, 256), 1) % 128 // 32)
    k.spread[...] = one_where(iota((1024, 64), 0) // 16 == iota((1024, 64), 1))
    k.gather[...] = one_where(iota((64, 1024), 1) // 16 == iota((64, 1024), 0))
    split, cell = iota((256, 256), 0), iota((256, 256), 1)
    k.split[...] = one_where(cell == split % 128 // 4 * 8 + split // 128 * 4 + split % 4)
    cell, split = iota((256, 256), 0), iota((256, 256), 1)
    k.join[...] = one_where(cell == split % 128 // 4 * 8 + split // 128 * 4 + split % 4)
    row, slab = iota((384, HALF), 0), iota((384, HALF), 1)
    member = row % 64
    k.unpack[...] = one_where(slab == member // 2 * 16 + row // 64 * 2 + member % 2)
    k.gain[...] = k.gains[...].reshape(1, D)
    k.cgain[...] = k.cgains[...].reshape(1, D)
    lane = iota((1, D), 1) // 64
    for tempers, wide in ((k.tempers, k.temper), (k.ctempers, k.ctemper)):
        total = jnp.zeros((1, D), F32)
        for h in range(12):
            total = jnp.where(lane == h, tempers[h], total)
        wide[...] = total


def fill_routes(k, lon):
    slab = iota((32, HALF), 1)
    eye = jnp.where(iota((32, 32), 0) == iota((32, 32), 1), 1.0, 0.0)
    for b in range(2):
        place = k.place[b : b + 1, :]
        place = jnp.sum(jnp.where(eye > 0, place, 0), axis=1, keepdims=True)
        partner = (place // 64 - lon + 32) % 32
        slot = partner * 16 + place % 2
        for c in range(6):
            rows = slice(b * 192 + c * 32, b * 192 + c * 32 + 32)
            k.routes[rows, :] = one_where(slab == slot + 2 * c)


def pack(matrix, parts):
    return tn(matrix, jnp.concatenate(parts, axis=0)).astype(BF).reshape(32, 16, 128)


def lane_parts(rows):
    return [rows[:, c * 128 : (c + 1) * 128] for c in range(6)]


def pack_home(k, rows):
    return pack(k.routes[...], lane_parts(rows[:32]) + lane_parts(rows[32:]))


def unpack_home(k, slabs):
    parts = nn(k.routes[...], slabs[...].reshape(HALF, 128)).astype(BF)
    sides = []
    for b in range(2):
        pieces = [parts[b * 192 + c * 32 : b * 192 + c * 32 + 32] for c in range(6)]
        sides.append(jnp.concatenate(pieces, axis=1))
    return jnp.concatenate(sides, axis=0)


def pack_owner(k, rows):
    return pack(k.unpack[...], lane_parts(rows))


def unpack_owner(k, slabs):
    parts = nn(k.unpack[...], slabs[...].reshape(HALF, 128)).astype(BF)
    return jnp.concatenate([parts[c * 64 : c * 64 + 64] for c in range(6)], axis=1)


def rms_inverse(x):
    return lax.rsqrt(jnp.mean(x * x, axis=-1, keepdims=True) + 1e-05)


def rms_back(x, gain, grad):
    inverse = rms_inverse(x)
    scaled = grad * gain
    along = jnp.mean(x * scaled, axis=-1, keepdims=True)
    return inverse * (scaled - x * (inverse * inverse * along))


def unit_scale(u, heads):
    return lax.rsqrt(nn((u * u).astype(BF), heads) + 64e-06)


def key_back(scale, key, grad, heads):
    along = nn((key * grad).astype(BF), heads)
    return scale * (grad - key * along)


def query_back(scale, query, temper, raw, heads):
    along = nn((query * raw).astype(BF), heads)
    return scale * (temper * raw - query * along * (LN2 * LN2 / temper))


def block_diagonal(rows, heads):
    return jnp.concatenate([rows] * 4, axis=0) * heads


def chunk_rows(chunk):
    return pl.ds(pl.multiple_of(chunk * 256, 256), 256)


def both(ref, quad, columns=slice(None)):
    first = pl.multiple_of(quad * 128, 128)
    return jnp.concatenate(
        [ref[pl.ds(first, 128), columns], ref[pl.ds(first + HALF, 128), columns]], axis=0
    )


def put_both(ref, quad, value, columns=slice(None)):
    first = pl.multiple_of(quad * 128, 128)
    ref[pl.ds(first, 128), columns] = value[:128]
    ref[pl.ds(first + HALF, 128), columns] = value[128:]


def window(rows, w):
    return jnp.concatenate([rows[w * 32 : w * 32 + 32], rows[w * 32 + 128 : w * 32 + 160]], axis=0)


def from_parts(parts):
    return jnp.concatenate([p[:32] for p in parts] + [p[32:] for p in parts], axis=0)


def cells_project(k, chunk):
    rows = chunk_rows(chunk)
    x = k.x[rows, :].astype(F32)
    hidden = (x * rms_inverse(x) * k.gain[...]).astype(BF)
    heads = k.heads[...]
    for n in range(GROUPS):
        u = nn(hidden, k.w[:, lanes(n)])
        scale = unit_scale(u, heads)
        k.sq[rows, lanes(n)] = scale
        k.q[rows, lanes(n)] = (u * scale * (k.temper[:, lanes(n)] * LOG2E)).astype(BF)
    for n in range(GROUPS):
        u = nn(hidden, k.w[:, lanes(3 + n)])
        scale = unit_scale(u, heads)
        k.sk[rows, lanes(n)] = scale
        k.k[rows, lanes(n)] = (u * scale).astype(BF)
    for n in range(GROUPS):
        k.v[rows, lanes(n)] = nn(hidden, k.w[:, lanes(6 + n)]).astype(BF)


def cells_sensitivity(k, quad):
    halves = nn(k.split[...], k.graw[chunk_rows(quad), :]).astype(BF)
    put_both(k.g, quad, halves)
    put_both(k.do, quad, nt(halves, k.we[...]).astype(BF))


def cells_attend(k, quad):
    heads = k.heads[...]
    for n in range(GROUPS):
        query, key, value = (both(ref, quad, lanes(n)) for ref in (k.q, k.k, k.v))
        weights, sums = [], []
        for w in range(4):
            keys = block_diagonal(window(key, w), heads)
            weights.append(jnp.exp2(nt(window(query, w), keys)).astype(BF))
        for w in range(4):
            sums.append(nn(weights[w], block_diagonal(window(value, w), heads)))
        weights = from_parts(weights)
        put_both(k.p, quad, weights, lanes(n))
        put_both(k.op, quad, from_parts(sums), lanes(n))
        put_both(k.lp, quad, nn(weights, heads), lanes(n))


def carriers_project(k):
    c = k.cn[...].astype(F32)
    hidden = (c * rms_inverse(c) * k.gain[...]).astype(BF)
    heads = k.heads[...]
    for n in range(GROUPS):
        u = nn(hidden, k.w[:, lanes(3 + n)])
        scale = unit_scale(u, heads)
        k.skc[:, lanes(n)] = scale
        key = (u * scale).astype(BF)
        k.kc[:, lanes(n)] = key
        value = nn(hidden, k.w[:, lanes(6 + n)]).astype(BF)
        k.vc[:, lanes(n)] = value
    for chunk in range(4):
        rows = slice(chunk * 256, (chunk + 1) * 256)
        mask = k.carrier_heads[...]
        k.kcb[rows, :] = nn(k.spread[rows, :], k.kc[...]).astype(BF) * mask
        k.vcb[rows, :] = nn(k.spread[rows, :], k.vc[...]).astype(BF) * mask


def windows_finish(k, quad):
    keys, values, query = both(k.kcb, quad), both(k.vcb, quad), both(k.q, quad)
    mask = k.carrier_heads[...]
    weights = jnp.exp2(nt(query, keys)).astype(BF) * k.same[...]
    along = jnp.zeros((256, 256), F32)
    for n in range(GROUPS):
        inverse = 1.0 / (both(k.lp, quad, lanes(n)) + nn(weights, mask[:, lanes(n)]))
        attended = both(k.op, quad, lanes(n)) + nn(weights, values[:, lanes(n)])
        attended = attended * inverse
        put_both(k.o, quad, attended.astype(BF), lanes(n))
        sensitivity = both(k.do, quad, lanes(n)).astype(F32) * inverse
        product = (sensitivity * attended).astype(BF)
        put_both(k.t, quad, product, lanes(n))
        sensitivity = sensitivity.astype(BF)
        put_both(k.do, quad, sensitivity, lanes(n))
        along += nt(sensitivity, values[:, lanes(n)]) - nt(product, mask[:, lanes(n)])
    grads = (weights.astype(F32) * along).astype(BF)
    put_both(k.cg, quad, grads)
    put_both(k.dqkv, quad, (tn(grads, query) * LN2).astype(BF) * mask, slice(0, D))
    put_both(k.dqkv, quad, tn(weights, both(k.do, quad)).astype(BF) * mask, slice(D, 2 * D))


def carriers_back(k):
    heads = k.heads[...]
    select = k.gather[...]
    grad = jnp.zeros((64, D), F32)
    for n in range(GROUPS):
        dk = nn(select, k.dqkv[:, lanes(n)])
        du = key_back(k.skc[:, lanes(n)], k.kc[:, lanes(n)].astype(F32), dk, heads)
        grad += nt(du.astype(BF), k.w[:, lanes(3 + n)])
        dv = nn(select, k.dqkv[:, lanes(3 + n)]).astype(BF)
        grad += nt(dv, k.w[:, lanes(6 + n)])
    grad = grad.astype(BF).astype(F32)
    back = rms_back(k.cn[...].astype(F32), k.gain[...], grad)
    return (back + k.gsum[...]).astype(BF)


def cells_result(k, quad):
    total = both(k.x, quad).astype(F32) + nn(both(k.o, quad), k.we[...])
    total = (total + nn(both(k.spread, quad), k.cn[...])).astype(BF)
    k.xraw[chunk_rows(quad), :] = nn(k.join[...], total).astype(BF)


def cells_back(k, quad):
    heads = k.heads[...]
    low = iota((64, 128), 1) < 64
    for n in range(GROUPS):
        query, key, value = (both(ref, quad, lanes(n)) for ref in (k.q, k.k, k.v))
        weights, sensitivity = (both(ref, quad, lanes(n)) for ref in (k.p, k.do))
        offset = nn(both(k.t, quad, lanes(n)), heads)
        along = []
        for w in range(4):
            values = block_diagonal(window(value, w), heads)
            along.append(nt(window(sensitivity, w), values))
        grads = (weights.astype(F32) * (from_parts(along) - offset)).astype(BF)
        raw, dk, dv = [], [], []
        for w in range(4):
            mine = window(grads, w)
            raw.append(nn(mine, block_diagonal(window(key, w), heads)))
            key_parts, value_parts = [], []
            for pair in range(2):
                part = slice(pair * 128, (pair + 1) * 128)
                pairs = tn(mine[:, part], window(query, w)[:, part])
                key_parts.append(jnp.where(low, pairs[:64], pairs[64:]))
                pairs = tn(window(weights, w)[:, part], window(sensitivity, w)[:, part])
                value_parts.append(jnp.where(low, pairs[:64], pairs[64:]))
            dk.append(jnp.concatenate(key_parts, axis=1))
            dv.append(jnp.concatenate(value_parts, axis=1))
        put_both(k.dqkv, quad, from_parts(dv).astype(BF), lanes(6 + n))
        raw = nn(both(k.cg, quad), both(k.kcb, quad, lanes(n))) + from_parts(raw)
        scale = both(k.sq, quad, lanes(n))
        du = query_back(scale, query.astype(F32), k.temper[:, lanes(n)], raw, heads)
        put_both(k.dqkv, quad, du.astype(BF), lanes(n))
        dk = (from_parts(dk) * LN2).astype(BF).astype(F32)
        du = key_back(both(k.sk, quad, lanes(n)), key.astype(F32), dk, heads)
        put_both(k.dqkv, quad, du.astype(BF), lanes(3 + n))


def cells_gradient(k, first, count):
    rows = slice(first, first + count)
    grad = nt(k.dqkv[rows, :], k.w[...]).astype(BF).astype(F32)
    back = rms_back(k.x[rows, :].astype(F32), k.gain[...], grad)
    k.dx[rows, :] = (back + k.g[rows, :].astype(F32)).astype(BF)


def pick(full):
    head = iota((64, 256), 1) // 64
    picked = full[:64]
    for h in range(1, 4):
        picked = jnp.where(head == h, full[h * 64 : h * 64 + 64], picked)
    return picked


def group_query(k, rows, n):
    u = nn(k.chid[rows, :], k.cw[:, lanes(n)])
    scale = unit_scale(u, k.heads[...])
    query = (u * scale * (k.ctemper[:, lanes(n)] * LOG2E)).astype(BF)
    k.cq[rows, lanes(n)] = query
    return query, scale


def group_forward(k):
    c = k.car[...].astype(F32)
    hidden = (c * rms_inverse(c) * k.cgain[...]).astype(BF)
    k.chid[...] = hidden
    heads = k.heads[...]
    ones = jnp.ones((256, 256), BF)
    for n in range(GROUPS):
        query, scale = group_query(k, slice(0, 64), n)
        k.csq[:, lanes(n)] = scale
        u = nn(hidden, k.cw[:, lanes(3 + n)])
        scale = unit_scale(u, heads)
        k.csk[:, lanes(n)] = scale[:64]
        key = (u * scale).astype(BF)
        k.ck[:, lanes(n)] = key
        value = nn(hidden, k.cw[:, lanes(6 + n)]).astype(BF)
        k.cv[:, lanes(n)] = value
        weights = jnp.exp2(nt(block_diagonal(query, heads), key)).astype(BF)
        k.crows[n] = weights
        inverse = 1.0 / nn(weights, ones)
        k.cl[:64, lanes(n)] = pick(inverse)
        k.co[:64, lanes(n)] = pick(nn(weights, value) * inverse)
    mixed = nn(k.co[:64, :].astype(BF), k.cwe[...])
    return (k.car[:64, :].astype(F32) + mixed).astype(BF)


def group_others(k):
    heads = k.heads[...]
    rows = slice(64, 256)
    for n in range(GROUPS):
        query, _ = group_query(k, rows, n)
        key, value = k.ck[:, lanes(n)], k.cv[:, lanes(n)]
        total = jnp.zeros((192, 256), F32)
        denominator = jnp.zeros((192, 256), F32)
        for h in range(4):
            mine = one_where(iota((256, 256), 1) // 64 == h)
            weights = jnp.exp2(nt(query, key * mine)).astype(BF)
            total += nn(weights, value * mine)
            denominator += nn(weights, mine)
        inverse = 1.0 / denominator
        k.cl[rows, lanes(n)] = inverse
        k.co[rows, lanes(n)] = total * inverse
        own = block_diagonal(key[:64], heads)
        k.ccolumns[n] = jnp.exp2(nt(own, k.cq[:, lanes(n)])).astype(BF)


def group_back(k):
    heads = k.heads[...]
    ones = jnp.ones((256, 256), BF)
    grad = jnp.zeros((64, D), F32)
    for n in range(GROUPS):
        sensitivity = nt(k.cgrad[...], k.cwe[lanes(n), :]).astype(BF).astype(F32)
        sensitivity = sensitivity * k.cl[:, lanes(n)]
        product = (sensitivity * k.co[:, lanes(n)]).astype(BF)
        sensitivity = sensitivity.astype(BF)
        query, key, value = k.cq[:, lanes(n)], k.ck[:, lanes(n)], k.cv[:, lanes(n)]
        along = nt(block_diagonal(sensitivity[:64], heads), value)
        along -= nn(block_diagonal(product[:64], heads), ones)
        grads = (k.crows[n].astype(F32) * along).astype(BF)
        raw = pick(nn(grads, key))
        du = query_back(
            k.csq[:, lanes(n)], query[:64].astype(F32), k.ctemper[:, lanes(n)], raw, heads
        )
        grad += nt(du.astype(BF), k.cw[:, lanes(n)])
        weights = k.ccolumns[n]
        along = nt(block_diagonal(value[:64], heads), sensitivity) - nt(heads, product)
        grads = (weights.astype(F32) * along).astype(BF)
        dk = (pick(nn(grads, query)) * LN2).astype(BF).astype(F32)
        du = key_back(k.csk[:, lanes(n)], key[:64].astype(F32), dk, heads)
        grad += nt(du.astype(BF), k.cw[:, lanes(3 + n)])
        dv = pick(nn(weights, sensitivity)).astype(BF)
        grad += nt(dv, k.cw[:, lanes(6 + n)])
    grad = grad.astype(BF).astype(F32)
    back = rms_back(k.car[:64, :].astype(F32), k.cgain[...], grad)
    return (back + k.cgrad[:64, :].astype(F32)).astype(BF)


def cells_split(k, quad):
    halves = nn(k.split[...], k.xraw[chunk_rows(quad), :]).astype(BF)
    first = quad * 128
    k.away[first : first + 128, :] = halves[:128]
    if quad == 0:
        k.rise[...] = halves[128:144]
        k.x[0:112, :] = halves[144:]
    else:
        k.x[first - 16 : first + 112, :] = halves[128:]
    means = nn(one_where(iota((16, 256), 1) // 16 == iota((16, 256), 0)), halves) * 0.0625
    k.means[0, quad * 8 : quad * 8 + 8, :] = means[:8]
    k.means[1, quad * 8 : quad * 8 + 8, :] = means[8:]


def field_rows(k, quad):
    first = quad * 128
    rows = slice(first, first + 128)
    mine = iota((128, 32), 0) // 16 + quad * 8 - 1 == iota((128, 32), 1)
    mine = one_where(mine)
    edge = one_where((iota((128, 16), 0) // 16 + quad * 8 == 0) & (iota((128, 16), 1) == 15))
    left = k.back[rows, :].astype(F32)
    left += (nn(mine, k.pool_beside[...]) + nn(edge, k.pool_corner[...])) * 0.0625
    if quad == 0:
        right = jnp.concatenate([k.fall[...], k.dx[0:112, :]], axis=0).astype(F32)
    else:
        right = k.dx[first - 16 : first + 112, :].astype(F32)
    right += (nn(mine, k.pool[0:32, :]) + nn(edge, k.pool_below[...])) * 0.0625
    both = jnp.concatenate([left.astype(BF), right.astype(BF)], axis=0)
    k.graw[quad * 256 : quad * 256 + 256, :] = nn(k.join[...], both).astype(BF)


def body(k):
    lat, lon = lax.axis_index("lat"), lax.axis_index("lon")
    has_above, has_below = lat > 0, lat < 3
    above, below = lax.rem(lat + 3, 4), lax.rem(lat + 1, 4)
    west, east = lax.rem(lon + 31, 32), lax.rem(lon + 1, 32)

    loads = []
    for i, (source, target) in enumerate(
        (
            (k.x_hbm, k.xraw),
            (k.w_hbm, k.w),
            (k.g_hbm, k.graw),
            (k.we_hbm, k.we),
            (k.cw_hbm, k.cw),
            (k.cwe_hbm, k.cwe),
        )
    ):
        load = pltpu.make_async_copy(source, target, k.load_sem.at[i])
        load.start()
        loads.append(load)
    load_x, load_w, load_g, load_we, load_cw, load_cwe = loads

    @pl.when(jnp.logical_not(has_below))
    def _():
        k.x[496:512, :] = jnp.zeros((16, D), BF)
        k.x[1008:1024, :] = jnp.zeros((16, D), BF)
        k.car_below[...] = jnp.zeros((16, D), BF)
        k.car_corner[...] = jnp.zeros((16, D), BF)

    @pl.when(jnp.logical_not(has_above))
    def _():
        k.back[0:16, :] = jnp.zeros((16, D), BF)
        k.fall[...] = jnp.zeros((16, D), BF)
        k.pool_below[...] = jnp.zeros((16, D), BF)
        k.pool_corner[...] = jnp.zeros((16, D), BF)

    barrier = pltpu.get_barrier_semaphore()

    def greet(to_lat, to_lon):
        pl.semaphore_signal(barrier, inc=1, device_id=(to_lat, to_lon), device_id_type=MESH)

    far, sibling = lax.rem(lat + 2, 4), lat // 2 * 2 + (1 - lat % 2)

    def greet_lon(i, carry):
        greet(lat, lax.rem(lon + i, 32))
        greet(far, lax.rem(lon + i, 32))
        return carry

    lax.fori_loop(1, 32, greet_lon, 0)
    for s in range(1, 4):
        greet(lax.rem(lat + s, 4), lon)
    greet(above, west)
    greet(below, east)

    def send(source, target, sem, to_lat, to_lon):
        return pltpu.make_async_remote_copy(
            src_ref=source,
            dst_ref=target,
            send_sem=k.send_sem.at[sem],
            recv_sem=k.recv_sem.at[sem],
            device_id=(to_lat, to_lon),
            device_id_type=MESH,
        )

    def start(copies):
        for copy in copies:
            copy.start()

    def wait_received(copies):
        for copy in copies:
            copy.wait_recv()

    def await_bytes(ref, sem):
        pltpu.make_async_copy(ref, ref, sem).wait()

    fill_constants(k)
    fill_routes(k, lon)

    load_x.wait()
    for quad in range(4):
        cells_split(k, quad)
    up = one_where(iota((32, 32), 1) == iota((32, 32), 0) + 1)
    top = one_where((iota((16, 32), 0) == 15) & (iota((16, 32), 1) == 0))
    left, right = k.means[0].astype(BF), k.means[1].astype(BF)
    k.car_send[0:32, :] = nn(up, left).astype(BF)
    k.car_send[32:48, :] = nn(top, left).astype(BF)
    k.car_send[48:64, :] = nn(top, right).astype(BF)
    own = nn(up, right)
    pl.semaphore_wait(barrier, 67)
    carriers_west = send(k.car_send.at[0:32], k.car_beside, 0, lat, west)
    carriers_corner = send(k.car_send.at[32:48], k.car_corner, 1, above, west)
    carriers_above = send(k.car_send.at[48:64], k.car_below, 2, above, lon)
    cells = []
    for first in range(0, 496, 64):
        last = min(first + 64, 496)
        cells.append(
            send(
                k.away.at[16 + first : 16 + last],
                k.x.at[512 + first : 512 + last],
                20 + first // 64,
                lat,
                west,
            )
        )
    cells_corner = send(k.away.at[0:16], k.x.at[1008:1024], 5, above, west)
    cells_above = send(k.rise, k.x.at[496:512], 6, above, lon)
    carriers_west.start()

    @pl.when(has_above)
    def _():
        carriers_corner.start()
        carriers_above.start()
        cells_above.start()

    start(cells[0:2])
    load_w.wait()
    cells_project(k, 0)
    start(cells[2:3])
    load_g.wait()
    load_we.wait()
    loop(2, cells_sensitivity, k)

    carriers_west.wait_recv()

    @pl.when(has_below)
    def _():
        carriers_corner.wait_recv()
        carriers_above.wait_recv()

    lower = jnp.concatenate([jnp.zeros((16, D), F32), k.car_below[...].astype(F32)], axis=0)
    own = (own + lower).astype(BF)
    lower = jnp.concatenate([jnp.zeros((16, D), F32), k.car_corner[...].astype(F32)], axis=0)
    beside = (k.car_beside[...].astype(F32) + lower).astype(BF)

    def exchange(index, slabs, direction):
        out, back = k.slab_out.at[index], k.slab_in.at[index]
        out[...] = slabs
        back[0] = slabs[0]

        def step(i, carry):
            to_lon = lax.rem(lon + direction * i + 32, 32)
            pltpu.make_async_remote_copy(
                src_ref=out.at[i],
                dst_ref=back.at[i],
                send_sem=k.slab_send_sem.at[index],
                recv_sem=k.slab_recv_sem.at[index],
                device_id=(lat, to_lon),
                device_id_type=MESH,
            ).start()
            return carry

        def far_step(i, carry):
            to_lon = lax.rem(lon + direction * i + 32, 32)
            pltpu.make_async_remote_copy(
                src_ref=out.at[i],
                dst_ref=k.slab_far.at[index // 2, i],
                send_sem=k.far_send_sem.at[index // 2],
                recv_sem=k.far_recv_sem.at[index // 2],
                device_id=(far, to_lon),
                device_id_type=MESH,
            ).start()
            return carry

        lax.fori_loop(1, 32, step, 0)
        if direction == 1:
            lax.fori_loop(0, 32, far_step, 0)

    def group_gather(index, ref, sem):
        ref[0:64, :] = unpack_owner(k, exchanged(index))
        await_bytes(k.slab_far.at[index // 2], k.far_recv_sem.at[index // 2])
        ref[64:128, :] = unpack_owner(k, k.slab_far.at[index // 2])
        copy = send(ref.at[0:128], ref.at[128:256], sem, sibling, lon)
        copy.start()
        return copy

    def exchanged(index):
        await_bytes(k.slab_in.at[index, 1:32], k.slab_recv_sem.at[index])
        return k.slab_in.at[index]

    exchange(0, pack_home(k, jnp.concatenate([own, beside], axis=0)), 1)

    @pl.when(has_below)
    def _():
        cells_above.wait_recv()

    start(cells[3:4])
    cells_project(k, 1)
    start(cells[4:6])
    loop_from(2, 4, cells_sensitivity, k)
    k.gsum[...] = nn(k.gather[...], k.g[...])
    wait_received(cells[0:4])
    cells_project(k, 2)

    members = group_gather(0, k.car, 7)
    start(cells[6:7])
    cells_attend(k, 0)
    load_cw.wait()
    load_cwe.wait()
    members.wait_recv()
    exchange(1, pack_owner(k, group_forward(k)), -1)

    start(cells[7:8])

    @pl.when(has_above)
    def _():
        cells_corner.start()

    cells_attend(k, 1)
    wait_received(cells[4:8])

    @pl.when(has_below)
    def _():
        cells_corner.wait_recv()

    cells_project(k, 3)
    loop_from(2, 4, cells_attend, k)

    k.cn[...] = unpack_home(k, exchanged(1))
    carriers_project(k)
    loop(4, windows_finish, k)
    exchange(2, pack_home(k, carriers_back(k)), 1)

    grads = []
    for first in range(0, 496, 64):
        last = min(first + 64, 496)
        grads.append(
            send(
                k.dx.at[512 + first : 512 + last],
                k.back.at[16 + first : 16 + last],
                28 + first // 64,
                lat,
                east,
            )
        )
    grads_corner = send(k.dx.at[1008:1024], k.back.at[0:16], 15, below, east)
    grads_below = send(k.dx.at[496:512], k.fall, 16, below, lon)
    cells_back(k, 0)
    cells_gradient(k, 512, 128)
    start(grads[0:1])
    cells_back(k, 1)
    cells_gradient(k, 640, 128)
    start(grads[1:2])
    group_others(k)
    sensitivities = group_gather(2, k.cgrad, 8)
    start(grads[2:3])
    cells_back(k, 2)
    cells_gradient(k, 768, 128)
    start(grads[3:5])
    sensitivities.wait_recv()
    exchange(3, pack_owner(k, group_back(k)), -1)
    start(grads[5:6])
    cells_back(k, 3)
    cells_gradient(k, 896, 128)
    start(grads[6:7])
    cells_gradient(k, 256, 256)
    start(grads[7:8])

    @pl.when(has_below)
    def _():
        grads_corner.start()
        grads_below.start()

    cells_gradient(k, 0, 256)
    k.pool[...] = unpack_home(k, exchanged(3))
    pool_east = send(k.pool.at[32:64], k.pool_beside, 17, lat, east)
    pool_corner = send(k.pool.at[48:64], k.pool_corner, 18, below, east)
    pool_below = send(k.pool.at[16:32], k.pool_below, 19, below, lon)
    pool_east.start()

    @pl.when(has_below)
    def _():
        pool_corner.start()
        pool_below.start()

    loop(4, cells_result, k)
    store_out = pltpu.make_async_copy(k.xraw, k.out_hbm, k.load_sem.at[6])
    store_out.start()

    wait_received(grads)
    pool_east.wait_recv()

    @pl.when(has_above)
    def _():
        grads_corner.wait_recv()
        grads_below.wait_recv()
        pool_corner.wait_recv()
        pool_below.wait_recv()

    stores = []
    for quad in range(4):
        field_rows(k, quad)
        rows = slice(quad * 256, quad * 256 + 256)
        store = pltpu.make_async_copy(k.graw.at[rows], k.field_hbm.at[rows], k.store_sem.at[quad])
        store.start()
        stores.append(store)

    for copy in [carriers_west, members, sensitivities, pool_east] + cells + grads:
        copy.wait_send()

    @pl.when(has_above)
    def _():
        for copy in (carriers_corner, carriers_above, cells_corner, cells_above):
            copy.wait_send()

    @pl.when(has_below)
    def _():
        for copy in (grads_corner, grads_below, pool_corner, pool_below):
            copy.wait_send()

    for index in range(4):
        await_bytes(k.slab_out.at[index, 1:32], k.slab_send_sem.at[index])
    for index in range(2):
        await_bytes(k.slab_out.at[0], k.far_send_sem.at[index])
    store_out.wait()
    for store in stores:
        store.wait()


def loop(count, step, k):
    loop_from(0, count, step, k)


def loop_from(first, last, step, k):
    lax.fori_loop(first, last, lambda i, _: (step(k, i), 0)[1], 0)


SCRATCH = {
    "heads": ((256, 256), BF),
    "carrier_heads": ((256, D), BF),
    "same": ((256, 256), BF),
    "spread": ((1024, 64), BF),
    "gather": ((64, 1024), BF),
    "split": ((256, 256), BF),
    "join": ((256, 256), BF),
    "unpack": ((384, HALF), BF),
    "routes": ((384, HALF), BF),
    "gain": ((1, D), F32),
    "cgain": ((1, D), F32),
    "temper": ((1, D), F32),
    "ctemper": ((1, D), F32),
    "xraw": ((1024, D), BF),
    "graw": ((1024, D), BF),
    "w": ((D, 3 * D), BF),
    "we": ((D, D), BF),
    "cw": ((D, 3 * D), BF),
    "cwe": ((D, D), BF),
    "x": ((1024, D), BF),
    "g": ((1024, D), BF),
    "away": ((HALF, D), BF),
    "rise": ((16, D), BF),
    "means": ((2, 32, D), F32),
    "car_send": ((64, D), BF),
    "car_beside": ((32, D), BF),
    "car_corner": ((16, D), BF),
    "car_below": ((16, D), BF),
    "slab_out": ((4, 32, 16, 128), BF),
    "slab_in": ((4, 32, 16, 128), BF),
    "slab_far": ((2, 32, 16, 128), BF),
    "car": ((256, D), BF),
    "cgrad": ((256, D), BF),
    "cn": ((64, D), BF),
    "pool": ((64, D), BF),
    "pool_beside": ((32, D), BF),
    "pool_corner": ((16, D), BF),
    "pool_below": ((16, D), BF),
    "back": ((HALF, D), BF),
    "fall": ((16, D), BF),
    "dx": ((1024, D), BF),
    "q": ((1024, D), BF),
    "k": ((1024, D), BF),
    "v": ((1024, D), BF),
    "do": ((1024, D), BF),
    "o": ((1024, D), BF),
    "t": ((1024, D), BF),
    "p": ((1024, D), BF),
    "sq": ((1024, D), F32),
    "sk": ((1024, D), F32),
    "op": ((1024, D), F32),
    "lp": ((1024, D), F32),
    "kcb": ((1024, D), BF),
    "vcb": ((1024, D), BF),
    "kc": ((64, D), BF),
    "vc": ((64, D), BF),
    "skc": ((64, D), F32),
    "dqkv": ((1024, 3 * D), BF),
    "cq": ((256, D), BF),
    "ck": ((256, D), BF),
    "cv": ((256, D), BF),
    "chid": ((256, D), BF),
    "crows": ((3, 256, 256), BF),
    "ccolumns": ((3, 256, 256), BF),
    "cg": ((1024, 256), BF),
    "gsum": ((64, D), F32),
    "csq": ((64, D), F32),
    "csk": ((64, D), F32),
    "cl": ((256, D), F32),
    "co": ((256, D), F32),
}
SEMAPHORES = {
    "load_sem": 7,
    "store_sem": 4,
    "send_sem": 36,
    "recv_sem": 36,
    "far_send_sem": 2,
    "far_recv_sem": 2,
    "slab_send_sem": 4,
    "slab_recv_sem": 4,
}
INPUTS = (
    "x_hbm",
    "g_hbm",
    "w_hbm",
    "we_hbm",
    "cw_hbm",
    "cwe_hbm",
    "gains",
    "cgains",
    "place",
    "tempers",
    "ctempers",
)


def per_device(x, g, gain, w, we, tempers, cgain, cw, cwe, ctempers, place):
    names = INPUTS + ("out_hbm", "field_hbm") + tuple(SCRATCH) + tuple(SEMAPHORES)

    def kernel(*refs):
        body(types.SimpleNamespace(**dict(zip(names, refs))))

    anywhere = pl.BlockSpec(memory_space=pl.ANY)
    vmem = pl.BlockSpec(memory_space=pltpu.VMEM)
    smem = pl.BlockSpec(memory_space=pltpu.SMEM)
    out, field = pl.pallas_call(
        kernel,
        out_shape=[jax.ShapeDtypeStruct((1024, D), BF)] * 2,
        in_specs=[anywhere] * 6 + [vmem] * 3 + [smem] * 2,
        out_specs=[anywhere] * 2,
        scratch_shapes=[pltpu.VMEM(shape, kind) for shape, kind in SCRATCH.values()]
        + [pltpu.SemaphoreType.DMA((count,)) for count in SEMAPHORES.values()],
        compiler_params=pltpu.CompilerParams(
            collective_id=0, has_side_effects=True, vmem_limit_bytes=62 * 1024 * 1024
        ),
        name="block",
    )(
        x.reshape(1024, D),
        g.reshape(1024, D),
        w,
        we,
        cw,
        cwe,
        gain,
        cgain,
        place.T,
        tempers,
        ctempers,
    )
    return out.reshape(128, 8, D), field.reshape(128, 8, D)


def solution(mesh):
    placed = (P("lat", "lon", None),) * 2 + (P(),) * 8 + (P("lat", "lon"),)
    return jax.shard_map(
        per_device,
        mesh=mesh,
        in_specs=placed,
        out_specs=(P("lat", "lon", None),) * 2,
        check_vma=False,
    )
```

```python
import types

import jax
import jax.numpy as jnp
from jax import lax
from jax.experimental import pallas as pl
from jax.experimental.pallas import tpu as pltpu
from jax.sharding import PartitionSpec as P

BF = jnp.bfloat16
F32 = jnp.float32
LOG2E = 1.4426950408889634
LN2 = 0.6931471805599453
D = 768
GROUPS = 3
WINDOWS = 16
CELLS = 64
HALF = 512
MESH = pl.DeviceIdType.MESH


def nn(a, b):
    return lax.dot_general(a, b, (((1,), (0,)), ((), ())), preferred_element_type=F32)


def nt(a, b):
    return lax.dot_general(a, b, (((1,), (1,)), ((), ())), preferred_element_type=F32)


def tn(a, b):
    return lax.dot_general(a, b, (((0,), (0,)), ((), ())), preferred_element_type=F32)


def iota(shape, axis):
    return lax.broadcasted_iota(jnp.int32, shape, axis)


def one_where(condition):
    return jnp.where(condition, 1.0, 0.0).astype(BF)


def lanes(n):
    return slice(n * 256, (n + 1) * 256)


def fill_constants(k):
    k.heads[...] = one_where(iota((256, 256), 0) // 64 == iota((256, 256), 1) // 64)
    k.carrier_heads[...] = one_where(iota((256, D), 0) % 16 == iota((256, D), 1) // 64)
    k.same[...] = one_where(iota((256, 256), 0) % 128 // 32 == iota((256, 256), 1) % 128 // 32)
    k.spread[...] = one_where(iota((1024, 64), 0) // 16 == iota((1024, 64), 1))
    k.gather[...] = one_where(iota((64, 1024), 1) // 16 == iota((64, 1024), 0))
    split, cell = iota((256, 256), 0), iota((256, 256), 1)
    k.split[...] = one_where(cell == split % 128 // 4 * 8 + split // 128 * 4 + split % 4)
    row, slab = iota((384, HALF), 0), iota((384, HALF), 1)
    member = row % 64
    k.unpack[...] = one_where(slab == member // 2 * 16 + row // 64 * 2 + member % 2)
    k.gain[...] = k.gains[...].reshape(1, D)
    k.cgain[...] = k.cgains[...].reshape(1, D)
    lane = iota((1, D), 1) // 64
    for tempers, wide in ((k.tempers, k.temper), (k.ctempers, k.ctemper)):
        total = jnp.zeros((1, D), F32)
        for h in range(12):
            total = jnp.where(lane == h, tempers[h], total)
        wide[...] = total


def fill_routes(k, lon):
    slab = iota((32, HALF), 1)
    eye = jnp.where(iota((32, 32), 0) == iota((32, 32), 1), 1.0, 0.0)
    for b in range(2):
        place = k.place[b : b + 1, :]
        place = jnp.sum(jnp.where(eye > 0, place, 0), axis=1, keepdims=True)
        partner = (place // 64 - lon + 32) % 32
        slot = partner * 16 + place % 2
        for c in range(6):
            rows = slice(b * 192 + c * 32, b * 192 + c * 32 + 32)
            k.routes[rows, :] = one_where(slab == slot + 2 * c)


def pack(matrix, parts):
    return tn(matrix, jnp.concatenate(parts, axis=0)).astype(BF).reshape(32, 16, 128)


def lane_parts(rows):
    return [rows[:, c * 128 : (c + 1) * 128] for c in range(6)]


def pack_home(k, rows):
    return pack(k.routes[...], lane_parts(rows[:32]) + lane_parts(rows[32:]))


def unpack_home(k, slabs):
    parts = nn(k.routes[...], slabs[...].reshape(HALF, 128)).astype(BF)
    sides = []
    for b in range(2):
        pieces = [parts[b * 192 + c * 32 : b * 192 + c * 32 + 32] for c in range(6)]
        sides.append(jnp.concatenate(pieces, axis=1))
    return jnp.concatenate(sides, axis=0)


def pack_owner(k, rows):
    return pack(k.unpack[...], lane_parts(rows))


def unpack_owner(k, slabs):
    parts = nn(k.unpack[...], slabs[...].reshape(HALF, 128)).astype(BF)
    return jnp.concatenate([parts[c * 64 : c * 64 + 64] for c in range(6)], axis=1)


def rms_inverse(x):
    return lax.rsqrt(jnp.mean(x * x, axis=-1, keepdims=True) + 1e-05)


def rms_back(x, gain, grad):
    inverse = rms_inverse(x)
    scaled = grad * gain
    along = jnp.mean(x * scaled, axis=-1, keepdims=True)
    return inverse * (scaled - x * (inverse * inverse * along))


def unit_scale(u, heads):
    return lax.rsqrt(nn((u * u).astype(BF), heads) + 64e-06)


def key_back(scale, key, grad, heads):
    along = nn((key * grad).astype(BF), heads)
    return scale * (grad - key * along)


def query_back(scale, query, temper, raw, heads):
    along = nn((query * raw).astype(BF), heads)
    return scale * (temper * raw - query * along * (LN2 * LN2 / temper))


def block_diagonal(rows, heads):
    return jnp.concatenate([rows] * 4, axis=0) * heads


def chunk_rows(chunk):
    return pl.ds(pl.multiple_of(chunk * 256, 256), 256)


def both(ref, quad, columns=slice(None)):
    first = pl.multiple_of(quad * 128, 128)
    return jnp.concatenate(
        [ref[pl.ds(first, 128), columns], ref[pl.ds(first + HALF, 128), columns]], axis=0
    )


def put_both(ref, quad, value, columns=slice(None)):
    first = pl.multiple_of(quad * 128, 128)
    ref[pl.ds(first, 128), columns] = value[:128]
    ref[pl.ds(first + HALF, 128), columns] = value[128:]


def window(rows, w):
    return jnp.concatenate([rows[w * 32 : w * 32 + 32], rows[w * 32 + 128 : w * 32 + 160]], axis=0)


def from_parts(parts):
    return jnp.concatenate([p[:32] for p in parts] + [p[32:] for p in parts], axis=0)


def cells_project(k, chunk):
    rows = chunk_rows(chunk)
    x = k.x[rows, :].astype(F32)
    hidden = (x * rms_inverse(x) * k.gain[...]).astype(BF)
    heads = k.heads[...]
    for n in range(GROUPS):
        u = nn(hidden, k.w[:, lanes(n)])
        scale = unit_scale(u, heads)
        k.sq[rows, lanes(n)] = scale
        k.q[rows, lanes(n)] = (u * scale * (k.temper[:, lanes(n)] * LOG2E)).astype(BF)
    for n in range(GROUPS):
        u = nn(hidden, k.w[:, lanes(3 + n)])
        scale = unit_scale(u, heads)
        k.sk[rows, lanes(n)] = scale
        k.k[rows, lanes(n)] = (u * scale).astype(BF)
    for n in range(GROUPS):
        k.v[rows, lanes(n)] = nn(hidden, k.w[:, lanes(6 + n)]).astype(BF)


def cells_sensitivity(k, quad):
    halves = nn(k.split[...], k.graw[chunk_rows(quad), :]).astype(BF)
    put_both(k.g, quad, halves)
    put_both(k.do, quad, nt(halves, k.we[...]).astype(BF))


def cells_attend(k, quad):
    heads = k.heads[...]
    for n in range(GROUPS):
        query, key, value = (both(ref, quad, lanes(n)) for ref in (k.q, k.k, k.v))
        weights, sums = [], []
        for w in range(4):
            keys = block_diagonal(window(key, w), heads)
            weights.append(jnp.exp2(nt(window(query, w), keys)).astype(BF))
        for w in range(4):
            sums.append(nn(weights[w], block_diagonal(window(value, w), heads)))
        weights = from_parts(weights)
        put_both(k.p, quad, weights, lanes(n))
        put_both(k.op, quad, from_parts(sums), lanes(n))
        put_both(k.lp, quad, nn(weights, heads), lanes(n))


def carriers_project(k):
    c = k.cn[...].astype(F32)
    hidden = (c * rms_inverse(c) * k.gain[...]).astype(BF)
    heads = k.heads[...]
    for n in range(GROUPS):
        u = nn(hidden, k.w[:, lanes(3 + n)])
        scale = unit_scale(u, heads)
        k.skc[:, lanes(n)] = scale
        key = (u * scale).astype(BF)
        k.kc[:, lanes(n)] = key
        value = nn(hidden, k.w[:, lanes(6 + n)]).astype(BF)
        k.vc[:, lanes(n)] = value
    for chunk in range(4):
        rows = slice(chunk * 256, (chunk + 1) * 256)
        mask = k.carrier_heads[...]
        k.kcb[rows, :] = nn(k.spread[rows, :], k.kc[...]).astype(BF) * mask
        k.vcb[rows, :] = nn(k.spread[rows, :], k.vc[...]).astype(BF) * mask


def windows_finish(k, quad):
    keys, values, query = both(k.kcb, quad), both(k.vcb, quad), both(k.q, quad)
    mask = k.carrier_heads[...]
    weights = jnp.exp2(nt(query, keys)).astype(BF) * k.same[...]
    along = jnp.zeros((256, 256), F32)
    for n in range(GROUPS):
        inverse = 1.0 / (both(k.lp, quad, lanes(n)) + nn(weights, mask[:, lanes(n)]))
        attended = both(k.op, quad, lanes(n)) + nn(weights, values[:, lanes(n)])
        attended = attended * inverse
        put_both(k.o, quad, attended.astype(BF), lanes(n))
        sensitivity = both(k.do, quad, lanes(n)).astype(F32) * inverse
        product = (sensitivity * attended).astype(BF)
        put_both(k.t, quad, product, lanes(n))
        sensitivity = sensitivity.astype(BF)
        put_both(k.do, quad, sensitivity, lanes(n))
        along += nt(sensitivity, values[:, lanes(n)]) - nt(product, mask[:, lanes(n)])
    grads = (weights.astype(F32) * along).astype(BF)
    put_both(k.cg, quad, grads)
    put_both(k.dqkv, quad, (tn(grads, query) * LN2).astype(BF) * mask, slice(0, D))
    put_both(k.dqkv, quad, tn(weights, both(k.do, quad)).astype(BF) * mask, slice(D, 2 * D))


def carriers_back(k):
    heads = k.heads[...]
    select = k.gather[...]
    grad = jnp.zeros((64, D), F32)
    for n in range(GROUPS):
        dk = nn(select, k.dqkv[:, lanes(n)])
        du = key_back(k.skc[:, lanes(n)], k.kc[:, lanes(n)].astype(F32), dk, heads)
        grad += nt(du.astype(BF), k.w[:, lanes(3 + n)])
        dv = nn(select, k.dqkv[:, lanes(3 + n)]).astype(BF)
        grad += nt(dv, k.w[:, lanes(6 + n)])
    grad = grad.astype(BF).astype(F32)
    back = rms_back(k.cn[...].astype(F32), k.gain[...], grad)
    return (back + k.gsum[...]).astype(BF)


def cells_result(k, quad):
    total = both(k.x, quad).astype(F32) + nn(both(k.o, quad), k.we[...])
    put_both(k.xraw, quad, (total + nn(both(k.spread, quad), k.cn[...])).astype(BF))


def cells_back(k, quad):
    heads = k.heads[...]
    low = iota((64, 128), 1) < 64
    for n in range(GROUPS):
        query, key, value = (both(ref, quad, lanes(n)) for ref in (k.q, k.k, k.v))
        weights, sensitivity = (both(ref, quad, lanes(n)) for ref in (k.p, k.do))
        offset = nn(both(k.t, quad, lanes(n)), heads)
        along = []
        for w in range(4):
            values = block_diagonal(window(value, w), heads)
            along.append(nt(window(sensitivity, w), values))
        grads = (weights.astype(F32) * (from_parts(along) - offset)).astype(BF)
        raw, dk, dv = [], [], []
        for w in range(4):
            mine = window(grads, w)
            raw.append(nn(mine, block_diagonal(window(key, w), heads)))
            key_parts, value_parts = [], []
            for pair in range(2):
                part = slice(pair * 128, (pair + 1) * 128)
                pairs = tn(mine[:, part], window(query, w)[:, part])
                key_parts.append(jnp.where(low, pairs[:64], pairs[64:]))
                pairs = tn(window(weights, w)[:, part], window(sensitivity, w)[:, part])
                value_parts.append(jnp.where(low, pairs[:64], pairs[64:]))
            dk.append(jnp.concatenate(key_parts, axis=1))
            dv.append(jnp.concatenate(value_parts, axis=1))
        put_both(k.dqkv, quad, from_parts(dv).astype(BF), lanes(6 + n))
        raw = nn(both(k.cg, quad), both(k.kcb, quad, lanes(n))) + from_parts(raw)
        scale = both(k.sq, quad, lanes(n))
        du = query_back(scale, query.astype(F32), k.temper[:, lanes(n)], raw, heads)
        put_both(k.dqkv, quad, du.astype(BF), lanes(n))
        dk = (from_parts(dk) * LN2).astype(BF).astype(F32)
        du = key_back(both(k.sk, quad, lanes(n)), key.astype(F32), dk, heads)
        put_both(k.dqkv, quad, du.astype(BF), lanes(3 + n))


def cells_gradient(k, first, count):
    rows = slice(first, first + count)
    grad = nt(k.dqkv[rows, :], k.w[...]).astype(BF).astype(F32)
    back = rms_back(k.x[rows, :].astype(F32), k.gain[...], grad)
    k.dx[rows, :] = (back + k.g[rows, :].astype(F32)).astype(BF)


def pick(full):
    head = iota((64, 256), 1) // 64
    picked = full[:64]
    for h in range(1, 4):
        picked = jnp.where(head == h, full[h * 64 : h * 64 + 64], picked)
    return picked


def group_query(k, rows, n):
    u = nn(k.chid[rows, :], k.cw[:, lanes(n)])
    scale = unit_scale(u, k.heads[...])
    query = (u * scale * (k.ctemper[:, lanes(n)] * LOG2E)).astype(BF)
    k.cq[rows, lanes(n)] = query
    return query, scale


def group_forward(k):
    c = k.car[...].astype(F32)
    hidden = (c * rms_inverse(c) * k.cgain[...]).astype(BF)
    k.chid[...] = hidden
    heads = k.heads[...]
    ones = jnp.ones((256, 256), BF)
    for n in range(GROUPS):
        query, scale = group_query(k, slice(0, 64), n)
        k.csq[:, lanes(n)] = scale
        u = nn(hidden, k.cw[:, lanes(3 + n)])
        scale = unit_scale(u, heads)
        k.csk[:, lanes(n)] = scale[:64]
        key = (u * scale).astype(BF)
        k.ck[:, lanes(n)] = key
        value = nn(hidden, k.cw[:, lanes(6 + n)]).astype(BF)
        k.cv[:, lanes(n)] = value
        weights = jnp.exp2(nt(block_diagonal(query, heads), key)).astype(BF)
        k.crows[n] = weights
        inverse = 1.0 / nn(weights, ones)
        k.cl[:64, lanes(n)] = pick(inverse)
        k.co[:64, lanes(n)] = pick(nn(weights, value) * inverse)
    mixed = nn(k.co[:64, :].astype(BF), k.cwe[...])
    return (k.car[:64, :].astype(F32) + mixed).astype(BF)


def group_others(k):
    heads = k.heads[...]
    rows = slice(64, 256)
    for n in range(GROUPS):
        query, _ = group_query(k, rows, n)
        key, value = k.ck[:, lanes(n)], k.cv[:, lanes(n)]
        total = jnp.zeros((192, 256), F32)
        denominator = jnp.zeros((192, 256), F32)
        for h in range(4):
            mine = one_where(iota((256, 256), 1) // 64 == h)
            weights = jnp.exp2(nt(query, key * mine)).astype(BF)
            total += nn(weights, value * mine)
            denominator += nn(weights, mine)
        inverse = 1.0 / denominator
        k.cl[rows, lanes(n)] = inverse
        k.co[rows, lanes(n)] = total * inverse
        own = block_diagonal(key[:64], heads)
        k.ccolumns[n] = jnp.exp2(nt(own, k.cq[:, lanes(n)])).astype(BF)


def group_back(k):
    heads = k.heads[...]
    ones = jnp.ones((256, 256), BF)
    grad = jnp.zeros((64, D), F32)
    for n in range(GROUPS):
        sensitivity = nt(k.cgrad[...], k.cwe[lanes(n), :]).astype(BF).astype(F32)
        sensitivity = sensitivity * k.cl[:, lanes(n)]
        product = (sensitivity * k.co[:, lanes(n)]).astype(BF)
        sensitivity = sensitivity.astype(BF)
        query, key, value = k.cq[:, lanes(n)], k.ck[:, lanes(n)], k.cv[:, lanes(n)]
        along = nt(block_diagonal(sensitivity[:64], heads), value)
        along -= nn(block_diagonal(product[:64], heads), ones)
        grads = (k.crows[n].astype(F32) * along).astype(BF)
        raw = pick(nn(grads, key))
        du = query_back(
            k.csq[:, lanes(n)], query[:64].astype(F32), k.ctemper[:, lanes(n)], raw, heads
        )
        grad += nt(du.astype(BF), k.cw[:, lanes(n)])
        weights = k.ccolumns[n]
        along = nt(block_diagonal(value[:64], heads), sensitivity) - nt(heads, product)
        grads = (weights.astype(F32) * along).astype(BF)
        dk = (pick(nn(grads, query)) * LN2).astype(BF).astype(F32)
        du = key_back(k.csk[:, lanes(n)], key[:64].astype(F32), dk, heads)
        grad += nt(du.astype(BF), k.cw[:, lanes(3 + n)])
        dv = pick(nn(weights, sensitivity)).astype(BF)
        grad += nt(dv, k.cw[:, lanes(6 + n)])
    grad = grad.astype(BF).astype(F32)
    back = rms_back(k.car[:64, :].astype(F32), k.cgain[...], grad)
    return (back + k.cgrad[:64, :].astype(F32)).astype(BF)


def cells_split(k, quad):
    halves = nn(k.split[...], k.xraw[chunk_rows(quad), :]).astype(BF)
    first = quad * 128
    k.away[first : first + 128, :] = halves[:128]
    if quad == 0:
        k.rise[...] = halves[128:144]
        k.x[0:112, :] = halves[144:]
    else:
        k.x[first - 16 : first + 112, :] = halves[128:]
    means = nn(one_where(iota((16, 256), 1) // 16 == iota((16, 256), 0)), halves) * 0.0625
    k.means[0, quad * 8 : quad * 8 + 8, :] = means[:8]
    k.means[1, quad * 8 : quad * 8 + 8, :] = means[8:]


def assemble(result, grads, edges, out, field):
    cell, split = iota((256, 256), 0), iota((256, 256), 1)
    join = one_where(cell == split % 128 // 4 * 8 + split // 128 * 4 + split % 4)
    for part in range(2):
        rows, cells = slice(part * 128, part * 128 + 128), slice(part * 256, part * 256 + 256)
        group = iota((128, 32), 0) // 16 + (pl.program_id(0) * 2 + part) * 8
        out[cells, :] = nn(join, result[:, rows, :].reshape(256, D)).astype(BF)
        mine = one_where(group - 1 == iota((128, 32), 1))
        edge = one_where((group[:, :16] == 0) & (iota((128, 16), 1) == 15))
        left = nn(mine, edges[64:96, :]) + nn(edge, edges[96:112, :])
        right = nn(mine, edges[0:32, :]) + nn(edge, edges[112:128, :])
        total = grads[:, rows, :].reshape(256, D).astype(F32)
        total += jnp.concatenate([left, right], axis=0) * 0.0625
        field[cells, :] = nn(join, total.astype(BF)).astype(BF)


def body(k):
    lat, lon = lax.axis_index("lat"), lax.axis_index("lon")
    has_above, has_below = lat > 0, lat < 3
    above, below = lax.rem(lat + 3, 4), lax.rem(lat + 1, 4)
    west, east = lax.rem(lon + 31, 32), lax.rem(lon + 1, 32)

    loads = []
    for i, (source, target) in enumerate(
        (
            (k.x_hbm, k.xraw),
            (k.w_hbm, k.w),
            (k.g_hbm, k.graw),
            (k.we_hbm, k.we),
            (k.cw_hbm, k.cw),
            (k.cwe_hbm, k.cwe),
        )
    ):
        load = pltpu.make_async_copy(source, target, k.load_sem.at[i])
        load.start()
        loads.append(load)
    load_x, load_w, load_g, load_we, load_cw, load_cwe = loads

    @pl.when(jnp.logical_not(has_below))
    def _():
        k.x[496:512, :] = jnp.zeros((16, D), BF)
        k.x[1008:1024, :] = jnp.zeros((16, D), BF)
        k.car_below[...] = jnp.zeros((16, D), BF)
        k.car_corner[...] = jnp.zeros((16, D), BF)

    @pl.when(jnp.logical_not(has_above))
    def _():
        k.back[0:16, :] = jnp.zeros((16, D), BF)
        k.fall[...] = jnp.zeros((16, D), BF)
        k.edges[96:128, :] = jnp.zeros((32, D), BF)

    barrier = pltpu.get_barrier_semaphore()

    def greet(to_lat, to_lon):
        pl.semaphore_signal(barrier, inc=1, device_id=(to_lat, to_lon), device_id_type=MESH)

    far, sibling = lax.rem(lat + 2, 4), lat // 2 * 2 + (1 - lat % 2)

    def greet_lon(i, carry):
        greet(lat, lax.rem(lon + i, 32))
        greet(far, lax.rem(lon + i, 32))
        return carry

    lax.fori_loop(1, 32, greet_lon, 0)
    for s in range(1, 4):
        greet(lax.rem(lat + s, 4), lon)
    greet(above, west)
    greet(below, east)

    def send(source, target, sem, to_lat, to_lon):
        return pltpu.make_async_remote_copy(
            src_ref=source,
            dst_ref=target,
            send_sem=k.send_sem.at[sem],
            recv_sem=k.recv_sem.at[sem],
            device_id=(to_lat, to_lon),
            device_id_type=MESH,
        )

    def start(copies):
        for copy in copies:
            copy.start()

    def wait_received(copies):
        for copy in copies:
            copy.wait_recv()

    def await_bytes(ref, sem):
        pltpu.make_async_copy(ref, ref, sem).wait()

    fill_constants(k)
    fill_routes(k, lon)

    load_x.wait()
    for quad in range(4):
        cells_split(k, quad)
    up = one_where(iota((32, 32), 1) == iota((32, 32), 0) + 1)
    top = one_where((iota((16, 32), 0) == 15) & (iota((16, 32), 1) == 0))
    left, right = k.means[0].astype(BF), k.means[1].astype(BF)
    k.car_send[0:32, :] = nn(up, left).astype(BF)
    k.car_send[32:48, :] = nn(top, left).astype(BF)
    k.car_send[48:64, :] = nn(top, right).astype(BF)
    own = nn(up, right)
    pl.semaphore_wait(barrier, 67)
    carriers_west = send(k.car_send.at[0:32], k.car_beside, 0, lat, west)
    carriers_corner = send(k.car_send.at[32:48], k.car_corner, 1, above, west)
    carriers_above = send(k.car_send.at[48:64], k.car_below, 2, above, lon)
    cells = []
    for first in range(0, 496, 64):
        last = min(first + 64, 496)
        cells.append(
            send(
                k.away.at[16 + first : 16 + last],
                k.x.at[512 + first : 512 + last],
                20 + first // 64,
                lat,
                west,
            )
        )
    cells_corner = send(k.away.at[0:16], k.x.at[1008:1024], 5, above, west)
    cells_above = send(k.rise, k.x.at[496:512], 6, above, lon)
    carriers_west.start()

    @pl.when(has_above)
    def _():
        carriers_corner.start()
        carriers_above.start()
        cells_above.start()

    start(cells[0:2])
    load_w.wait()
    cells_project(k, 0)
    start(cells[2:3])
    load_g.wait()
    load_we.wait()
    loop(2, cells_sensitivity, k)

    carriers_west.wait_recv()

    @pl.when(has_below)
    def _():
        carriers_corner.wait_recv()
        carriers_above.wait_recv()

    lower = jnp.concatenate([jnp.zeros((16, D), F32), k.car_below[...].astype(F32)], axis=0)
    own = (own + lower).astype(BF)
    lower = jnp.concatenate([jnp.zeros((16, D), F32), k.car_corner[...].astype(F32)], axis=0)
    beside = (k.car_beside[...].astype(F32) + lower).astype(BF)

    def exchange(index, slabs, direction):
        out, back = k.slab_out.at[index], k.slab_in.at[index]
        out[...] = slabs
        back[0] = slabs[0]

        def step(i, carry):
            to_lon = lax.rem(lon + direction * i + 32, 32)
            pltpu.make_async_remote_copy(
                src_ref=out.at[i],
                dst_ref=back.at[i],
                send_sem=k.slab_send_sem.at[index],
                recv_sem=k.slab_recv_sem.at[index],
                device_id=(lat, to_lon),
                device_id_type=MESH,
            ).start()
            return carry

        def far_step(i, carry):
            to_lon = lax.rem(lon + direction * i + 32, 32)
            pltpu.make_async_remote_copy(
                src_ref=out.at[i],
                dst_ref=k.slab_far.at[index // 2, i],
                send_sem=k.far_send_sem.at[index // 2],
                recv_sem=k.far_recv_sem.at[index // 2],
                device_id=(far, to_lon),
                device_id_type=MESH,
            ).start()
            return carry

        lax.fori_loop(1, 32, step, 0)
        if direction == 1:
            lax.fori_loop(0, 32, far_step, 0)

    def group_gather(index, ref, sem):
        ref[0:64, :] = unpack_owner(k, exchanged(index))
        await_bytes(k.slab_far.at[index // 2], k.far_recv_sem.at[index // 2])
        ref[64:128, :] = unpack_owner(k, k.slab_far.at[index // 2])
        copy = send(ref.at[0:128], ref.at[128:256], sem, sibling, lon)
        copy.start()
        return copy

    def exchanged(index):
        await_bytes(k.slab_in.at[index, 1:32], k.slab_recv_sem.at[index])
        return k.slab_in.at[index]

    exchange(0, pack_home(k, jnp.concatenate([own, beside], axis=0)), 1)

    @pl.when(has_below)
    def _():
        cells_above.wait_recv()

    start(cells[3:4])
    cells_project(k, 1)
    start(cells[4:6])
    loop_from(2, 4, cells_sensitivity, k)
    k.gsum[...] = nn(k.gather[...], k.g[...])
    wait_received(cells[0:4])
    cells_project(k, 2)

    members = group_gather(0, k.car, 7)
    start(cells[6:7])
    cells_attend(k, 0)
    load_cw.wait()
    load_cwe.wait()
    members.wait_recv()
    exchange(1, pack_owner(k, group_forward(k)), -1)

    start(cells[7:8])

    @pl.when(has_above)
    def _():
        cells_corner.start()

    cells_attend(k, 1)
    wait_received(cells[4:8])

    @pl.when(has_below)
    def _():
        cells_corner.wait_recv()

    cells_project(k, 3)
    loop_from(2, 4, cells_attend, k)

    k.cn[...] = unpack_home(k, exchanged(1))
    carriers_project(k)
    loop(4, windows_finish, k)
    exchange(2, pack_home(k, carriers_back(k)), 1)

    grads = []
    for first in range(0, 496, 64):
        last = min(first + 64, 496)
        grads.append(
            send(
                k.dx.at[512 + first : 512 + last],
                k.back.at[16 + first : 16 + last],
                28 + first // 64,
                lat,
                east,
            )
        )
    grads_corner = send(k.dx.at[1008:1024], k.back.at[0:16], 15, below, east)
    grads_below = send(k.dx.at[496:512], k.fall, 16, below, lon)
    cells_back(k, 0)
    cells_gradient(k, 512, 128)
    start(grads[0:1])
    cells_back(k, 1)
    cells_gradient(k, 640, 128)
    start(grads[1:2])
    group_others(k)
    sensitivities = group_gather(2, k.cgrad, 8)
    start(grads[2:3])
    cells_back(k, 2)
    cells_gradient(k, 768, 128)
    start(grads[3:5])
    sensitivities.wait_recv()
    exchange(3, pack_owner(k, group_back(k)), -1)
    start(grads[5:6])
    cells_back(k, 3)
    cells_gradient(k, 896, 128)
    start(grads[6:7])
    cells_gradient(k, 256, 256)
    start(grads[7:8])

    @pl.when(has_below)
    def _():
        grads_corner.start()
        grads_below.start()

    cells_gradient(k, 0, 256)
    k.edges[0:64, :] = unpack_home(k, exchanged(3))
    pool_east = send(k.edges.at[32:64], k.edges.at[64:96], 17, lat, east)
    pool_corner = send(k.edges.at[48:64], k.edges.at[96:112], 18, below, east)
    pool_below = send(k.edges.at[16:32], k.edges.at[112:128], 19, below, lon)
    pool_east.start()

    @pl.when(has_below)
    def _():
        pool_corner.start()
        pool_below.start()

    loop(4, cells_result, k)
    store_out = pltpu.make_async_copy(k.xraw, k.result_hbm, k.load_sem.at[6])
    store_out.start()
    stores = [
        pltpu.make_async_copy(k.dx.at[0:496], k.grads_hbm.at[528:1024], k.store_sem.at[0]),
        pltpu.make_async_copy(k.back, k.grads_hbm.at[0:512], k.store_sem.at[1]),
        pltpu.make_async_copy(k.fall, k.grads_hbm.at[512:528], k.store_sem.at[2]),
        pltpu.make_async_copy(k.edges, k.edges_hbm, k.store_sem.at[3]),
    ]
    stores[0].start()

    wait_received(grads)

    @pl.when(has_above)
    def _():
        grads_corner.wait_recv()
        grads_below.wait_recv()

    start(stores[1:3])
    pool_east.wait_recv()

    @pl.when(has_above)
    def _():
        pool_corner.wait_recv()
        pool_below.wait_recv()

    stores[3].start()

    for copy in [carriers_west, members, sensitivities, pool_east] + cells + grads:
        copy.wait_send()

    @pl.when(has_above)
    def _():
        for copy in (carriers_corner, carriers_above, cells_corner, cells_above):
            copy.wait_send()

    @pl.when(has_below)
    def _():
        for copy in (grads_corner, grads_below, pool_corner, pool_below):
            copy.wait_send()

    for index in range(4):
        await_bytes(k.slab_out.at[index, 1:32], k.slab_send_sem.at[index])
    for index in range(2):
        await_bytes(k.slab_out.at[0], k.far_send_sem.at[index])
    store_out.wait()
    for store in stores:
        store.wait()


def loop(count, step, k):
    loop_from(0, count, step, k)


def loop_from(first, last, step, k):
    lax.fori_loop(first, last, lambda i, _: (step(k, i), 0)[1], 0)


SCRATCH = {
    "heads": ((256, 256), BF),
    "carrier_heads": ((256, D), BF),
    "same": ((256, 256), BF),
    "spread": ((1024, 64), BF),
    "gather": ((64, 1024), BF),
    "split": ((256, 256), BF),
    "unpack": ((384, HALF), BF),
    "routes": ((384, HALF), BF),
    "gain": ((1, D), F32),
    "cgain": ((1, D), F32),
    "temper": ((1, D), F32),
    "ctemper": ((1, D), F32),
    "xraw": ((1024, D), BF),
    "graw": ((1024, D), BF),
    "w": ((D, 3 * D), BF),
    "we": ((D, D), BF),
    "cw": ((D, 3 * D), BF),
    "cwe": ((D, D), BF),
    "x": ((1024, D), BF),
    "g": ((1024, D), BF),
    "away": ((HALF, D), BF),
    "rise": ((16, D), BF),
    "means": ((2, 32, D), F32),
    "car_send": ((64, D), BF),
    "car_beside": ((32, D), BF),
    "car_corner": ((16, D), BF),
    "car_below": ((16, D), BF),
    "slab_out": ((4, 32, 16, 128), BF),
    "slab_in": ((4, 32, 16, 128), BF),
    "slab_far": ((2, 32, 16, 128), BF),
    "car": ((256, D), BF),
    "cgrad": ((256, D), BF),
    "cn": ((64, D), BF),
    "edges": ((128, D), BF),
    "back": ((HALF, D), BF),
    "fall": ((16, D), BF),
    "dx": ((1024, D), BF),
    "q": ((1024, D), BF),
    "k": ((1024, D), BF),
    "v": ((1024, D), BF),
    "do": ((1024, D), BF),
    "o": ((1024, D), BF),
    "t": ((1024, D), BF),
    "p": ((1024, D), BF),
    "sq": ((1024, D), F32),
    "sk": ((1024, D), F32),
    "op": ((1024, D), F32),
    "lp": ((1024, D), F32),
    "kcb": ((1024, D), BF),
    "vcb": ((1024, D), BF),
    "kc": ((64, D), BF),
    "vc": ((64, D), BF),
    "skc": ((64, D), F32),
    "dqkv": ((1024, 3 * D), BF),
    "cq": ((256, D), BF),
    "ck": ((256, D), BF),
    "cv": ((256, D), BF),
    "chid": ((256, D), BF),
    "crows": ((3, 256, 256), BF),
    "ccolumns": ((3, 256, 256), BF),
    "cg": ((1024, 256), BF),
    "gsum": ((64, D), F32),
    "csq": ((64, D), F32),
    "csk": ((64, D), F32),
    "cl": ((256, D), F32),
    "co": ((256, D), F32),
}
SEMAPHORES = {
    "load_sem": 7,
    "store_sem": 4,
    "send_sem": 36,
    "recv_sem": 36,
    "far_send_sem": 2,
    "far_recv_sem": 2,
    "slab_send_sem": 4,
    "slab_recv_sem": 4,
}
INPUTS = (
    "x_hbm",
    "g_hbm",
    "w_hbm",
    "we_hbm",
    "cw_hbm",
    "cwe_hbm",
    "gains",
    "cgains",
    "place",
    "tempers",
    "ctempers",
)


def per_device(x, g, gain, w, we, tempers, cgain, cw, cwe, ctempers, place):
    names = INPUTS + ("result_hbm", "grads_hbm", "edges_hbm") + tuple(SCRATCH) + tuple(SEMAPHORES)

    def kernel(*refs):
        body(types.SimpleNamespace(**dict(zip(names, refs))))

    anywhere = pl.BlockSpec(memory_space=pl.ANY)
    vmem = pl.BlockSpec(memory_space=pltpu.VMEM)
    smem = pl.BlockSpec(memory_space=pltpu.SMEM)
    result, grads, edges = pl.pallas_call(
        kernel,
        out_shape=[jax.ShapeDtypeStruct((rows, D), BF) for rows in (1024, 1024, 128)],
        in_specs=[anywhere] * 6 + [vmem] * 3 + [smem] * 2,
        out_specs=[anywhere] * 3,
        scratch_shapes=[pltpu.VMEM(shape, kind) for shape, kind in SCRATCH.values()]
        + [pltpu.SemaphoreType.DMA((count,)) for count in SEMAPHORES.values()],
        compiler_params=pltpu.CompilerParams(
            collective_id=0, has_side_effects=True, vmem_limit_bytes=62 * 1024 * 1024
        ),
        name="block",
    )(
        x.reshape(1024, D),
        g.reshape(1024, D),
        w,
        we,
        cw,
        cwe,
        gain,
        cgain,
        place.T,
        tempers,
        ctempers,
    )
    halves = pl.BlockSpec((2, 256, D), lambda step: (0, step, 0))
    cells = pl.BlockSpec((512, D), lambda step: (step, 0))
    out, field = pl.pallas_call(
        assemble,
        grid=(2,),
        out_shape=[jax.ShapeDtypeStruct((1024, D), BF)] * 2,
        in_specs=[halves, halves, pl.BlockSpec((128, D), lambda step: (0, 0))],
        out_specs=[cells, cells],
        name="assemble",
    )(result.reshape(2, HALF, D), grads.reshape(2, HALF, D), edges)
    return out.reshape(128, 8, D), field.reshape(128, 8, D)


def solution(mesh):
    placed = (P("lat", "lon", None),) * 2 + (P(),) * 8 + (P("lat", "lon"),)
    return jax.shard_map(
        per_device,
        mesh=mesh,
        in_specs=placed,
        out_specs=(P("lat", "lon", None),) * 2,
        check_vma=False,
    )
```

```python
import types

import jax
import jax.numpy as jnp
from jax import lax
from jax.experimental import pallas as pl
from jax.experimental.pallas import tpu as pltpu
from jax.sharding import PartitionSpec as P

BF = jnp.bfloat16
F32 = jnp.float32
LOG2E = 1.4426950408889634
LN2 = 0.6931471805599453
D = 768
GROUPS = 3
WINDOWS = 16
CELLS = 64
HALF = 512
MESH = pl.DeviceIdType.MESH


def nn(a, b):
    return lax.dot_general(a, b, (((1,), (0,)), ((), ())), preferred_element_type=F32)


def nt(a, b):
    return lax.dot_general(a, b, (((1,), (1,)), ((), ())), preferred_element_type=F32)


def tn(a, b):
    return lax.dot_general(a, b, (((0,), (0,)), ((), ())), preferred_element_type=F32)


def iota(shape, axis):
    return lax.broadcasted_iota(jnp.int32, shape, axis)


def one_where(condition):
    return jnp.where(condition, 1.0, 0.0).astype(BF)


def lanes(n):
    return slice(n * 256, (n + 1) * 256)


def fill_constants(k):
    k.heads[...] = one_where(iota((256, 256), 0) // 64 == iota((256, 256), 1) // 64)
    k.carrier_heads[...] = one_where(iota((256, D), 0) % 16 == iota((256, D), 1) // 64)
    k.same[...] = one_where(iota((256, 256), 0) % 128 // 32 == iota((256, 256), 1) % 128 // 32)
    k.spread[...] = one_where(iota((1024, 64), 0) // 16 == iota((1024, 64), 1))
    k.gather[...] = one_where(iota((64, 1024), 1) // 16 == iota((64, 1024), 0))
    split, cell = iota((256, 256), 0), iota((256, 256), 1)
    k.split[...] = one_where(cell == split % 128 // 4 * 8 + split // 128 * 4 + split % 4)
    row, slab = iota((384, HALF), 0), iota((384, HALF), 1)
    member = row % 64
    k.unpack[...] = one_where(slab == member // 2 * 16 + row // 64 * 2 + member % 2)
    k.gain[...] = k.gains[...].reshape(1, D)
    k.cgain[...] = k.cgains[...].reshape(1, D)
    lane = iota((1, D), 1) // 64
    for tempers, wide in ((k.tempers, k.temper), (k.ctempers, k.ctemper)):
        total = jnp.zeros((1, D), F32)
        for h in range(12):
            total = jnp.where(lane == h, tempers[h], total)
        wide[...] = total


def fill_routes(k, lon):
    slab = iota((32, HALF), 1)
    eye = jnp.where(iota((32, 32), 0) == iota((32, 32), 1), 1.0, 0.0)
    for b in range(2):
        place = k.place[b : b + 1, :]
        place = jnp.sum(jnp.where(eye > 0, place, 0), axis=1, keepdims=True)
        partner = (place // 64 - lon + 32) % 32
        slot = partner * 16 + place % 2
        for c in range(6):
            rows = slice(b * 192 + c * 32, b * 192 + c * 32 + 32)
            k.routes[rows, :] = one_where(slab == slot + 2 * c)


def pack(matrix, parts):
    return tn(matrix, jnp.concatenate(parts, axis=0)).astype(BF).reshape(32, 16, 128)


def lane_parts(rows):
    return [rows[:, c * 128 : (c + 1) * 128] for c in range(6)]


def pack_home(k, rows):
    return pack(k.routes[...], lane_parts(rows[:32]) + lane_parts(rows[32:]))


def unpack_home(k, slabs):
    parts = nn(k.routes[...], slabs[...].reshape(HALF, 128)).astype(BF)
    sides = []
    for b in range(2):
        pieces = [parts[b * 192 + c * 32 : b * 192 + c * 32 + 32] for c in range(6)]
        sides.append(jnp.concatenate(pieces, axis=1))
    return jnp.concatenate(sides, axis=0)


def pack_owner(k, rows):
    return pack(k.unpack[...], lane_parts(rows))


def unpack_owner(k, slabs):
    parts = nn(k.unpack[...], slabs[...].reshape(HALF, 128)).astype(BF)
    return jnp.concatenate([parts[c * 64 : c * 64 + 64] for c in range(6)], axis=1)


def rms_inverse(x):
    return lax.rsqrt(jnp.mean(x * x, axis=-1, keepdims=True) + 1e-05)


def rms_back(x, gain, grad):
    inverse = rms_inverse(x)
    scaled = grad * gain
    along = jnp.mean(x * scaled, axis=-1, keepdims=True)
    return inverse * (scaled - x * (inverse * inverse * along))


def unit_scale(u, heads):
    return lax.rsqrt(nn((u * u).astype(BF), heads) + 64e-06)


def key_back(scale, key, grad, heads):
    along = nn((key * grad).astype(BF), heads)
    return scale * (grad - key * along)


def query_back(scale, query, temper, raw, heads):
    along = nn((query * raw).astype(BF), heads)
    return scale * (temper * raw - query * along * (LN2 * LN2 / temper))


def block_diagonal(rows, heads):
    return jnp.concatenate([rows] * 4, axis=0) * heads


def chunk_rows(chunk):
    return pl.ds(pl.multiple_of(chunk * 256, 256), 256)


def both(ref, quad, columns=slice(None)):
    first = pl.multiple_of(quad * 128, 128)
    return jnp.concatenate(
        [ref[pl.ds(first, 128), columns], ref[pl.ds(first + HALF, 128), columns]], axis=0
    )


def put_both(ref, quad, value, columns=slice(None)):
    first = pl.multiple_of(quad * 128, 128)
    ref[pl.ds(first, 128), columns] = value[:128]
    ref[pl.ds(first + HALF, 128), columns] = value[128:]


def window(rows, w):
    return jnp.concatenate([rows[w * 32 : w * 32 + 32], rows[w * 32 + 128 : w * 32 + 160]], axis=0)


def from_parts(parts):
    return jnp.concatenate([p[:32] for p in parts] + [p[32:] for p in parts], axis=0)


def cells_project(k, chunk):
    rows = chunk_rows(chunk)
    x = k.x[rows, :].astype(F32)
    hidden = (x * rms_inverse(x) * k.gain[...]).astype(BF)
    heads = k.heads[...]
    for n in range(GROUPS):
        u = nn(hidden, k.w[:, lanes(n)])
        scale = unit_scale(u, heads)
        k.sq[rows, lanes(n)] = scale
        k.q[rows, lanes(n)] = (u * scale * (k.temper[:, lanes(n)] * LOG2E)).astype(BF)
    for n in range(GROUPS):
        u = nn(hidden, k.w[:, lanes(3 + n)])
        scale = unit_scale(u, heads)
        k.sk[rows, lanes(n)] = scale
        k.k[rows, lanes(n)] = (u * scale).astype(BF)
    for n in range(GROUPS):
        k.v[rows, lanes(n)] = nn(hidden, k.w[:, lanes(6 + n)]).astype(BF)


def cells_sensitivity(k, quad):
    halves = nn(k.split[...], k.graw[chunk_rows(quad), :]).astype(BF)
    put_both(k.g, quad, halves)
    put_both(k.do, quad, nt(halves, k.we[...]).astype(BF))


def cells_attend(k, quad):
    heads = k.heads[...]
    for n in range(GROUPS):
        query, key, value = (both(ref, quad, lanes(n)) for ref in (k.q, k.k, k.v))
        weights, sums = [], []
        for w in range(4):
            keys = block_diagonal(window(key, w), heads)
            weights.append(jnp.exp2(nt(window(query, w), keys)).astype(BF))
        for w in range(4):
            sums.append(nn(weights[w], block_diagonal(window(value, w), heads)))
        weights = from_parts(weights)
        put_both(k.p, quad, weights, lanes(n))
        put_both(k.op, quad, from_parts(sums), lanes(n))
        put_both(k.lp, quad, nn(weights, heads), lanes(n))


def carriers_project(k):
    c = k.cn[...].astype(F32)
    hidden = (c * rms_inverse(c) * k.gain[...]).astype(BF)
    heads = k.heads[...]
    for n in range(GROUPS):
        u = nn(hidden, k.w[:, lanes(3 + n)])
        scale = unit_scale(u, heads)
        k.skc[:, lanes(n)] = scale
        key = (u * scale).astype(BF)
        k.kc[:, lanes(n)] = key
        value = nn(hidden, k.w[:, lanes(6 + n)]).astype(BF)
        k.vc[:, lanes(n)] = value
    for chunk in range(4):
        rows = slice(chunk * 256, (chunk + 1) * 256)
        mask = k.carrier_heads[...]
        k.kcb[rows, :] = nn(k.spread[rows, :], k.kc[...]).astype(BF) * mask
        k.vcb[rows, :] = nn(k.spread[rows, :], k.vc[...]).astype(BF) * mask


def windows_finish(k, quad):
    keys, values, query = both(k.kcb, quad), both(k.vcb, quad), both(k.q, quad)
    mask = k.carrier_heads[...]
    weights = jnp.exp2(nt(query, keys)).astype(BF) * k.same[...]
    along = jnp.zeros((256, 256), F32)
    for n in range(GROUPS):
        inverse = 1.0 / (both(k.lp, quad, lanes(n)) + nn(weights, mask[:, lanes(n)]))
        attended = both(k.op, quad, lanes(n)) + nn(weights, values[:, lanes(n)])
        attended = attended * inverse
        put_both(k.o, quad, attended.astype(BF), lanes(n))
        sensitivity = both(k.do, quad, lanes(n)).astype(F32) * inverse
        product = (sensitivity * attended).astype(BF)
        put_both(k.t, quad, product, lanes(n))
        sensitivity = sensitivity.astype(BF)
        put_both(k.do, quad, sensitivity, lanes(n))
        along += nt(sensitivity, values[:, lanes(n)]) - nt(product, mask[:, lanes(n)])
    grads = (weights.astype(F32) * along).astype(BF)
    put_both(k.cg, quad, grads)
    put_both(k.dqkv, quad, (tn(grads, query) * LN2).astype(BF) * mask, slice(0, D))
    put_both(k.dqkv, quad, tn(weights, both(k.do, quad)).astype(BF) * mask, slice(D, 2 * D))


def carriers_back(k):
    heads = k.heads[...]
    select = k.gather[...]
    grad = jnp.zeros((64, D), F32)
    for n in range(GROUPS):
        dk = nn(select, k.dqkv[:, lanes(n)])
        du = key_back(k.skc[:, lanes(n)], k.kc[:, lanes(n)].astype(F32), dk, heads)
        grad += nt(du.astype(BF), k.w[:, lanes(3 + n)])
        dv = nn(select, k.dqkv[:, lanes(3 + n)]).astype(BF)
        grad += nt(dv, k.w[:, lanes(6 + n)])
    grad = grad.astype(BF).astype(F32)
    back = rms_back(k.cn[...].astype(F32), k.gain[...], grad)
    return (back + k.gsum[...]).astype(BF)


def cells_result(k, quad):
    total = both(k.x, quad).astype(F32) + nn(both(k.o, quad), k.we[...])
    put_both(k.xraw, quad, (total + nn(both(k.spread, quad), k.cn[...])).astype(BF))


def cells_back(k, quad):
    heads = k.heads[...]
    low = iota((64, 128), 1) < 64
    for n in range(GROUPS):
        query, key, value = (both(ref, quad, lanes(n)) for ref in (k.q, k.k, k.v))
        weights, sensitivity = (both(ref, quad, lanes(n)) for ref in (k.p, k.do))
        offset = nn(both(k.t, quad, lanes(n)), heads)
        along = []
        for w in range(4):
            values = block_diagonal(window(value, w), heads)
            along.append(nt(window(sensitivity, w), values))
        grads = (weights.astype(F32) * (from_parts(along) - offset)).astype(BF)
        raw, dk, dv = [], [], []
        for w in range(4):
            mine = window(grads, w)
            raw.append(nn(mine, block_diagonal(window(key, w), heads)))
            key_parts, value_parts = [], []
            for pair in range(2):
                part = slice(pair * 128, (pair + 1) * 128)
                pairs = tn(mine[:, part], window(query, w)[:, part])
                key_parts.append(jnp.where(low, pairs[:64], pairs[64:]))
                pairs = tn(window(weights, w)[:, part], window(sensitivity, w)[:, part])
                value_parts.append(jnp.where(low, pairs[:64], pairs[64:]))
            dk.append(jnp.concatenate(key_parts, axis=1))
            dv.append(jnp.concatenate(value_parts, axis=1))
        put_both(k.dqkv, quad, from_parts(dv).astype(BF), lanes(6 + n))
        raw = nn(both(k.cg, quad), both(k.kcb, quad, lanes(n))) + from_parts(raw)
        scale = both(k.sq, quad, lanes(n))
        du = query_back(scale, query.astype(F32), k.temper[:, lanes(n)], raw, heads)
        put_both(k.dqkv, quad, du.astype(BF), lanes(n))
        dk = (from_parts(dk) * LN2).astype(BF).astype(F32)
        du = key_back(both(k.sk, quad, lanes(n)), key.astype(F32), dk, heads)
        put_both(k.dqkv, quad, du.astype(BF), lanes(3 + n))


def cells_gradient(k, first, count):
    rows = pl.ds(pl.multiple_of(first, 128), count)
    grad = nt(k.dqkv[rows, :], k.w[...]).astype(BF).astype(F32)
    back = rms_back(k.x[rows, :].astype(F32), k.gain[...], grad)
    k.dx[rows, :] = (back + k.g[rows, :].astype(F32)).astype(BF)


def pick(full):
    head = iota((64, 256), 1) // 64
    picked = full[:64]
    for h in range(1, 4):
        picked = jnp.where(head == h, full[h * 64 : h * 64 + 64], picked)
    return picked


def group_query(k, rows, n):
    u = nn(k.chid[rows, :], k.cw[:, lanes(n)])
    scale = unit_scale(u, k.heads[...])
    query = (u * scale * (k.ctemper[:, lanes(n)] * LOG2E)).astype(BF)
    k.cq[rows, lanes(n)] = query
    return query, scale


def group_forward(k):
    c = k.car[...].astype(F32)
    hidden = (c * rms_inverse(c) * k.cgain[...]).astype(BF)
    k.chid[...] = hidden
    heads = k.heads[...]
    ones = jnp.ones((256, 256), BF)
    for n in range(GROUPS):
        query, scale = group_query(k, slice(0, 64), n)
        k.csq[:, lanes(n)] = scale
        u = nn(hidden, k.cw[:, lanes(3 + n)])
        scale = unit_scale(u, heads)
        k.csk[:, lanes(n)] = scale[:64]
        key = (u * scale).astype(BF)
        k.ck[:, lanes(n)] = key
        value = nn(hidden, k.cw[:, lanes(6 + n)]).astype(BF)
        k.cv[:, lanes(n)] = value
        weights = jnp.exp2(nt(block_diagonal(query, heads), key)).astype(BF)
        k.crows[n] = weights
        inverse = 1.0 / nn(weights, ones)
        k.cl[:64, lanes(n)] = pick(inverse)
        k.co[:64, lanes(n)] = pick(nn(weights, value) * inverse)
    mixed = nn(k.co[:64, :].astype(BF), k.cwe[...])
    return (k.car[:64, :].astype(F32) + mixed).astype(BF)


def group_others(k):
    heads = k.heads[...]
    rows = slice(64, 256)
    for n in range(GROUPS):
        query, _ = group_query(k, rows, n)
        key, value = k.ck[:, lanes(n)], k.cv[:, lanes(n)]
        total = jnp.zeros((192, 256), F32)
        denominator = jnp.zeros((192, 256), F32)
        for h in range(4):
            mine = one_where(iota((256, 256), 1) // 64 == h)
            weights = jnp.exp2(nt(query, key * mine)).astype(BF)
            total += nn(weights, value * mine)
            denominator += nn(weights, mine)
        inverse = 1.0 / denominator
        k.cl[rows, lanes(n)] = inverse
        k.co[rows, lanes(n)] = total * inverse
        own = block_diagonal(key[:64], heads)
        k.ccolumns[n] = jnp.exp2(nt(own, k.cq[:, lanes(n)])).astype(BF)


def group_back(k):
    heads = k.heads[...]
    ones = jnp.ones((256, 256), BF)
    grad = jnp.zeros((64, D), F32)
    for n in range(GROUPS):
        sensitivity = nt(k.cgrad[...], k.cwe[lanes(n), :]).astype(BF).astype(F32)
        sensitivity = sensitivity * k.cl[:, lanes(n)]
        product = (sensitivity * k.co[:, lanes(n)]).astype(BF)
        sensitivity = sensitivity.astype(BF)
        query, key, value = k.cq[:, lanes(n)], k.ck[:, lanes(n)], k.cv[:, lanes(n)]
        along = nt(block_diagonal(sensitivity[:64], heads), value)
        along -= nn(block_diagonal(product[:64], heads), ones)
        grads = (k.crows[n].astype(F32) * along).astype(BF)
        raw = pick(nn(grads, key))
        du = query_back(
            k.csq[:, lanes(n)], query[:64].astype(F32), k.ctemper[:, lanes(n)], raw, heads
        )
        grad += nt(du.astype(BF), k.cw[:, lanes(n)])
        weights = k.ccolumns[n]
        along = nt(block_diagonal(value[:64], heads), sensitivity) - nt(heads, product)
        grads = (weights.astype(F32) * along).astype(BF)
        dk = (pick(nn(grads, query)) * LN2).astype(BF).astype(F32)
        du = key_back(k.csk[:, lanes(n)], key[:64].astype(F32), dk, heads)
        grad += nt(du.astype(BF), k.cw[:, lanes(3 + n)])
        dv = pick(nn(weights, sensitivity)).astype(BF)
        grad += nt(dv, k.cw[:, lanes(6 + n)])
    grad = grad.astype(BF).astype(F32)
    back = rms_back(k.car[:64, :].astype(F32), k.cgain[...], grad)
    return (back + k.cgrad[:64, :].astype(F32)).astype(BF)


def cells_split(k, quad):
    halves = nn(k.split[...], k.xraw[chunk_rows(quad), :]).astype(BF)
    first = quad * 128
    k.away[first : first + 128, :] = halves[:128]
    if quad == 0:
        k.rise[...] = halves[128:144]
        k.x[0:112, :] = halves[144:]
    else:
        k.x[first - 16 : first + 112, :] = halves[128:]
    means = nn(one_where(iota((16, 256), 1) // 16 == iota((16, 256), 0)), halves) * 0.0625
    k.means[0, quad * 8 : quad * 8 + 8, :] = means[:8]
    k.means[1, quad * 8 : quad * 8 + 8, :] = means[8:]


def assemble(result, grads, edges, out, field):
    cell, split = iota((256, 256), 0), iota((256, 256), 1)
    join = one_where(cell == split % 128 // 4 * 8 + split // 128 * 4 + split % 4)
    for part in range(2):
        rows, cells = slice(part * 128, part * 128 + 128), slice(part * 256, part * 256 + 256)
        group = iota((128, 32), 0) // 16 + (pl.program_id(0) * 2 + part) * 8
        out[cells, :] = nn(join, result[:, rows, :].reshape(256, D)).astype(BF)
        mine = one_where(group - 1 == iota((128, 32), 1))
        edge = one_where((group[:, :16] == 0) & (iota((128, 16), 1) == 15))
        left = nn(mine, edges[64:96, :]) + nn(edge, edges[96:112, :])
        right = nn(mine, edges[0:32, :]) + nn(edge, edges[112:128, :])
        total = grads[:, rows, :].reshape(256, D).astype(F32)
        total += jnp.concatenate([left, right], axis=0) * 0.0625
        field[cells, :] = nn(join, total.astype(BF)).astype(BF)


def body(k):
    lat, lon = lax.axis_index("lat"), lax.axis_index("lon")
    has_above, has_below = lat > 0, lat < 3
    above, below = lax.rem(lat + 3, 4), lax.rem(lat + 1, 4)
    west, east = lax.rem(lon + 31, 32), lax.rem(lon + 1, 32)

    loads = []
    for i, (source, target) in enumerate(
        (
            (k.x_hbm, k.xraw),
            (k.w_hbm, k.w),
            (k.g_hbm, k.graw),
            (k.we_hbm, k.we),
            (k.cw_hbm, k.cw),
            (k.cwe_hbm, k.cwe),
        )
    ):
        load = pltpu.make_async_copy(source, target, k.load_sem.at[i])
        load.start()
        loads.append(load)
    load_x, load_w, load_g, load_we, load_cw, load_cwe = loads

    @pl.when(jnp.logical_not(has_below))
    def _():
        k.x[496:512, :] = jnp.zeros((16, D), BF)
        k.x[1008:1024, :] = jnp.zeros((16, D), BF)
        k.car_below[...] = jnp.zeros((16, D), BF)
        k.car_corner[...] = jnp.zeros((16, D), BF)

    @pl.when(jnp.logical_not(has_above))
    def _():
        k.back[0:16, :] = jnp.zeros((16, D), BF)
        k.fall[...] = jnp.zeros((16, D), BF)
        k.edges[96:128, :] = jnp.zeros((32, D), BF)

    barrier = pltpu.get_barrier_semaphore()

    def greet(to_lat, to_lon):
        pl.semaphore_signal(barrier, inc=1, device_id=(to_lat, to_lon), device_id_type=MESH)

    far, sibling = lax.rem(lat + 2, 4), lat // 2 * 2 + (1 - lat % 2)

    def greet_lon(i, carry):
        greet(lat, lax.rem(lon + i, 32))
        greet(far, lax.rem(lon + i, 32))
        return carry

    lax.fori_loop(1, 32, greet_lon, 0)
    for s in range(1, 4):
        greet(lax.rem(lat + s, 4), lon)
    greet(above, west)
    greet(below, east)

    def send(source, target, sem, to_lat, to_lon):
        return pltpu.make_async_remote_copy(
            src_ref=source,
            dst_ref=target,
            send_sem=k.send_sem.at[sem],
            recv_sem=k.recv_sem.at[sem],
            device_id=(to_lat, to_lon),
            device_id_type=MESH,
        )

    def start(copies):
        for copy in copies:
            copy.start()

    def wait_received(copies):
        for copy in copies:
            copy.wait_recv()

    def await_bytes(ref, sem):
        pltpu.make_async_copy(ref, ref, sem).wait()

    fill_constants(k)
    fill_routes(k, lon)

    load_x.wait()
    for quad in range(4):
        cells_split(k, quad)
    up = one_where(iota((32, 32), 1) == iota((32, 32), 0) + 1)
    top = one_where((iota((16, 32), 0) == 15) & (iota((16, 32), 1) == 0))
    left, right = k.means[0].astype(BF), k.means[1].astype(BF)
    k.car_send[0:32, :] = nn(up, left).astype(BF)
    k.car_send[32:48, :] = nn(top, left).astype(BF)
    k.car_send[48:64, :] = nn(top, right).astype(BF)
    own = nn(up, right)
    pl.semaphore_wait(barrier, 67)
    carriers_west = send(k.car_send.at[0:32], k.car_beside, 0, lat, west)
    carriers_corner = send(k.car_send.at[32:48], k.car_corner, 1, above, west)
    carriers_above = send(k.car_send.at[48:64], k.car_below, 2, above, lon)
    cells = []
    for first in range(0, 496, 64):
        last = min(first + 64, 496)
        cells.append(
            send(
                k.away.at[16 + first : 16 + last],
                k.x.at[512 + first : 512 + last],
                20 + first // 64,
                lat,
                west,
            )
        )
    cells_corner = send(k.away.at[0:16], k.x.at[1008:1024], 5, above, west)
    cells_above = send(k.rise, k.x.at[496:512], 6, above, lon)
    carriers_west.start()

    @pl.when(has_above)
    def _():
        carriers_corner.start()
        carriers_above.start()
        cells_above.start()

    start(cells[0:2])
    load_w.wait()
    cells_project(k, 0)
    start(cells[2:3])
    load_g.wait()
    load_we.wait()
    loop(2, cells_sensitivity, k)

    carriers_west.wait_recv()

    @pl.when(has_below)
    def _():
        carriers_corner.wait_recv()
        carriers_above.wait_recv()

    lower = jnp.concatenate([jnp.zeros((16, D), F32), k.car_below[...].astype(F32)], axis=0)
    own = (own + lower).astype(BF)
    lower = jnp.concatenate([jnp.zeros((16, D), F32), k.car_corner[...].astype(F32)], axis=0)
    beside = (k.car_beside[...].astype(F32) + lower).astype(BF)

    def exchange(index, slabs, direction):
        out, back = k.slab_out.at[index], k.slab_in.at[index]
        out[...] = slabs
        back[0] = slabs[0]

        def step(i, carry):
            to_lon = lax.rem(lon + direction * i + 32, 32)
            pltpu.make_async_remote_copy(
                src_ref=out.at[i],
                dst_ref=back.at[i],
                send_sem=k.slab_send_sem.at[index],
                recv_sem=k.slab_recv_sem.at[index],
                device_id=(lat, to_lon),
                device_id_type=MESH,
            ).start()
            return carry

        def far_step(i, carry):
            to_lon = lax.rem(lon + direction * i + 32, 32)
            pltpu.make_async_remote_copy(
                src_ref=out.at[i],
                dst_ref=k.slab_far.at[index // 2, i],
                send_sem=k.far_send_sem.at[index // 2],
                recv_sem=k.far_recv_sem.at[index // 2],
                device_id=(far, to_lon),
                device_id_type=MESH,
            ).start()
            return carry

        lax.fori_loop(1, 32, step, 0)
        if direction == 1:
            lax.fori_loop(0, 32, far_step, 0)

    def group_gather(index, ref, sem):
        ref[0:64, :] = unpack_owner(k, exchanged(index))
        await_bytes(k.slab_far.at[index // 2], k.far_recv_sem.at[index // 2])
        ref[64:128, :] = unpack_owner(k, k.slab_far.at[index // 2])
        copy = send(ref.at[0:128], ref.at[128:256], sem, sibling, lon)
        copy.start()
        return copy

    def exchanged(index):
        await_bytes(k.slab_in.at[index, 1:32], k.slab_recv_sem.at[index])
        return k.slab_in.at[index]

    exchange(0, pack_home(k, jnp.concatenate([own, beside], axis=0)), 1)

    @pl.when(has_below)
    def _():
        cells_above.wait_recv()

    start(cells[3:4])
    cells_project(k, 1)
    start(cells[4:6])
    loop_from(2, 4, cells_sensitivity, k)
    k.gsum[...] = nn(k.gather[...], k.g[...])
    wait_received(cells[0:4])
    cells_project(k, 2)

    members = group_gather(0, k.car, 7)
    start(cells[6:7])
    cells_attend(k, 0)
    load_cw.wait()
    load_cwe.wait()
    members.wait_recv()
    exchange(1, pack_owner(k, group_forward(k)), -1)

    start(cells[7:8])

    @pl.when(has_above)
    def _():
        cells_corner.start()

    cells_attend(k, 1)
    wait_received(cells[4:8])

    @pl.when(has_below)
    def _():
        cells_corner.wait_recv()

    cells_project(k, 3)
    loop_from(2, 4, cells_attend, k)

    k.cn[...] = unpack_home(k, exchanged(1))
    carriers_project(k)
    loop(4, windows_finish, k)
    exchange(2, pack_home(k, carriers_back(k)), 1)

    grads = []
    for first in range(0, 496, 64):
        last = min(first + 64, 496)
        grads.append(
            send(
                k.dx.at[512 + first : 512 + last],
                k.back.at[16 + first : 16 + last],
                28 + first // 64,
                lat,
                east,
            )
        )
    grads_corner = send(k.dx.at[1008:1024], k.back.at[0:16], 15, below, east)
    grads_below = send(k.dx.at[496:512], k.fall, 16, below, lon)
    sensitivities = send(k.cgrad.at[0:128], k.cgrad.at[128:256], 8, sibling, lon)

    def back_step(quad, carry):
        @pl.when(quad == 2)
        def _():
            group_others(k)
            group_gather(2, k.cgrad, 8)
            start(grads[2:3])

        @pl.when(quad == 3)
        def _():
            start(grads[3:5])
            sensitivities.wait_recv()
            exchange(3, pack_owner(k, group_back(k)), -1)
            start(grads[5:6])

        cells_back(k, quad)
        cells_gradient(k, 512 + quad * 128, 128)
        for piece, at in ((0, 0), (1, 1), (6, 3)):
            pl.when(quad == at)(grads[piece].start)
        return carry

    lax.fori_loop(0, 4, back_step, 0)

    def left_step(i, carry):
        cells_gradient(k, 256 - 256 * i, 256)
        pl.when(i == 0)(grads[7].start)

        @pl.when((i == 0) & has_below)
        def _():
            grads_corner.start()
            grads_below.start()

        return carry

    lax.fori_loop(0, 2, left_step, 0)
    k.edges[0:64, :] = unpack_home(k, exchanged(3))
    pool_east = send(k.edges.at[32:64], k.edges.at[64:96], 17, lat, east)
    pool_corner = send(k.edges.at[48:64], k.edges.at[96:112], 18, below, east)
    pool_below = send(k.edges.at[16:32], k.edges.at[112:128], 19, below, lon)
    pool_east.start()

    @pl.when(has_below)
    def _():
        pool_corner.start()
        pool_below.start()

    loop(4, cells_result, k)
    store_out = pltpu.make_async_copy(k.xraw, k.result_hbm, k.load_sem.at[6])
    store_out.start()
    stores = [
        pltpu.make_async_copy(k.dx.at[0:496], k.grads_hbm.at[528:1024], k.store_sem.at[0]),
        pltpu.make_async_copy(k.back, k.grads_hbm.at[0:512], k.store_sem.at[1]),
        pltpu.make_async_copy(k.fall, k.grads_hbm.at[512:528], k.store_sem.at[2]),
        pltpu.make_async_copy(k.edges, k.edges_hbm, k.store_sem.at[3]),
    ]
    stores[0].start()

    wait_received(grads)

    @pl.when(has_above)
    def _():
        grads_corner.wait_recv()
        grads_below.wait_recv()

    start(stores[1:3])
    pool_east.wait_recv()

    @pl.when(has_above)
    def _():
        pool_corner.wait_recv()
        pool_below.wait_recv()

    stores[3].start()

    for copy in [carriers_west, members, sensitivities, pool_east] + cells + grads:
        copy.wait_send()

    @pl.when(has_above)
    def _():
        for copy in (carriers_corner, carriers_above, cells_corner, cells_above):
            copy.wait_send()

    @pl.when(has_below)
    def _():
        for copy in (grads_corner, grads_below, pool_corner, pool_below):
            copy.wait_send()

    for index in range(4):
        await_bytes(k.slab_out.at[index, 1:32], k.slab_send_sem.at[index])
    for index in range(2):
        await_bytes(k.slab_out.at[0], k.far_send_sem.at[index])
    store_out.wait()
    for store in stores:
        store.wait()


def loop(count, step, k):
    loop_from(0, count, step, k)


def loop_from(first, last, step, k):
    lax.fori_loop(first, last, lambda i, _: (step(k, i), 0)[1], 0)


SCRATCH = {
    "heads": ((256, 256), BF),
    "carrier_heads": ((256, D), BF),
    "same": ((256, 256), BF),
    "spread": ((1024, 64), BF),
    "gather": ((64, 1024), BF),
    "split": ((256, 256), BF),
    "unpack": ((384, HALF), BF),
    "routes": ((384, HALF), BF),
    "gain": ((1, D), F32),
    "cgain": ((1, D), F32),
    "temper": ((1, D), F32),
    "ctemper": ((1, D), F32),
    "xraw": ((1024, D), BF),
    "graw": ((1024, D), BF),
    "w": ((D, 3 * D), BF),
    "we": ((D, D), BF),
    "cw": ((D, 3 * D), BF),
    "cwe": ((D, D), BF),
    "x": ((1024, D), BF),
    "g": ((1024, D), BF),
    "away": ((HALF, D), BF),
    "rise": ((16, D), BF),
    "means": ((2, 32, D), F32),
    "car_send": ((64, D), BF),
    "car_beside": ((32, D), BF),
    "car_corner": ((16, D), BF),
    "car_below": ((16, D), BF),
    "slab_out": ((4, 32, 16, 128), BF),
    "slab_in": ((4, 32, 16, 128), BF),
    "slab_far": ((2, 32, 16, 128), BF),
    "car": ((256, D), BF),
    "cgrad": ((256, D), BF),
    "cn": ((64, D), BF),
    "edges": ((128, D), BF),
    "back": ((HALF, D), BF),
    "fall": ((16, D), BF),
    "dx": ((1024, D), BF),
    "q": ((1024, D), BF),
    "k": ((1024, D), BF),
    "v": ((1024, D), BF),
    "do": ((1024, D), BF),
    "o": ((1024, D), BF),
    "t": ((1024, D), BF),
    "p": ((1024, D), BF),
    "sq": ((1024, D), F32),
    "sk": ((1024, D), F32),
    "op": ((1024, D), F32),
    "lp": ((1024, D), F32),
    "kcb": ((1024, D), BF),
    "vcb": ((1024, D), BF),
    "kc": ((64, D), BF),
    "vc": ((64, D), BF),
    "skc": ((64, D), F32),
    "dqkv": ((1024, 3 * D), BF),
    "cq": ((256, D), BF),
    "ck": ((256, D), BF),
    "cv": ((256, D), BF),
    "chid": ((256, D), BF),
    "crows": ((3, 256, 256), BF),
    "ccolumns": ((3, 256, 256), BF),
    "cg": ((1024, 256), BF),
    "gsum": ((64, D), F32),
    "csq": ((64, D), F32),
    "csk": ((64, D), F32),
    "cl": ((256, D), F32),
    "co": ((256, D), F32),
}
SEMAPHORES = {
    "load_sem": 7,
    "store_sem": 4,
    "send_sem": 36,
    "recv_sem": 36,
    "far_send_sem": 2,
    "far_recv_sem": 2,
    "slab_send_sem": 4,
    "slab_recv_sem": 4,
}
INPUTS = (
    "x_hbm",
    "g_hbm",
    "w_hbm",
    "we_hbm",
    "cw_hbm",
    "cwe_hbm",
    "gains",
    "cgains",
    "place",
    "tempers",
    "ctempers",
)


def per_device(x, g, gain, w, we, tempers, cgain, cw, cwe, ctempers, place):
    names = INPUTS + ("result_hbm", "grads_hbm", "edges_hbm") + tuple(SCRATCH) + tuple(SEMAPHORES)

    def kernel(*refs):
        body(types.SimpleNamespace(**dict(zip(names, refs))))

    anywhere = pl.BlockSpec(memory_space=pl.ANY)
    vmem = pl.BlockSpec(memory_space=pltpu.VMEM)
    smem = pl.BlockSpec(memory_space=pltpu.SMEM)
    result, grads, edges = pl.pallas_call(
        kernel,
        out_shape=[jax.ShapeDtypeStruct((rows, D), BF) for rows in (1024, 1024, 128)],
        in_specs=[anywhere] * 6 + [vmem] * 3 + [smem] * 2,
        out_specs=[anywhere] * 3,
        scratch_shapes=[pltpu.VMEM(shape, kind) for shape, kind in SCRATCH.values()]
        + [pltpu.SemaphoreType.DMA((count,)) for count in SEMAPHORES.values()],
        compiler_params=pltpu.CompilerParams(
            collective_id=0, has_side_effects=True, vmem_limit_bytes=62 * 1024 * 1024
        ),
        name="block",
    )(
        x.reshape(1024, D),
        g.reshape(1024, D),
        w,
        we,
        cw,
        cwe,
        gain,
        cgain,
        place.T,
        tempers,
        ctempers,
    )
    halves = pl.BlockSpec((2, 256, D), lambda step: (0, step, 0))
    cells = pl.BlockSpec((512, D), lambda step: (step, 0))
    out, field = pl.pallas_call(
        assemble,
        grid=(2,),
        out_shape=[jax.ShapeDtypeStruct((1024, D), BF)] * 2,
        in_specs=[halves, halves, pl.BlockSpec((128, D), lambda step: (0, 0))],
        out_specs=[cells, cells],
        name="assemble",
    )(result.reshape(2, HALF, D), grads.reshape(2, HALF, D), edges)
    return out.reshape(128, 8, D), field.reshape(128, 8, D)


def solution(mesh):
    placed = (P("lat", "lon", None),) * 2 + (P(),) * 8 + (P("lat", "lon"),)
    return jax.shard_map(
        per_device,
        mesh=mesh,
        in_specs=placed,
        out_specs=(P("lat", "lon", None),) * 2,
        check_vma=False,
    )
```

```python
import types

import jax
import jax.numpy as jnp
from jax import lax
from jax.experimental import pallas as pl
from jax.experimental.pallas import tpu as pltpu
from jax.sharding import PartitionSpec as P

BF = jnp.bfloat16
F32 = jnp.float32
LOG2E = 1.4426950408889634
LN2 = 0.6931471805599453
D = 768
GROUPS = 3
WINDOWS = 16
CELLS = 64
HALF = 512
MESH = pl.DeviceIdType.MESH


def nn(a, b):
    return lax.dot_general(a, b, (((1,), (0,)), ((), ())), preferred_element_type=F32)


def nt(a, b):
    return lax.dot_general(a, b, (((1,), (1,)), ((), ())), preferred_element_type=F32)


def tn(a, b):
    return lax.dot_general(a, b, (((0,), (0,)), ((), ())), preferred_element_type=F32)


def iota(shape, axis):
    return lax.broadcasted_iota(jnp.int32, shape, axis)


def one_where(condition):
    return jnp.where(condition, 1.0, 0.0).astype(BF)


def lanes(n):
    return slice(n * 256, (n + 1) * 256)


def fill_constants(k):
    k.heads[...] = one_where(iota((256, 256), 0) // 64 == iota((256, 256), 1) // 64)
    k.carrier_heads[...] = one_where(iota((256, D), 0) % 16 == iota((256, D), 1) // 64)
    k.same[...] = one_where(iota((256, 256), 0) % 128 // 32 == iota((256, 256), 1) % 128 // 32)
    k.spread[...] = one_where(iota((1024, 64), 0) // 16 == iota((1024, 64), 1))
    k.gather[...] = one_where(iota((64, 1024), 1) // 16 == iota((64, 1024), 0))
    split, cell = iota((256, 256), 0), iota((256, 256), 1)
    k.split[...] = one_where(cell == split % 128 // 4 * 8 + split // 128 * 4 + split % 4)
    row, slab = iota((384, HALF), 0), iota((384, HALF), 1)
    member = row % 64
    k.unpack[...] = one_where(slab == member // 2 * 16 + row // 64 * 2 + member % 2)
    k.gain[...] = k.gains[...].reshape(1, D)
    k.cgain[...] = k.cgains[...].reshape(1, D)
    lane = iota((1, D), 1) // 64
    for tempers, wide in ((k.tempers, k.temper), (k.ctempers, k.ctemper)):
        total = jnp.zeros((1, D), F32)
        for h in range(12):
            total = jnp.where(lane == h, tempers[h], total)
        wide[...] = total


def fill_routes(k, lon):
    slab = iota((32, HALF), 1)
    eye = jnp.where(iota((32, 32), 0) == iota((32, 32), 1), 1.0, 0.0)
    for b in range(2):
        place = k.place[b : b + 1, :]
        place = jnp.sum(jnp.where(eye > 0, place, 0), axis=1, keepdims=True)
        partner = (place // 64 - lon + 32) % 32
        slot = partner * 16 + place % 2
        for c in range(6):
            rows = slice(b * 192 + c * 32, b * 192 + c * 32 + 32)
            k.routes[rows, :] = one_where(slab == slot + 2 * c)


def pack(matrix, parts):
    return tn(matrix, jnp.concatenate(parts, axis=0)).astype(BF).reshape(32, 16, 128)


def lane_parts(rows):
    return [rows[:, c * 128 : (c + 1) * 128] for c in range(6)]


def pack_home(k, rows):
    return pack(k.routes[...], lane_parts(rows[:32]) + lane_parts(rows[32:]))


def unpack_home(k, slabs):
    parts = nn(k.routes[...], slabs[...].reshape(HALF, 128)).astype(BF)
    sides = []
    for b in range(2):
        pieces = [parts[b * 192 + c * 32 : b * 192 + c * 32 + 32] for c in range(6)]
        sides.append(jnp.concatenate(pieces, axis=1))
    return jnp.concatenate(sides, axis=0)


def pack_owner(k, rows):
    return pack(k.unpack[...], lane_parts(rows))


def unpack_owner(k, slabs):
    parts = nn(k.unpack[...], slabs[...].reshape(HALF, 128)).astype(BF)
    return jnp.concatenate([parts[c * 64 : c * 64 + 64] for c in range(6)], axis=1)


def rms_inverse(x):
    return lax.rsqrt(jnp.mean(x * x, axis=-1, keepdims=True) + 1e-05)


def rms_back(x, gain, grad):
    inverse = rms_inverse(x)
    scaled = grad * gain
    along = jnp.mean(x * scaled, axis=-1, keepdims=True)
    return inverse * (scaled - x * (inverse * inverse * along))


def unit_scale(u, heads):
    return lax.rsqrt(nn((u * u).astype(BF), heads) + 64e-06)


def key_back(scale, key, grad, heads):
    along = nn((key * grad).astype(BF), heads)
    return scale * (grad - key * along)


def query_back(scale, query, temper, raw, heads):
    along = nn((query * raw).astype(BF), heads)
    return scale * (temper * raw - query * along * (LN2 * LN2 / temper))


def block_diagonal(rows, heads):
    return jnp.concatenate([rows] * 4, axis=0) * heads


def chunk_rows(chunk):
    return pl.ds(pl.multiple_of(chunk * 256, 256), 256)


def both(ref, quad, columns=slice(None)):
    first = pl.multiple_of(quad * 128, 128)
    return jnp.concatenate(
        [ref[pl.ds(first, 128), columns], ref[pl.ds(first + HALF, 128), columns]], axis=0
    )


def put_both(ref, quad, value, columns=slice(None)):
    first = pl.multiple_of(quad * 128, 128)
    ref[pl.ds(first, 128), columns] = value[:128]
    ref[pl.ds(first + HALF, 128), columns] = value[128:]


def window(rows, w):
    return jnp.concatenate([rows[w * 32 : w * 32 + 32], rows[w * 32 + 128 : w * 32 + 160]], axis=0)


def from_parts(parts):
    return jnp.concatenate([p[:32] for p in parts] + [p[32:] for p in parts], axis=0)


def cells_project(k, chunk):
    rows = chunk_rows(chunk)
    x = k.x[rows, :].astype(F32)
    hidden = (x * rms_inverse(x) * k.gain[...]).astype(BF)
    heads = k.heads[...]
    for n in range(GROUPS):
        u = nn(hidden, k.w[:, lanes(n)])
        scale = unit_scale(u, heads)
        k.sq[rows, lanes(n)] = scale
        k.q[rows, lanes(n)] = (u * scale * (k.temper[:, lanes(n)] * LOG2E)).astype(BF)
    for n in range(GROUPS):
        u = nn(hidden, k.w[:, lanes(3 + n)])
        scale = unit_scale(u, heads)
        k.sk[rows, lanes(n)] = scale
        k.k[rows, lanes(n)] = (u * scale).astype(BF)
    for n in range(GROUPS):
        k.v[rows, lanes(n)] = nn(hidden, k.w[:, lanes(6 + n)]).astype(BF)


def cells_sensitivity(k, quad):
    halves = nn(k.split[...], k.graw[chunk_rows(quad), :]).astype(BF)
    put_both(k.g, quad, halves)
    put_both(k.do, quad, nt(halves, k.we[...]).astype(BF))


def cells_attend(k, quad):
    heads = k.heads[...]
    for n in range(GROUPS):
        query, key, value = (both(ref, quad, lanes(n)) for ref in (k.q, k.k, k.v))
        weights, sums = [], []
        for w in range(4):
            keys = block_diagonal(window(key, w), heads)
            weights.append(jnp.exp2(nt(window(query, w), keys)).astype(BF))
        for w in range(4):
            sums.append(nn(weights[w], block_diagonal(window(value, w), heads)))
        weights = from_parts(weights)
        put_both(k.p, quad, weights, lanes(n))
        put_both(k.op, quad, from_parts(sums), lanes(n))
        put_both(k.lp, quad, nn(weights, heads), lanes(n))


def carriers_project(k):
    c = k.cn[...].astype(F32)
    hidden = (c * rms_inverse(c) * k.gain[...]).astype(BF)
    heads = k.heads[...]
    for n in range(GROUPS):
        u = nn(hidden, k.w[:, lanes(3 + n)])
        scale = unit_scale(u, heads)
        k.skc[:, lanes(n)] = scale
        key = (u * scale).astype(BF)
        k.kc[:, lanes(n)] = key
        value = nn(hidden, k.w[:, lanes(6 + n)]).astype(BF)
        k.vc[:, lanes(n)] = value
    for chunk in range(4):
        rows = slice(chunk * 256, (chunk + 1) * 256)
        mask = k.carrier_heads[...]
        k.kcb[rows, :] = nn(k.spread[rows, :], k.kc[...]).astype(BF) * mask
        k.vcb[rows, :] = nn(k.spread[rows, :], k.vc[...]).astype(BF) * mask


def windows_finish(k, quad):
    keys, values, query = both(k.kcb, quad), both(k.vcb, quad), both(k.q, quad)
    mask = k.carrier_heads[...]
    weights = jnp.exp2(nt(query, keys)).astype(BF) * k.same[...]
    along = jnp.zeros((256, 256), F32)
    for n in range(GROUPS):
        inverse = 1.0 / (both(k.lp, quad, lanes(n)) + nn(weights, mask[:, lanes(n)]))
        attended = both(k.op, quad, lanes(n)) + nn(weights, values[:, lanes(n)])
        attended = attended * inverse
        put_both(k.o, quad, attended.astype(BF), lanes(n))
        sensitivity = both(k.do, quad, lanes(n)).astype(F32) * inverse
        product = (sensitivity * attended).astype(BF)
        put_both(k.t, quad, product, lanes(n))
        sensitivity = sensitivity.astype(BF)
        put_both(k.do, quad, sensitivity, lanes(n))
        along += nt(sensitivity, values[:, lanes(n)]) - nt(product, mask[:, lanes(n)])
    grads = (weights.astype(F32) * along).astype(BF)
    put_both(k.cg, quad, grads)
    put_both(k.dqkv, quad, (tn(grads, query) * LN2).astype(BF) * mask, slice(0, D))
    put_both(k.dqkv, quad, tn(weights, both(k.do, quad)).astype(BF) * mask, slice(D, 2 * D))


def carriers_back(k):
    heads = k.heads[...]
    select = k.gather[...]
    grad = jnp.zeros((64, D), F32)
    for n in range(GROUPS):
        dk = nn(select, k.dqkv[:, lanes(n)])
        du = key_back(k.skc[:, lanes(n)], k.kc[:, lanes(n)].astype(F32), dk, heads)
        grad += nt(du.astype(BF), k.w[:, lanes(3 + n)])
        dv = nn(select, k.dqkv[:, lanes(3 + n)]).astype(BF)
        grad += nt(dv, k.w[:, lanes(6 + n)])
    grad = grad.astype(BF).astype(F32)
    back = rms_back(k.cn[...].astype(F32), k.gain[...], grad)
    return (back + k.gsum[...]).astype(BF)


def cells_result(k, quad):
    total = both(k.x, quad).astype(F32) + nn(both(k.o, quad), k.we[...])
    put_both(k.xraw, quad, (total + nn(both(k.spread, quad), k.cn[...])).astype(BF))


def cells_back(k, quad):
    heads = k.heads[...]
    low = iota((64, 128), 1) < 64
    for n in range(GROUPS):
        query, key, value = (both(ref, quad, lanes(n)) for ref in (k.q, k.k, k.v))
        weights, sensitivity = (both(ref, quad, lanes(n)) for ref in (k.p, k.do))
        offset = nn(both(k.t, quad, lanes(n)), heads)
        along = []
        for w in range(4):
            values = block_diagonal(window(value, w), heads)
            along.append(nt(window(sensitivity, w), values))
        grads = (weights.astype(F32) * (from_parts(along) - offset)).astype(BF)
        raw, dk, dv = [], [], []
        for w in range(4):
            mine = window(grads, w)
            raw.append(nn(mine, block_diagonal(window(key, w), heads)))
            key_parts, value_parts = [], []
            for pair in range(2):
                part = slice(pair * 128, (pair + 1) * 128)
                pairs = tn(mine[:, part], window(query, w)[:, part])
                key_parts.append(jnp.where(low, pairs[:64], pairs[64:]))
                pairs = tn(window(weights, w)[:, part], window(sensitivity, w)[:, part])
                value_parts.append(jnp.where(low, pairs[:64], pairs[64:]))
            dk.append(jnp.concatenate(key_parts, axis=1))
            dv.append(jnp.concatenate(value_parts, axis=1))
        put_both(k.dqkv, quad, from_parts(dv).astype(BF), lanes(6 + n))
        raw = nn(both(k.cg, quad), both(k.kcb, quad, lanes(n))) + from_parts(raw)
        scale = both(k.sq, quad, lanes(n))
        du = query_back(scale, query.astype(F32), k.temper[:, lanes(n)], raw, heads)
        put_both(k.dqkv, quad, du.astype(BF), lanes(n))
        dk = (from_parts(dk) * LN2).astype(BF).astype(F32)
        du = key_back(both(k.sk, quad, lanes(n)), key.astype(F32), dk, heads)
        put_both(k.dqkv, quad, du.astype(BF), lanes(3 + n))


def cells_gradient(k, first, count):
    rows = pl.ds(pl.multiple_of(first, 128), count)
    grad = nt(k.dqkv[rows, :], k.w[...]).astype(BF).astype(F32)
    back = rms_back(k.x[rows, :].astype(F32), k.gain[...], grad)
    k.dx[rows, :] = (back + k.g[rows, :].astype(F32)).astype(BF)


def pick(full):
    head = iota((64, 256), 1) // 64
    picked = full[:64]
    for h in range(1, 4):
        picked = jnp.where(head == h, full[h * 64 : h * 64 + 64], picked)
    return picked


def group_query(k, rows, n):
    u = nn(k.chid[rows, :], k.cw[:, lanes(n)])
    scale = unit_scale(u, k.heads[...])
    query = (u * scale * (k.ctemper[:, lanes(n)] * LOG2E)).astype(BF)
    k.cq[rows, lanes(n)] = query
    return query, scale


def group_forward(k):
    c = k.car[...].astype(F32)
    hidden = (c * rms_inverse(c) * k.cgain[...]).astype(BF)
    k.chid[...] = hidden
    heads = k.heads[...]
    ones = jnp.ones((256, 256), BF)
    for n in range(GROUPS):
        query, scale = group_query(k, slice(0, 64), n)
        k.csq[:, lanes(n)] = scale
        u = nn(hidden, k.cw[:, lanes(3 + n)])
        scale = unit_scale(u, heads)
        k.csk[:, lanes(n)] = scale[:64]
        key = (u * scale).astype(BF)
        k.ck[:, lanes(n)] = key
        value = nn(hidden, k.cw[:, lanes(6 + n)]).astype(BF)
        k.cv[:, lanes(n)] = value
        weights = jnp.exp2(nt(block_diagonal(query, heads), key)).astype(BF)
        k.crows[n] = weights
        inverse = 1.0 / nn(weights, ones)
        k.cl[:64, lanes(n)] = pick(inverse)
        k.co[:64, lanes(n)] = pick(nn(weights, value) * inverse)
    mixed = nn(k.co[:64, :].astype(BF), k.cwe[...])
    return (k.car[:64, :].astype(F32) + mixed).astype(BF)


def group_others(k):
    heads = k.heads[...]
    rows = slice(64, 256)
    for n in range(GROUPS):
        query, _ = group_query(k, rows, n)
        key, value = k.ck[:, lanes(n)], k.cv[:, lanes(n)]
        total = jnp.zeros((192, 256), F32)
        denominator = jnp.zeros((192, 256), F32)
        for h in range(4):
            mine = one_where(iota((256, 256), 1) // 64 == h)
            weights = jnp.exp2(nt(query, key * mine)).astype(BF)
            total += nn(weights, value * mine)
            denominator += nn(weights, mine)
        inverse = 1.0 / denominator
        k.cl[rows, lanes(n)] = inverse
        k.co[rows, lanes(n)] = total * inverse
        own = block_diagonal(key[:64], heads)
        k.ccolumns[n] = jnp.exp2(nt(own, k.cq[:, lanes(n)])).astype(BF)


def group_back(k):
    heads = k.heads[...]
    ones = jnp.ones((256, 256), BF)
    grad = jnp.zeros((64, D), F32)
    for n in range(GROUPS):
        sensitivity = nt(k.cgrad[...], k.cwe[lanes(n), :]).astype(BF).astype(F32)
        sensitivity = sensitivity * k.cl[:, lanes(n)]
        product = (sensitivity * k.co[:, lanes(n)]).astype(BF)
        sensitivity = sensitivity.astype(BF)
        query, key, value = k.cq[:, lanes(n)], k.ck[:, lanes(n)], k.cv[:, lanes(n)]
        along = nt(block_diagonal(sensitivity[:64], heads), value)
        along -= nn(block_diagonal(product[:64], heads), ones)
        grads = (k.crows[n].astype(F32) * along).astype(BF)
        raw = pick(nn(grads, key))
        du = query_back(
            k.csq[:, lanes(n)], query[:64].astype(F32), k.ctemper[:, lanes(n)], raw, heads
        )
        grad += nt(du.astype(BF), k.cw[:, lanes(n)])
        weights = k.ccolumns[n]
        along = nt(block_diagonal(value[:64], heads), sensitivity) - nt(heads, product)
        grads = (weights.astype(F32) * along).astype(BF)
        dk = (pick(nn(grads, query)) * LN2).astype(BF).astype(F32)
        du = key_back(k.csk[:, lanes(n)], key[:64].astype(F32), dk, heads)
        grad += nt(du.astype(BF), k.cw[:, lanes(3 + n)])
        dv = pick(nn(weights, sensitivity)).astype(BF)
        grad += nt(dv, k.cw[:, lanes(6 + n)])
    grad = grad.astype(BF).astype(F32)
    back = rms_back(k.car[:64, :].astype(F32), k.cgain[...], grad)
    return (back + k.cgrad[:64, :].astype(F32)).astype(BF)


def cells_split(k, quad):
    halves = nn(k.split[...], k.xraw[chunk_rows(quad), :]).astype(BF)
    first = quad * 128
    k.away[first : first + 128, :] = halves[:128]
    if quad == 0:
        k.rise[...] = halves[128:144]
        k.x[0:112, :] = halves[144:]
    else:
        k.x[first - 16 : first + 112, :] = halves[128:]
    means = nn(one_where(iota((16, 256), 1) // 16 == iota((16, 256), 0)), halves) * 0.0625
    k.means[0, quad * 8 : quad * 8 + 8, :] = means[:8]
    k.means[1, quad * 8 : quad * 8 + 8, :] = means[8:]


def assemble(result, grads, edges, out, field):
    cell, split = iota((256, 256), 0), iota((256, 256), 1)
    join = one_where(cell == split % 128 // 4 * 8 + split // 128 * 4 + split % 4)
    for part in range(2):
        rows, cells = slice(part * 128, part * 128 + 128), slice(part * 256, part * 256 + 256)
        group = iota((128, 32), 0) // 16 + (pl.program_id(0) * 2 + part) * 8
        out[cells, :] = nn(join, result[:, rows, :].reshape(256, D)).astype(BF)
        mine = one_where(group - 1 == iota((128, 32), 1))
        edge = one_where((group[:, :16] == 0) & (iota((128, 16), 1) == 15))
        left = nn(mine, edges[64:96, :]) + nn(edge, edges[96:112, :])
        right = nn(mine, edges[0:32, :]) + nn(edge, edges[112:128, :])
        total = grads[:, rows, :].reshape(256, D).astype(F32)
        total += jnp.concatenate([left, right], axis=0) * 0.0625
        field[cells, :] = nn(join, total.astype(BF)).astype(BF)


def body(k):
    lat, lon = lax.axis_index("lat"), lax.axis_index("lon")
    has_above, has_below = lat > 0, lat < 3
    above, below = lax.rem(lat + 3, 4), lax.rem(lat + 1, 4)
    west, east = lax.rem(lon + 31, 32), lax.rem(lon + 1, 32)

    loads = []
    for i, (source, target) in enumerate(
        (
            (k.x_hbm, k.xraw),
            (k.w_hbm, k.w),
            (k.g_hbm, k.graw),
            (k.we_hbm, k.we),
            (k.cw_hbm, k.cw),
            (k.cwe_hbm, k.cwe),
        )
    ):
        load = pltpu.make_async_copy(source, target, k.load_sem.at[i])
        load.start()
        loads.append(load)
    load_x, load_w, load_g, load_we, load_cw, load_cwe = loads

    @pl.when(jnp.logical_not(has_below))
    def _():
        k.x[496:512, :] = jnp.zeros((16, D), BF)
        k.x[1008:1024, :] = jnp.zeros((16, D), BF)
        k.car_below[...] = jnp.zeros((16, D), BF)
        k.car_corner[...] = jnp.zeros((16, D), BF)

    @pl.when(jnp.logical_not(has_above))
    def _():
        k.back[0:16, :] = jnp.zeros((16, D), BF)
        k.fall[...] = jnp.zeros((16, D), BF)
        k.edges[96:128, :] = jnp.zeros((32, D), BF)

    barrier = pltpu.get_barrier_semaphore()

    def greet(to_lat, to_lon):
        pl.semaphore_signal(barrier, inc=1, device_id=(to_lat, to_lon), device_id_type=MESH)

    far, sibling = lax.rem(lat + 2, 4), lat // 2 * 2 + (1 - lat % 2)

    def greet_lon(i, carry):
        greet(lat, lax.rem(lon + i, 32))
        greet(far, lax.rem(lon + i, 32))
        return carry

    lax.fori_loop(1, 32, greet_lon, 0)
    for s in range(1, 4):
        greet(lax.rem(lat + s, 4), lon)
    greet(above, west)
    greet(below, east)

    def send(source, target, sem, to_lat, to_lon):
        return pltpu.make_async_remote_copy(
            src_ref=source,
            dst_ref=target,
            send_sem=k.send_sem.at[sem],
            recv_sem=k.recv_sem.at[sem],
            device_id=(to_lat, to_lon),
            device_id_type=MESH,
        )

    def start(copies):
        for copy in copies:
            copy.start()

    def wait_received(copies):
        for copy in copies:
            copy.wait_recv()

    def await_bytes(ref, sem):
        pltpu.make_async_copy(ref, ref, sem).wait()

    fill_constants(k)
    fill_routes(k, lon)

    load_x.wait()
    for quad in range(4):
        cells_split(k, quad)
    up = one_where(iota((32, 32), 1) == iota((32, 32), 0) + 1)
    top = one_where((iota((16, 32), 0) == 15) & (iota((16, 32), 1) == 0))
    left, right = k.means[0].astype(BF), k.means[1].astype(BF)
    k.car_send[0:32, :] = nn(up, left).astype(BF)
    k.car_send[32:48, :] = nn(top, left).astype(BF)
    k.car_send[48:64, :] = nn(top, right).astype(BF)
    own = nn(up, right)
    pl.semaphore_wait(barrier, 67)
    carriers_west = send(k.car_send.at[0:32], k.car_beside, 0, lat, west)
    carriers_corner = send(k.car_send.at[32:48], k.car_corner, 1, above, west)
    carriers_above = send(k.car_send.at[48:64], k.car_below, 2, above, lon)
    cells = []
    for first in range(0, 496, 64):
        last = min(first + 64, 496)
        cells.append(
            send(
                k.away.at[16 + first : 16 + last],
                k.x.at[512 + first : 512 + last],
                20 + first // 64,
                lat,
                west,
            )
        )
    cells_corner = send(k.away.at[0:16], k.x.at[1008:1024], 5, above, west)
    cells_above = send(k.rise, k.x.at[496:512], 6, above, lon)
    carriers_west.start()

    @pl.when(has_above)
    def _():
        carriers_corner.start()
        carriers_above.start()
        cells_above.start()

    start(cells[0:2])
    load_w.wait()
    cells_project(k, 0)
    start(cells[2:3])
    load_g.wait()
    load_we.wait()
    loop(2, cells_sensitivity, k)

    carriers_west.wait_recv()

    @pl.when(has_below)
    def _():
        carriers_corner.wait_recv()
        carriers_above.wait_recv()

    lower = jnp.concatenate([jnp.zeros((16, D), F32), k.car_below[...].astype(F32)], axis=0)
    own = (own + lower).astype(BF)
    lower = jnp.concatenate([jnp.zeros((16, D), F32), k.car_corner[...].astype(F32)], axis=0)
    beside = (k.car_beside[...].astype(F32) + lower).astype(BF)

    def exchange(index, slabs, direction):
        out, back = k.slab_out.at[index], k.slab_in.at[index]
        out[...] = slabs
        back[0] = slabs[0]

        def step(i, carry):
            to_lon = lax.rem(lon + direction * i + 32, 32)
            pltpu.make_async_remote_copy(
                src_ref=out.at[i],
                dst_ref=back.at[i],
                send_sem=k.slab_send_sem.at[index],
                recv_sem=k.slab_recv_sem.at[index],
                device_id=(lat, to_lon),
                device_id_type=MESH,
            ).start()
            return carry

        def far_step(i, carry):
            to_lon = lax.rem(lon + direction * i + 32, 32)
            pltpu.make_async_remote_copy(
                src_ref=out.at[i],
                dst_ref=k.slab_far.at[index // 2, i],
                send_sem=k.far_send_sem.at[index // 2],
                recv_sem=k.far_recv_sem.at[index // 2],
                device_id=(far, to_lon),
                device_id_type=MESH,
            ).start()
            return carry

        lax.fori_loop(1, 32, step, 0)
        if direction == 1:
            lax.fori_loop(0, 32, far_step, 0)

    def group_gather(index, ref, sem):
        ref[0:64, :] = unpack_owner(k, exchanged(index))
        await_bytes(k.slab_far.at[index // 2], k.far_recv_sem.at[index // 2])
        ref[64:128, :] = unpack_owner(k, k.slab_far.at[index // 2])
        copy = send(ref.at[0:128], ref.at[128:256], sem, sibling, lon)
        copy.start()
        return copy

    def exchanged(index):
        await_bytes(k.slab_in.at[index, 1:32], k.slab_recv_sem.at[index])
        return k.slab_in.at[index]

    exchange(0, pack_home(k, jnp.concatenate([own, beside], axis=0)), 1)

    @pl.when(has_below)
    def _():
        cells_above.wait_recv()

    start(cells[3:4])
    cells_project(k, 1)
    start(cells[4:6])
    loop_from(2, 4, cells_sensitivity, k)
    k.gsum[...] = nn(k.gather[...], k.g[...])
    wait_received(cells[0:4])
    cells_project(k, 2)

    members = group_gather(0, k.car, 7)
    start(cells[6:7])
    cells_attend(k, 0)
    load_cw.wait()
    load_cwe.wait()
    members.wait_recv()
    exchange(1, pack_owner(k, group_forward(k)), -1)

    start(cells[7:8])

    @pl.when(has_above)
    def _():
        cells_corner.start()

    cells_attend(k, 1)
    group_others(k)
    wait_received(cells[4:8])

    @pl.when(has_below)
    def _():
        cells_corner.wait_recv()

    cells_project(k, 3)
    loop_from(2, 4, cells_attend, k)

    k.cn[...] = unpack_home(k, exchanged(1))
    carriers_project(k)
    loop(4, windows_finish, k)
    exchange(2, pack_home(k, carriers_back(k)), 1)

    grads = []
    for first in range(0, 496, 64):
        last = min(first + 64, 496)
        grads.append(
            send(
                k.dx.at[512 + first : 512 + last],
                k.back.at[16 + first : 16 + last],
                28 + first // 64,
                lat,
                east,
            )
        )
    grads_corner = send(k.dx.at[1008:1024], k.back.at[0:16], 15, below, east)
    grads_below = send(k.dx.at[496:512], k.fall, 16, below, lon)
    sensitivities = send(k.cgrad.at[0:128], k.cgrad.at[128:256], 8, sibling, lon)

    def back_step(quad, carry):
        @pl.when(quad == 2)
        def _():
            group_gather(2, k.cgrad, 8)
            start(grads[2:3])

        @pl.when(quad == 3)
        def _():
            start(grads[3:5])
            sensitivities.wait_recv()
            exchange(3, pack_owner(k, group_back(k)), -1)
            start(grads[5:6])

        cells_back(k, quad)
        cells_gradient(k, 512 + quad * 128, 128)
        for piece, at in ((0, 0), (1, 1), (6, 3)):
            pl.when(quad == at)(grads[piece].start)
        return carry

    lax.fori_loop(0, 4, back_step, 0)

    def left_step(i, carry):
        cells_gradient(k, 256 - 256 * i, 256)
        pl.when(i == 0)(grads[7].start)

        @pl.when((i == 0) & has_below)
        def _():
            grads_corner.start()
            grads_below.start()

        return carry

    lax.fori_loop(0, 2, left_step, 0)
    k.edges[0:64, :] = unpack_home(k, exchanged(3))
    pool_east = send(k.edges.at[32:64], k.edges.at[64:96], 17, lat, east)
    pool_corner = send(k.edges.at[48:64], k.edges.at[96:112], 18, below, east)
    pool_below = send(k.edges.at[16:32], k.edges.at[112:128], 19, below, lon)
    pool_east.start()

    @pl.when(has_below)
    def _():
        pool_corner.start()
        pool_below.start()

    loop(4, cells_result, k)
    store_out = pltpu.make_async_copy(k.xraw, k.result_hbm, k.load_sem.at[6])
    store_out.start()
    stores = [
        pltpu.make_async_copy(k.dx.at[0:496], k.grads_hbm.at[528:1024], k.store_sem.at[0]),
        pltpu.make_async_copy(k.back, k.grads_hbm.at[0:512], k.store_sem.at[1]),
        pltpu.make_async_copy(k.fall, k.grads_hbm.at[512:528], k.store_sem.at[2]),
        pltpu.make_async_copy(k.edges, k.edges_hbm, k.store_sem.at[3]),
    ]
    stores[0].start()

    wait_received(grads)

    @pl.when(has_above)
    def _():
        grads_corner.wait_recv()
        grads_below.wait_recv()

    start(stores[1:3])
    pool_east.wait_recv()

    @pl.when(has_above)
    def _():
        pool_corner.wait_recv()
        pool_below.wait_recv()

    stores[3].start()

    for copy in [carriers_west, members, sensitivities, pool_east] + cells + grads:
        copy.wait_send()

    @pl.when(has_above)
    def _():
        for copy in (carriers_corner, carriers_above, cells_corner, cells_above):
            copy.wait_send()

    @pl.when(has_below)
    def _():
        for copy in (grads_corner, grads_below, pool_corner, pool_below):
            copy.wait_send()

    for index in range(4):
        await_bytes(k.slab_out.at[index, 1:32], k.slab_send_sem.at[index])
    for index in range(2):
        await_bytes(k.slab_out.at[0], k.far_send_sem.at[index])
    store_out.wait()
    for store in stores:
        store.wait()


def loop(count, step, k):
    loop_from(0, count, step, k)


def loop_from(first, last, step, k):
    lax.fori_loop(first, last, lambda i, _: (step(k, i), 0)[1], 0)


SCRATCH = {
    "heads": ((256, 256), BF),
    "carrier_heads": ((256, D), BF),
    "same": ((256, 256), BF),
    "spread": ((1024, 64), BF),
    "gather": ((64, 1024), BF),
    "split": ((256, 256), BF),
    "unpack": ((384, HALF), BF),
    "routes": ((384, HALF), BF),
    "gain": ((1, D), F32),
    "cgain": ((1, D), F32),
    "temper": ((1, D), F32),
    "ctemper": ((1, D), F32),
    "xraw": ((1024, D), BF),
    "graw": ((1024, D), BF),
    "w": ((D, 3 * D), BF),
    "we": ((D, D), BF),
    "cw": ((D, 3 * D), BF),
    "cwe": ((D, D), BF),
    "x": ((1024, D), BF),
    "g": ((1024, D), BF),
    "away": ((HALF, D), BF),
    "rise": ((16, D), BF),
    "means": ((2, 32, D), F32),
    "car_send": ((64, D), BF),
    "car_beside": ((32, D), BF),
    "car_corner": ((16, D), BF),
    "car_below": ((16, D), BF),
    "slab_out": ((4, 32, 16, 128), BF),
    "slab_in": ((4, 32, 16, 128), BF),
    "slab_far": ((2, 32, 16, 128), BF),
    "car": ((256, D), BF),
    "cgrad": ((256, D), BF),
    "cn": ((64, D), BF),
    "edges": ((128, D), BF),
    "back": ((HALF, D), BF),
    "fall": ((16, D), BF),
    "dx": ((1024, D), BF),
    "q": ((1024, D), BF),
    "k": ((1024, D), BF),
    "v": ((1024, D), BF),
    "do": ((1024, D), BF),
    "o": ((1024, D), BF),
    "t": ((1024, D), BF),
    "p": ((1024, D), BF),
    "sq": ((1024, D), F32),
    "sk": ((1024, D), F32),
    "op": ((1024, D), F32),
    "lp": ((1024, D), F32),
    "kcb": ((1024, D), BF),
    "vcb": ((1024, D), BF),
    "kc": ((64, D), BF),
    "vc": ((64, D), BF),
    "skc": ((64, D), F32),
    "dqkv": ((1024, 3 * D), BF),
    "cq": ((256, D), BF),
    "ck": ((256, D), BF),
    "cv": ((256, D), BF),
    "chid": ((256, D), BF),
    "crows": ((3, 256, 256), BF),
    "ccolumns": ((3, 256, 256), BF),
    "cg": ((1024, 256), BF),
    "gsum": ((64, D), F32),
    "csq": ((64, D), F32),
    "csk": ((64, D), F32),
    "cl": ((256, D), F32),
    "co": ((256, D), F32),
}
SEMAPHORES = {
    "load_sem": 7,
    "store_sem": 4,
    "send_sem": 36,
    "recv_sem": 36,
    "far_send_sem": 2,
    "far_recv_sem": 2,
    "slab_send_sem": 4,
    "slab_recv_sem": 4,
}
INPUTS = (
    "x_hbm",
    "g_hbm",
    "w_hbm",
    "we_hbm",
    "cw_hbm",
    "cwe_hbm",
    "gains",
    "cgains",
    "place",
    "tempers",
    "ctempers",
)


def per_device(x, g, gain, w, we, tempers, cgain, cw, cwe, ctempers, place):
    names = INPUTS + ("result_hbm", "grads_hbm", "edges_hbm") + tuple(SCRATCH) + tuple(SEMAPHORES)

    def kernel(*refs):
        body(types.SimpleNamespace(**dict(zip(names, refs))))

    anywhere = pl.BlockSpec(memory_space=pl.ANY)
    vmem = pl.BlockSpec(memory_space=pltpu.VMEM)
    smem = pl.BlockSpec(memory_space=pltpu.SMEM)
    result, grads, edges = pl.pallas_call(
        kernel,
        out_shape=[jax.ShapeDtypeStruct((rows, D), BF) for rows in (1024, 1024, 128)],
        in_specs=[anywhere] * 6 + [vmem] * 3 + [smem] * 2,
        out_specs=[anywhere] * 3,
        scratch_shapes=[pltpu.VMEM(shape, kind) for shape, kind in SCRATCH.values()]
        + [pltpu.SemaphoreType.DMA((count,)) for count in SEMAPHORES.values()],
        compiler_params=pltpu.CompilerParams(
            collective_id=0, has_side_effects=True, vmem_limit_bytes=62 * 1024 * 1024
        ),
        name="block",
    )(
        x.reshape(1024, D),
        g.reshape(1024, D),
        w,
        we,
        cw,
        cwe,
        gain,
        cgain,
        place.T,
        tempers,
        ctempers,
    )
    halves = pl.BlockSpec((2, 256, D), lambda step: (0, step, 0))
    cells = pl.BlockSpec((512, D), lambda step: (step, 0))
    out, field = pl.pallas_call(
        assemble,
        grid=(2,),
        out_shape=[jax.ShapeDtypeStruct((1024, D), BF)] * 2,
        in_specs=[halves, halves, pl.BlockSpec((128, D), lambda step: (0, 0))],
        out_specs=[cells, cells],
        name="assemble",
    )(result.reshape(2, HALF, D), grads.reshape(2, HALF, D), edges)
    return out.reshape(128, 8, D), field.reshape(128, 8, D)


def solution(mesh):
    placed = (P("lat", "lon", None),) * 2 + (P(),) * 8 + (P("lat", "lon"),)
    return jax.shard_map(
        per_device,
        mesh=mesh,
        in_specs=placed,
        out_specs=(P("lat", "lon", None),) * 2,
        check_vma=False,
    )
```
